32 devices in a mesh: grp: 2 (over y), row: 4 (over x, core), slab: 4 (over z).
Axes of the slice: x: 2, y: 2, z: 4, core: 2. Of those that a mesh axis runs over, the one named last changes fastest.
Arguments:
- observed: float32 [128, 256, 256], P(('grp', 'slab'), 'row'), parts along dimension 0, may hold values from 0.25 to 4
- band_index: int32 [64], P('slab'), may hold values from 0 to 15
- taps_x: float32 [16, 31], replicated, may hold values from 0.005 to 0.12
- taps_y: float32 [16, 31], replicated, may hold values from 0.005 to 0.12
- taps_z: float32 [31], replicated, may hold values from 0.005 to 0.12
Outputs:
- estimate: float32 [128, 256, 256], P(('grp', 'slab'), 'row'), parts along dimension 0
The draws below stay inside these ranges and needn't reach their ends.
There are 2 independent parts, one for each index of `grp`. The reference program is written for one: setup_inputs(seed, part) draws one part's arguments, and reference() takes and returns one part's arrays. A program takes and returns all parts, laid end to end along the dimension named above; an argument that names none is the same for every part. Nothing has to cross between parts.
All inputs are finite; a program needn't handle non-finite values.
Results may differ from the reference program's by a relative error of at most 0.00015.
Values sent between devices are 32-bit elements; how exact they have to be, the bound alone decides.
No kernel may reach another device: no remote copies, remote signals or barrier semaphores. Data moves between devices by JAX's collectives and lax.ppermute only.
A program may use at most 64 MiB of HBM per device.

```python
import math
import jax
import jax.numpy as jnp
from jax import lax

NY = 256
TAPS = 31
NB = 16
ITERS = 2
NX = 256
NZ = 64


def plant(array, key, least, top_value):
    extent = array.shape
    place = [jax.random.randint(jax.random.fold_in(key, axis), (), 0, extent[axis]) for axis in range(len(extent))]
    array = array.at[tuple(place)].set(least)
    longest = extent.index(max(extent))
    place[longest] = (place[longest] + 1) % extent[longest]
    return array.at[tuple(place)].set(top_value)


def block_scale(own_key, extent, pieces, low, top_value):
    gain = 1.0
    for position, parts in pieces:
        heights = jax.random.uniform(jax.random.fold_in(jax.random.fold_in(own_key, 6), position), (parts,), jnp.float32, low / len(pieces), top_value / len(pieces))
        gain = gain * jnp.repeat(jnp.exp(heights), extent[position] // parts).reshape((-1,) + (1,) * (len(extent) - 1 - position))
    return gain


def setup_inputs(seed: int = 0, part: int = 0) -> dict:
    keys = jax.random.split(jax.random.key(seed), 6)
    own_keys = jax.random.split(jax.random.fold_in(keys[5], part), 6)
    return {
        "observed": jnp.clip(0.25 + 3.75 * jax.random.uniform(own_keys[0], (NZ, NX, NY), jnp.float32) ** block_scale(own_keys[0], (NZ, NX, NY), ((0, 4), (1, 4)), -0.2, 0.2), 0.25, 4.0),
        "band_index": plant(jax.random.randint(keys[1], (NZ,), 0, NB), jax.random.fold_in(keys[1], 1), 0, NB - 1).astype(jnp.int32),
        "taps_x": jnp.clip(jnp.exp(jax.random.uniform(keys[2], (NB, TAPS), jnp.float32, math.log(0.005), math.log(0.12))), 0.005, 0.12),
        "taps_y": jnp.clip(jnp.exp(jax.random.uniform(keys[3], (NB, TAPS), jnp.float32, math.log(0.005), math.log(0.12))), 0.005, 0.12),
        "taps_z": jnp.clip(jnp.exp(jax.random.uniform(keys[4], (TAPS,), jnp.float32, math.log(0.005), math.log(0.12))), 0.005, 0.12),
    }


def correlate(field, taps, dim):
    radius = taps.shape[-1] // 2
    length = field.shape[dim]
    widths = [(0, 0), (0, 0), (0, 0)]
    widths[dim] = (radius, radius)
    padded = jnp.pad(field, widths)
    total = jnp.zeros(field.shape, jnp.float32)
    for k in range(taps.shape[-1]):
        piece = lax.slice_in_dim(padded, k, k + length, axis=dim)
        if taps.ndim == 2:
            weight = taps[:, k][:, None, None]
        else:
            weight = taps[k]
        total = total + weight * piece
    return total


def forward(field, plane_x, plane_y, taps_z):
    field = correlate(field, plane_x, 1)
    field = correlate(field, plane_y, 2)
    return correlate(field, taps_z, 0)


def adjoint(field, plane_x, plane_y, taps_z):
    field = correlate(field, taps_z[::-1], 0)
    field = correlate(field, plane_y[:, ::-1], 2)
    return correlate(field, plane_x[:, ::-1], 1)


def reference(observed, band_index, taps_x, taps_y, taps_z):
    plane_x = taps_x[band_index]
    plane_y = taps_y[band_index]
    norm = adjoint(jnp.ones(observed.shape, jnp.float32), plane_x, plane_y, taps_z)
    estimate = observed
    for step in range(ITERS):
        blurred = forward(estimate, plane_x, plane_y, taps_z)
        ratio = observed / blurred
        estimate = estimate * adjoint(ratio, plane_x, plane_y, taps_z) / norm
    return estimate
```

```python
import functools

import jax
import jax.numpy as jnp
from jax import lax
from jax.experimental import pallas as pl
from jax.experimental.pallas import tpu as pltpu
from jax.sharding import PartitionSpec as P

ITERS = 2
F32 = jnp.float32
BF16 = jnp.bfloat16
VMEM_LIMIT = 40 * 1024 * 1024
SMEM = pl.BlockSpec(memory_space=pltpu.SMEM)


def up(value, step):
    return -(-value // step) * step


def split(x):
    hi = x.astype(BF16)
    return hi, (x - hi.astype(F32)).astype(BF16)


def mm(a, b, transposed=False):
    dims = (((1,), (1 if transposed else 0,)), ((), ()))
    return lax.dot_general(a, b, dims, preferred_element_type=F32)


def blur_rows(w_hi, w_lo, v_hi, v_lo):
    count = w_hi.shape[0]
    both = mm(jnp.concatenate([w_hi, w_lo], axis=0), v_hi)
    return both[:count] + both[count:] + mm(w_hi, v_lo)


def blur_columns(u, a_hi, a_lo, transposed):
    count = u.shape[0]
    u_hi, u_lo = split(u)
    both = mm(jnp.concatenate([u_hi, u_lo], axis=0), a_hi, transposed)
    return both[:count] + both[count:] + mm(u_hi, a_lo, transposed)


def full(shape):
    return pl.BlockSpec(shape, lambda i: (0,) * len(shape))


def planes(shape, per):
    return pl.BlockSpec((per,) + shape[1:], lambda i: (i,) + (0,) * (len(shape) - 1))


def spread(ref, band, lanes, shape, radius, flip):
    base = jnp.zeros(shape, F32)
    for k in range(2 * radius + 1):
        base = jnp.where(lanes == (2 * radius - k if flip else k), ref[band, k], base)
    return base


def row_matrix(base, rows, radius, width):
    parts = []
    for first in range(0, rows, 16):
        parts.append(
            pltpu.roll(base, (first - radius) % width, 1, stride=1, stride_axis=0)
        )
    return jnp.concatenate(parts, axis=0)


def forward_weights_kernel(per, radius, band_ref, tx_ref, ty_ref, ah_ref, al_ref, wx_ref):
    rows, width = wx_ref.shape[2], wx_ref.shape[3]
    columns = ah_ref.shape[1]
    lanes = lax.broadcasted_iota(jnp.int32, (16, 128), 1)
    offset = lanes - lax.broadcasted_iota(jnp.int32, (16, 128), 0)
    wide = lax.broadcasted_iota(jnp.int32, (16, width), 1)
    for p in range(per):
        band = band_ref[pl.program_id(0) * per + p]
        base = spread(ty_ref, band, lanes, (16, 128), radius, False)
        rolled = {}
        for first in range(0, columns, 16):
            key = first % 128
            if key not in rolled:
                rolled[key] = pltpu.roll(
                    base, (key - radius) % 128, 1, stride=1, stride_axis=0
                )
            for left in range(0, columns, 128):
                here = (p, slice(first, first + 16), slice(left, left + 128))
                if left > first + 15 + radius or left + 127 < first - radius:
                    zero = jnp.zeros((16, 128), BF16)
                    ah_ref[here] = zero
                    al_ref[here] = zero
                else:
                    distance = offset + (left - first)
                    tile = jnp.where(jnp.abs(distance) <= radius, rolled[key], 0.0)
                    hi, lo = split(tile)
                    ah_ref[here] = hi
                    al_ref[here] = lo
        base = spread(tx_ref, band, wide, (16, width), radius, False)
        hi, lo = split(row_matrix(base, rows, radius, width))
        wx_ref[p, 0] = hi
        wx_ref[p, 1] = lo


def forward_weights(band_index, taps_x, taps_y, n, rows, columns, width, per):
    radius = taps_x.shape[1] // 2
    a = jax.ShapeDtypeStruct((n, columns, columns), BF16)
    w = jax.ShapeDtypeStruct((n, 2, rows, width), BF16)
    return pl.pallas_call(
        functools.partial(forward_weights_kernel, per, radius),
        grid=(n // per,),
        in_specs=[SMEM] * 3,
        out_specs=[planes(a.shape, per), planes(a.shape, per), planes(w.shape, per)],
        out_shape=[a, a, w],
        compiler_params=pltpu.CompilerParams(vmem_limit_bytes=VMEM_LIMIT),
    )(band_index, taps_x, taps_y)


def adjoint_weights_kernel(
    per, radius, halo, depth, place_ref, band_ref, tx_ref, tz_ref, ah_ref, al_ref, wx_ref, rn_ref
):
    rows, width = wx_ref.shape[2], wx_ref.shape[3]
    wide = lax.broadcasted_iota(jnp.int32, (16, width), 1)
    at = lax.broadcasted_iota(jnp.int32, (rows, width), 1)
    own = at < rows
    above = (at < width - halo) & (place_ref[2] != 0)
    below = (at >= width - halo) & (place_ref[1] != 0)
    valid = own | above | below
    for p in range(per):
        plane = pl.program_id(0) * per + p
        band = band_ref[plane]
        base = spread(tx_ref, band, wide, (16, width), radius, True)
        matrix = row_matrix(base, rows, radius, width)
        hi, lo = split(matrix)
        wx_ref[p, 0] = hi
        wx_ref[p, 1] = lo
        along_x = jnp.sum(jnp.where(valid, matrix, 0.0), axis=1, keepdims=True)
        columns = ah_ref[p].astype(F32) + al_ref[p].astype(F32)
        along_y = jnp.sum(columns, axis=0, keepdims=True)
        along_z = jnp.float32(0.0)
        z = place_ref[0] + plane
        for k in range(2 * radius + 1):
            source = z - k + radius
            inside = (source >= 0) & (source < depth)
            along_z = along_z + jnp.where(inside, tz_ref[k], 0.0)
        rn_ref[p] = 1.0 / (along_x * (along_y * along_z))


def adjoint_weights(place, band_index, taps_x, taps_z, ah, al, rows, width, halo, depth, per):
    radius = taps_x.shape[1] // 2
    n, columns = ah.shape[:2]
    w = jax.ShapeDtypeStruct((n, 2, rows, width), BF16)
    r = jax.ShapeDtypeStruct((n, rows, columns), F32)
    return pl.pallas_call(
        functools.partial(adjoint_weights_kernel, per, radius, halo, depth),
        grid=(n // per,),
        in_specs=[SMEM] * 4 + [planes(ah.shape, per)] * 2,
        out_specs=[planes(w.shape, per), planes(r.shape, per)],
        out_shape=[w, r],
        compiler_params=pltpu.CompilerParams(vmem_limit_bytes=VMEM_LIMIT),
    )(place, band_index, taps_x, taps_z, ah, al)


def store_sends(v, plane, n, radius, low_ref, high_ref):
    @pl.when(plane < radius)
    def _():
        low_ref[jnp.minimum(plane, radius - 1)] = v

    @pl.when(plane >= n - radius)
    def _():
        high_ref[jnp.maximum(plane - (n - radius), 0)] = v


def interior(est_hi, est_lo, wx_ref, ah_ref, al_ref, p, halo, plane, n, radius, sends):
    rows = est_hi.shape[0]
    w_hi = wx_ref[p, 0, halo : rows - halo, :rows]
    w_lo = wx_ref[p, 1, halo : rows - halo, :rows]
    u = blur_rows(w_hi, w_lo, est_hi, est_lo)
    v = blur_columns(u, ah_ref[p], al_ref[p], True)
    for c in range(0, len(sends), 2):
        part = v[c // 2 * halo : (c // 2 + 1) * halo]
        store_sends(part, plane, n, radius, sends[c], sends[c + 1])


def interior_kernel(per, n, radius, halo, est_ref, wx_ref, ah_ref, al_ref, *sends):
    for p in range(per):
        plane = pl.program_id(0) * per + p
        est_hi, est_lo = split(est_ref[p])
        interior(est_hi, est_lo, wx_ref, ah_ref, al_ref, p, halo, plane, n, radius, sends)


def forward_interior(est, wx, ah, al, halo, radius, per):
    n, rows, columns = est.shape
    send = jax.ShapeDtypeStruct((radius, halo, columns), F32)
    count = 2 * (rows // halo - 2)
    return pl.pallas_call(
        functools.partial(interior_kernel, per, n, radius, halo),
        grid=(n // per,),
        in_specs=[planes(x.shape, per) for x in (est, wx, ah, al)],
        out_specs=[full(send.shape)] * count,
        out_shape=[send] * count,
        compiler_params=pltpu.CompilerParams(vmem_limit_bytes=VMEM_LIMIT),
    )(est, wx, ah, al)


def stacked(own, high, low, width):
    rows, columns = own.shape
    gap = width - rows - high.shape[0] - low.shape[0]
    parts = [own, high]
    if gap:
        parts.append(jnp.zeros((gap, columns), own.dtype))
    return jnp.concatenate(parts + [low], axis=0)


def edge_kernel(
    per, n, radius, halo, est_ref, xlo_ref, xhi_ref, wx_ref, ah_ref, al_ref, low_ref, high_ref
):
    rows = est_ref.shape[1]
    width = wx_ref.shape[3]
    for p in range(per):
        plane = pl.program_id(0) * per + p
        v_hi, v_lo = split(stacked(est_ref[p], xhi_ref[p], xlo_ref[p], width))
        w_hi = jnp.concatenate([wx_ref[p, 0, :halo], wx_ref[p, 0, rows - halo :]], axis=0)
        w_lo = jnp.concatenate([wx_ref[p, 1, :halo], wx_ref[p, 1, rows - halo :]], axis=0)
        u = blur_rows(w_hi, w_lo, v_hi, v_lo)
        v = blur_columns(u, ah_ref[p], al_ref[p], True)
        store_sends(v, plane, n, radius, low_ref, high_ref)


def forward_edge(est, xlo, xhi, wx, ah, al, halo, radius, per):
    n, rows, columns = est.shape
    send = jax.ShapeDtypeStruct((radius, 2 * halo, columns), F32)
    return pl.pallas_call(
        functools.partial(edge_kernel, per, n, radius, halo),
        grid=(n // per,),
        in_specs=[planes(x.shape, per) for x in (est, xlo, xhi, wx, ah, al)],
        out_specs=[full(send.shape)] * 2,
        out_shape=[send] * 2,
        compiler_params=pltpu.CompilerParams(vmem_limit_bytes=VMEM_LIMIT),
    )(est, xlo, xhi, wx, ah, al)


def depth_sum(n, radius, flip, tz_ref, low_ref, high_ref, zlo_ref, zhi_ref, rows, lanes):
    last = 2 * radius
    taps = [tz_ref[last - k if flip else k] for k in range(last + 1)]
    total = [None] * n
    for j in range(-radius, n + radius):
        if j < 0:
            piece = zlo_ref[j + radius, rows, lanes]
        elif j < radius:
            piece = low_ref[j, rows, lanes]
        elif j < n:
            piece = high_ref[j - (n - radius), rows, lanes]
        else:
            piece = zhi_ref[j - n, rows, lanes]
        for i in range(max(0, j - radius), min(n, j + radius + 1)):
            term = taps[j - i + radius] * piece
            total[i] = term if total[i] is None else total[i] + term
    return total


def ratio_kernel(
    n, radius, tz_ref, low_ref, high_ref, zlo_ref, zhi_ref, obs_ref, rlow_ref, rhigh_ref
):
    halo, columns = obs_ref.shape[1:]

    def body(t, carry):
        rows = pl.ds(pl.multiple_of(t * 8, 8), 8)
        for left in range(0, columns, 128):
            lanes = slice(left, left + 128)
            total = depth_sum(
                n, radius, False, tz_ref, low_ref, high_ref, zlo_ref, zhi_ref, rows, lanes
            )
            for i in range(n):
                ratio = obs_ref[i, rows, lanes] / total[i]
                if i < radius:
                    rlow_ref[i, rows, lanes] = ratio
                if i >= n - radius:
                    rhigh_ref[i - (n - radius), rows, lanes] = ratio
        return carry

    lax.fori_loop(0, halo // 8, body, 0)


def depth_ratio(taps_z, low, high, zlo, zhi, obs, first, step, halo):
    n, _, columns = obs.shape
    radius, count = low.shape[:2]
    part = pl.BlockSpec((radius, halo, columns), lambda i: (0, i, 0))
    send = jax.ShapeDtypeStruct(low.shape, F32)
    return pl.pallas_call(
        functools.partial(ratio_kernel, n, radius),
        grid=(count // halo,),
        in_specs=[SMEM]
        + [part] * 4
        + [pl.BlockSpec((n, halo, columns), lambda i: (0, first + step * i, 0))],
        out_specs=[part] * 2,
        out_shape=[send] * 2,
        compiler_params=pltpu.CompilerParams(vmem_limit_bytes=VMEM_LIMIT),
    )(taps_z, low, high, zlo, zhi, obs)


def back_kernel(n, radius, tz_ref, low_ref, high_ref, zlo_ref, zhi_ref, *out_refs):
    halo, columns = out_refs[0].shape[1:]

    def run(out_ref):
        def body(t, carry):
            rows = pl.ds(pl.multiple_of(t * 8, 8), 8)
            for left in range(0, columns, 128):
                lanes = slice(left, left + 128)
                total = depth_sum(
                    n, radius, True, tz_ref, low_ref, high_ref, zlo_ref, zhi_ref, rows, lanes
                )
                for i in range(n):
                    out_ref[i, rows, lanes] = total[i]
            return carry

        lax.fori_loop(0, halo // 8, body, 0)

    if len(out_refs) == 1:
        run(out_refs[0])
    else:
        for s, out_ref in enumerate(out_refs):
            pl.when(pl.program_id(0) == s)(functools.partial(run, out_ref))


def depth_back(taps_z, low, high, zlo, zhi, n, halo):
    radius, count, columns = low.shape
    part = pl.BlockSpec((radius, halo, columns), lambda i: (0, i, 0))
    out = jax.ShapeDtypeStruct((n, halo, columns), F32)
    return pl.pallas_call(
        functools.partial(back_kernel, n, radius),
        grid=(count // halo,),
        in_specs=[SMEM] + [part] * 4,
        out_specs=[full(out.shape)] * (count // halo),
        out_shape=[out] * (count // halo),
        compiler_params=pltpu.CompilerParams(vmem_limit_bytes=VMEM_LIMIT),
    )(taps_z, low, high, zlo, zhi)


def update_kernel(per, n, radius, halo, pieces, last, *refs):
    c_refs, refs = refs[:pieces], refs[pieces:]
    xlo_ref, xhi_ref, est_ref, rn_ref, wa_ref, ah_ref, al_ref = refs[:7]
    refs = refs[7:]
    rows = est_ref.shape[1]
    width = wa_ref.shape[3]
    if last:
        (out_ref,) = refs
    else:
        wx_ref, out_ref, top_ref, bottom_ref = refs[:4]
        sends = refs[4:]
    for p in range(per):
        plane = pl.program_id(0) * per + p
        own = jnp.concatenate([c_ref[p] for c_ref in c_refs], axis=0)
        c_hi, c_lo = split(stacked(own, xhi_ref[p], xlo_ref[p], width))
        u = blur_rows(wa_ref[p, 0], wa_ref[p, 1], c_hi, c_lo)
        u = blur_columns(u, ah_ref[p], al_ref[p], False)
        est = est_ref[p] * u * rn_ref[p]
        out_ref[p] = est
        if not last:
            top_ref[p] = est[:halo]
            bottom_ref[p] = est[rows - halo :]
            est_hi, est_lo = split(est)
            interior(est_hi, est_lo, wx_ref, ah_ref, al_ref, p, halo, plane, n, radius, sends)


def update(pieces, xlo, xhi, est, rn, wa, ah, al, wx, halo, radius, per):
    n, rows, columns = est.shape
    last = wx is None
    args = list(pieces) + [xlo, xhi, est, rn, wa, ah, al] + ([] if last else [wx])
    out = jax.ShapeDtypeStruct(est.shape, F32)
    out_specs, out_shape = [planes(out.shape, per)], [out]
    if not last:
        edge = jax.ShapeDtypeStruct((n, halo, columns), F32)
        send = jax.ShapeDtypeStruct((radius, halo, columns), F32)
        count = 2 * (rows // halo - 2)
        out_specs += [planes(edge.shape, per)] * 2 + [full(send.shape)] * count
        out_shape += [edge] * 2 + [send] * count
    return pl.pallas_call(
        functools.partial(update_kernel, per, n, radius, halo, len(pieces), last),
        grid=(n // per,),
        in_specs=[planes(x.shape, per) for x in args],
        out_specs=out_specs,
        out_shape=out_shape,
        compiler_params=pltpu.CompilerParams(vmem_limit_bytes=VMEM_LIMIT),
    )(*args)


def exchange(first, last, axis):
    count = lax.axis_size(axis)
    forward = [(i, i + 1) for i in range(count - 1)]
    backward = [(i + 1, i) for i in range(count - 1)]
    return lax.ppermute(last, axis, forward), lax.ppermute(first, axis, backward)


def on_device(observed, band_index, taps_x, taps_y, taps_z):
    n, rows, columns = observed.shape
    radius = taps_z.shape[0] // 2
    halo = up(radius, 16)
    width = up(rows + 2 * halo, 128)
    per = 4 if n % 4 == 0 else 1
    depth = n * lax.axis_size("slab")
    row, row_count = lax.axis_index("row"), lax.axis_size("row")
    place = jnp.stack(
        [lax.axis_index("slab") * n, row, row_count - 1 - row]
    ).astype(jnp.int32)
    inner = rows // halo - 2

    top, bottom = observed[:, :halo], observed[:, rows - halo :]
    xlo, xhi = exchange(top, bottom, "row")
    ah, al, wx = forward_weights(
        band_index, taps_x, taps_y, n, rows, columns, width, per
    )
    est = observed
    sends = forward_interior(est, wx, ah, al, halo, radius, per)
    wa = None
    for step in range(ITERS):
        chunks = []
        for c in range(inner):
            low, high = sends[2 * c], sends[2 * c + 1]
            zlo, zhi = exchange(low, high, "slab")
            chunks.append((low, high, zlo, zhi, 1 + c, 1))
        low, high = forward_edge(est, xlo, xhi, wx, ah, al, halo, radius, per)
        zlo, zhi = exchange(low, high, "slab")
        chunks.insert(1, (low, high, zlo, zhi, 0, rows // halo - 1))
        if wa is None:
            wa, rn = adjoint_weights(
                place, band_index, taps_x, taps_z, ah, al, rows, width, halo, depth, per
            )
        ratios = []
        for low, high, zlo, zhi, first, stride in chunks:
            low, high = depth_ratio(
                taps_z, low, high, zlo, zhi, observed, first, stride, halo
            )
            zlo, zhi = exchange(low, high, "slab")
            ratios.append((low, high, zlo, zhi))
        inside = []
        for c, (low, high, zlo, zhi) in enumerate(ratios):
            out = depth_back(taps_z, low, high, zlo, zhi, n, halo)
            if c == 1:
                top, bottom = out
                xlo, xhi = exchange(top, bottom, "row")
            else:
                inside += out
        pieces = [top] + inside + [bottom]
        last = step == ITERS - 1
        out = update(
            pieces, xlo, xhi, est, rn, wa, ah, al, None if last else wx, halo, radius, per
        )
        est = out[0]
        if not last:
            xlo, xhi = exchange(out[1], out[2], "row")
            sends = out[3:]
    return est


def solution(mesh):
    in_specs = (P(("grp", "slab"), "row", None), P("slab"), P(), P(), P())
    out_specs = P(("grp", "slab"), "row", None)
    return jax.shard_map(
        on_device, mesh=mesh, in_specs=in_specs, out_specs=out_specs, check_vma=False
    )
```

```python
import functools

import jax
import jax.numpy as jnp
from jax import lax
from jax.experimental import pallas as pl
from jax.experimental.pallas import tpu as pltpu
from jax.sharding import PartitionSpec as P

ITERS = 2
F32 = jnp.float32
BF16 = jnp.bfloat16
PARAMS = pltpu.CompilerParams(vmem_limit_bytes=40 * 1024 * 1024)
SMEM = pl.BlockSpec(memory_space=pltpu.SMEM)
VMEM = pl.BlockSpec(memory_space=pltpu.VMEM)
ANY = pl.BlockSpec(memory_space=pl.ANY)


def up(value, step):
    return -(-value // step) * step


def split(x):
    hi = x.astype(BF16)
    return hi, (x - hi.astype(F32)).astype(BF16)


def mm(a, b):
    return jnp.dot(a, b, preferred_element_type=F32)


def blur_rows(w_hi, w_lo, v_hi, v_lo):
    count = w_hi.shape[0]
    both = mm(jnp.concatenate([w_hi, w_lo], axis=0), v_hi)
    return both[:count] + both[count:] + mm(w_hi, v_lo)


def blur_columns(u, a_hi, a_lo):
    count = u.shape[0]
    u_hi, u_lo = split(u)
    both = mm(jnp.concatenate([u_hi, u_lo], axis=0), a_hi)
    return both[:count] + both[count:] + mm(u_hi, a_lo)


def full(shape):
    return pl.BlockSpec(shape, lambda i: (0,) * len(shape))


def planes(shape, per):
    return pl.BlockSpec((per,) + shape[1:], lambda i: (i,) + (0,) * (len(shape) - 1))


def shape_of(*dims, dtype=F32):
    return jax.ShapeDtypeStruct(dims, dtype)


def spread(ref, band, lanes, radius, flip):
    base = jnp.zeros(lanes.shape, F32)
    for k in range(2 * radius + 1):
        base = jnp.where(lanes == (2 * radius - k if flip else k), ref[band, k], base)
    return base


def iotas(rows, lanes):
    shape = (rows, lanes)
    return (
        lax.broadcasted_iota(jnp.int32, shape, 0),
        lax.broadcasted_iota(jnp.int32, shape, 1),
    )


def column_matrix(base, radius, h_ref, l_ref, p):
    columns = h_ref.shape[1]
    sub, lane = iotas(16, 128)
    rolled = {}
    sums = [None] * (columns // 128)
    for first in range(0, columns, 16):
        key = first % 128
        if key not in rolled:
            rolled[key] = pltpu.roll(base, (key - radius) % 128, 1, stride=1, stride_axis=0)
        for block in range(columns // 128):
            left = block * 128
            here = (p, slice(first, first + 16), slice(left, left + 128))
            if left > first + 15 + radius or left + 127 < first - radius:
                zero = jnp.zeros((16, 128), BF16)
                h_ref[here] = zero
                l_ref[here] = zero
                continue
            inside = jnp.abs(lane - sub + (left - first)) <= radius
            tile = jnp.where(inside, rolled[key], 0.0)
            h_ref[here], l_ref[here] = split(tile)
            sums[block] = tile if sums[block] is None else sums[block] + tile
    return [jnp.sum(s, axis=0, keepdims=True) for s in sums]


def row_matrix(base, rows, shift, width):
    return jnp.concatenate(
        [
            pltpu.roll(base, (first + shift) % width, 1, stride=1, stride_axis=0)
            for first in range(0, rows, 16)
        ],
        axis=0,
    )


def store_sends(v, plane, n, radius, low_ref, high_ref):
    @pl.when(plane < radius)
    def _():
        low_ref[jnp.minimum(plane, radius - 1)] = v

    @pl.when(plane >= n - radius)
    def _():
        high_ref[jnp.maximum(plane - (n - radius), 0)] = v


def own_rows(est, wx_ref, ah_ref, al_ref, p, inner):
    rows = est.shape[0]
    est_hi, est_lo = split(est)
    u = blur_rows(wx_ref[p, 0, :inner, :rows], wx_ref[p, 1, :inner, :rows], est_hi, est_lo)
    return blur_columns(u, ah_ref[p], al_ref[p])


def first_kernel(
    per, n, radius, halo, place_ref, band_ref, tx_ref, ty_ref, est_ref,
    ah_ref, al_ref, wx_ref, low_ref, high_ref,
):
    rows, width = wx_ref.shape[2], wx_ref.shape[3]
    _, lane = iotas(16, 128)
    _, wide = iotas(16, width)
    row, lanes = iotas(rows, width)
    keep = (place_ref[2] == 0) | ((row < rows - radius) == (lanes < rows))
    for p in range(per):
        plane = pl.program_id(0) * per + p
        band = band_ref[plane]
        column_matrix(spread(ty_ref, band, lane, radius, True), radius, ah_ref, al_ref, p)
        matrix = row_matrix(spread(tx_ref, band, wide, radius, False), rows, 0, width)
        wx_ref[p, 0], wx_ref[p, 1] = split(jnp.where(keep, matrix, 0.0))
        v = own_rows(est_ref[p], wx_ref, ah_ref, al_ref, p, rows - halo)
        store_sends(v, plane, n, radius, low_ref, high_ref)


def first_blur(place, band_index, taps_x, taps_y, est, halo, width, per):
    n, rows, columns = est.shape
    radius = taps_x.shape[1] // 2
    a = shape_of(n, columns, columns, dtype=BF16)
    w = shape_of(n, 2, rows, width, dtype=BF16)
    send = shape_of(radius, rows - halo, columns)
    return pl.pallas_call(
        functools.partial(first_kernel, per, n, radius, halo),
        grid=(n // per,),
        in_specs=[SMEM] * 4 + [planes(est.shape, per)],
        out_specs=[planes(x.shape, per) for x in (a, a, w)] + [full(send.shape)] * 2,
        out_shape=[a, a, w, send, send],
        compiler_params=PARAMS,
    )(place, band_index, taps_x, taps_y, est)


def second_kernel(
    per, n, radius, halo, depth, place_ref, band_ref, tx_ref, ty_ref, tz_ref, after_ref,
    obs_ref, next_ref, ah_ref, al_ref, wx_ref, rn_ref, shifted_ref,
):
    rows, width = wx_ref.shape[2], wx_ref.shape[3]
    _, lane = iotas(16, 128)
    _, wide = iotas(16, width)
    _, lanes = iotas(rows, width)
    lower = (place_ref[1] == 0) | (lanes >= rows - radius - (rows - halo))
    upper = (place_ref[2] == 0) | (lanes < rows - radius + halo)
    keep = ((lanes < halo) & lower) | ((lanes >= halo) & upper)
    for p in range(per):
        plane = pl.program_id(0) * per + p
        band = band_ref[plane]
        sums = column_matrix(
            spread(ty_ref, band, lane, radius, False), radius, ah_ref, al_ref, p
        )
        matrix = row_matrix(
            spread(tx_ref, band, wide, radius, True), rows, halo - 2 * radius, width
        )
        matrix = jnp.where(keep, matrix, 0.0)
        wx_ref[p, 0], wx_ref[p, 1] = split(matrix)
        along_x = jnp.sum(matrix, axis=1, keepdims=True)
        along_z = jnp.float32(0.0)
        z = place_ref[0] + plane
        for k in range(2 * radius + 1):
            source = z - k + radius
            inside = (source >= 0) & (source < depth)
            along_z = along_z + jnp.where(inside, tz_ref[k], 0.0)
        for block, along_y in enumerate(sums):
            rn_ref[p, :, block * 128 : block * 128 + 128] = 1.0 / (
                along_x * (along_y * along_z)
            )
        shifted_ref[p, : rows - radius] = obs_ref[p, radius:]
        shifted_ref[p, rows - radius :] = next_ref[p, :radius]


def second_weights(
    place, band_index, taps_x, taps_y, taps_z, after, obs, beyond, halo, width, depth, per
):
    n, rows, columns = obs.shape
    radius = taps_x.shape[1] // 2
    a = shape_of(n, columns, columns, dtype=BF16)
    w = shape_of(n, 2, rows, width, dtype=BF16)
    field = shape_of(*obs.shape)
    return pl.pallas_call(
        functools.partial(second_kernel, per, n, radius, halo, depth),
        grid=(n // per,),
        in_specs=[SMEM] * 5 + [ANY] + [planes(x.shape, per) for x in (obs, beyond)],
        out_specs=[planes(x.shape, per) for x in (a, a, w, field, field)],
        out_shape=[a, a, w, field, field],
        compiler_params=PARAMS,
    )(place, band_index, taps_x, taps_y, taps_z, after, obs, beyond)


def edge_kernel(
    per, n, radius, halo, est_ref, next_ref, wx_ref, ah_ref, al_ref, low_ref, high_ref
):
    rows = est_ref.shape[1]
    inner, used = rows - halo, rows + halo
    for p in range(per):
        plane = pl.program_id(0) * per + p
        v_hi, v_lo = split(jnp.concatenate([est_ref[p], next_ref[p]], axis=0))
        u = blur_rows(wx_ref[p, 0, inner:, :used], wx_ref[p, 1, inner:, :used], v_hi, v_lo)
        v = blur_columns(u, ah_ref[p], al_ref[p])
        store_sends(v, plane, n, radius, low_ref, high_ref)


def edge_blur(est, beyond, wx, ah, al, radius, per):
    n, _, columns = est.shape
    halo = beyond.shape[1]
    send = shape_of(radius, halo, columns)
    args = (est, beyond, wx, ah, al)
    return pl.pallas_call(
        functools.partial(edge_kernel, per, n, radius, halo),
        grid=(n // per,),
        in_specs=[planes(x.shape, per) for x in args],
        out_specs=[full(send.shape)] * 2,
        out_shape=[send] * 2,
        compiler_params=PARAMS,
    )(*args)


def depth_sum(n, radius, flip, tz_ref, refs, rows, lanes):
    low_ref, high_ref, zlo_ref, zhi_ref = refs
    last = 2 * radius
    taps = [tz_ref[last - k if flip else k] for k in range(last + 1)]
    total = [None] * n
    for j in range(-radius, n + radius):
        if j < 0:
            piece = zlo_ref[j + radius, rows, lanes]
        elif j < radius:
            piece = low_ref[j, rows, lanes]
        elif j < n:
            piece = high_ref[j - (n - radius), rows, lanes]
        else:
            piece = zhi_ref[j - n, rows, lanes]
        for i in range(max(0, j - radius), min(n, j + radius + 1)):
            term = taps[j - i + radius] * piece
            total[i] = term if total[i] is None else total[i] + term
    return total


def tiles(count, columns, body):
    def step(t, carry):
        for left in range(0, columns, 128):
            body(t * 8, slice(left, left + 128))
        return carry

    lax.fori_loop(0, count // 8, step, 0)


def at(start, offset):
    return pl.ds(pl.multiple_of(start + offset, 8), 8)


def ratio_kernel(n, radius, skip, obs_skip, tz_ref, obs_ref, *refs):
    rlow_ref, rhigh_ref = refs[-2:]
    _, count, columns = rlow_ref.shape

    def body(start, lanes):
        total = depth_sum(n, radius, False, tz_ref, refs[:4], at(start, skip), lanes)
        rows = at(start, 0)
        for i in range(n):
            ratio = obs_ref[i, at(start, obs_skip), lanes] / total[i]
            if i < radius:
                rlow_ref[i, rows, lanes] = ratio
            if i >= n - radius:
                rhigh_ref[i - (n - radius), rows, lanes] = ratio

    tiles(count, columns, body)


def depth_ratio(taps_z, obs, chunk, skip, obs_skip, count, after=None):
    n, _, columns = obs.shape
    radius = taps_z.shape[0] // 2
    send = shape_of(radius, count, columns)
    extra = [] if after is None else [after]
    return pl.pallas_call(
        functools.partial(ratio_kernel, n, radius, skip, obs_skip),
        in_specs=[SMEM] + [VMEM] * 5 + [ANY] * len(extra),
        out_specs=[VMEM] * 2,
        out_shape=[send] * 2,
        compiler_params=PARAMS,
    )(taps_z, obs, *chunk, *extra)


def back_kernel(n, radius, groups, tz_ref, *refs):
    out_ref = refs[-1]
    columns = out_ref.shape[2]
    first = 0
    for g in range(groups):
        own = refs[4 * g : 4 * g + 4]
        count = own[0].shape[1]

        def body(start, lanes):
            total = depth_sum(n, radius, True, tz_ref, own, at(start, 0), lanes)
            for i in range(n):
                out_ref[i, at(start, first), lanes] = total[i]

        tiles(count, columns, body)
        first += count


def depth_back(taps_z, chunks, n, after=None):
    radius, _, columns = chunks[0][0].shape
    count = sum(chunk[0].shape[1] for chunk in chunks)
    extra = [] if after is None else [after]
    return pl.pallas_call(
        functools.partial(back_kernel, n, radius, len(chunks)),
        in_specs=[SMEM] + [VMEM] * (4 * len(chunks)) + [ANY] * len(extra),
        out_specs=VMEM,
        out_shape=shape_of(n, count, columns),
        compiler_params=PARAMS,
    )(taps_z, *(x for chunk in chunks for x in chunk), *extra)


def update_kernel(per, n, radius, last, *refs):
    before_ref, inner_ref, edge_ref, est_ref, rn_ref, wa_ref, bh_ref, bl_ref = refs[:8]
    refs = refs[8:]
    rows = est_ref.shape[1]
    halo = edge_ref.shape[1]
    if last:
        (out_ref,) = refs
    else:
        wx_ref, ah_ref, al_ref, out_ref, top_ref, low_ref, high_ref = refs
    for p in range(per):
        plane = pl.program_id(0) * per + p
        c = jnp.concatenate([before_ref[p], inner_ref[p], edge_ref[p]], axis=0)
        c_hi, c_lo = split(c)
        used = rows + halo
        u = blur_rows(wa_ref[p, 0, :, :used], wa_ref[p, 1, :, :used], c_hi, c_lo)
        u = blur_columns(u, bh_ref[p], bl_ref[p])
        est = est_ref[p] * u * rn_ref[p]
        out_ref[p] = est
        if not last:
            top_ref[p] = est[:halo]
            v = own_rows(est, wx_ref, ah_ref, al_ref, p, rows - halo)
            store_sends(v, plane, n, radius, low_ref, high_ref)


def update(before, inner, edge, est, rn, adjoint, forward, radius, per):
    n, rows, columns = est.shape
    halo = edge.shape[1]
    last = forward is None
    args = [before, inner, edge, est, rn, *adjoint] + ([] if last else [*forward])
    out_specs, out_shape = [planes(est.shape, per)], [shape_of(*est.shape)]
    if not last:
        top = shape_of(n, halo, columns)
        send = shape_of(radius, rows - halo, columns)
        out_specs += [planes(top.shape, per)] + [full(send.shape)] * 2
        out_shape += [top, send, send]
    return pl.pallas_call(
        functools.partial(update_kernel, per, n, radius, last),
        grid=(n // per,),
        in_specs=[planes(x.shape, per) for x in args],
        out_specs=out_specs,
        out_shape=out_shape,
        compiler_params=PARAMS,
    )(*args)


def depth_exchange(low, high):
    count = lax.axis_size("slab")
    forward = [(i, i + 1) for i in range(count - 1)]
    backward = [(i + 1, i) for i in range(count - 1)]
    zlo = lax.ppermute(high, "slab", forward)
    zhi = lax.ppermute(low, "slab", backward)
    return low, high, zlo, zhi


def ring(x, step):
    count = lax.axis_size("row")
    return lax.ppermute(x, "row", [(i, (i + step) % count) for i in range(count)])


def on_device(observed, band_index, taps_x, taps_y, taps_z):
    n, rows, columns = observed.shape
    radius = taps_z.shape[0] // 2
    halo = up(2 * radius, 16)
    inner = rows - halo
    half = up(inner // 2, 16)
    width = up(rows + halo, 128)
    per = 4 if n % 4 == 0 else 1
    depth = n * lax.axis_size("slab")
    row = lax.axis_index("row")
    last_row = row == lax.axis_size("row") - 1
    place = jnp.stack([lax.axis_index("slab") * n, row == 0, last_row]).astype(jnp.int32)

    beyond = ring(observed[:, :halo], -1)
    ah, al, wx, low, high = first_blur(
        place, band_index, taps_x, taps_y, observed, halo, width, per
    )
    est, adjoint = observed, None
    for step in range(ITERS):
        v_inner = depth_exchange(low, high)
        low, high = edge_blur(est, beyond, wx, ah, al, radius, per)
        v_edge = depth_exchange(low, high)
        if adjoint is None:
            bh, bl, wa, rn, shifted = second_weights(
                place, band_index, taps_x, taps_y, taps_z, low, observed, beyond, halo,
                width, depth, per,
            )
            adjoint = (wa, bh, bl)
        r_first = depth_exchange(
            *depth_ratio(taps_z, shifted, v_inner, 0, 0, half, after=low)
        )
        r_edge = depth_exchange(*depth_ratio(taps_z, shifted, v_edge, 0, inner, halo))
        r_second = depth_exchange(
            *depth_ratio(
                taps_z, shifted, v_inner, half, half, inner - half, after=r_edge[0]
            )
        )
        c_edge = depth_back(taps_z, [r_edge], n)
        before = ring(c_edge, 1)
        c_inner = depth_back(taps_z, [r_first, r_second], n, after=c_edge)
        last = step == ITERS - 1
        out = update(
            before, c_inner, c_edge, est, rn, adjoint, None if last else (wx, ah, al),
            radius, per,
        )
        est = out[0]
        if not last:
            top, low, high = out[1:]
            beyond = ring(top, -1)
    return est


def solution(mesh):
    in_specs = (P(("grp", "slab"), "row", None), P("slab"), P(), P(), P())
    out_specs = P(("grp", "slab"), "row", None)
    return jax.shard_map(
        on_device, mesh=mesh, in_specs=in_specs, out_specs=out_specs, check_vma=False
    )
```

```python
import functools

import jax
import jax.numpy as jnp
from jax import lax
from jax.experimental import pallas as pl
from jax.experimental.pallas import tpu as pltpu
from jax.sharding import PartitionSpec as P

ITERS = 2
F32 = jnp.float32
BF16 = jnp.bfloat16
PARAMS = pltpu.CompilerParams(vmem_limit_bytes=40 * 1024 * 1024)
SMEM = pl.BlockSpec(memory_space=pltpu.SMEM)
VMEM = pl.BlockSpec(memory_space=pltpu.VMEM)
ANY = pl.BlockSpec(memory_space=pl.ANY)


def up(value, step):
    return -(-value // step) * step


def split(x):
    hi = x.astype(BF16)
    return hi, (x - hi.astype(F32)).astype(BF16)


def mm(a, b):
    return jnp.dot(a, b, preferred_element_type=F32)


def blur_rows(w_hi, w_lo, v_hi, v_lo):
    count = w_hi.shape[0]
    both = mm(jnp.concatenate([w_hi, w_lo], axis=0), v_hi)
    return both[:count] + both[count:] + mm(w_hi, v_lo)


def blur_columns(u, a_hi, a_lo):
    count = u.shape[0]
    u_hi, u_lo = split(u)
    both = mm(jnp.concatenate([u_hi, u_lo], axis=0), a_hi)
    return both[:count] + both[count:] + mm(u_hi, a_lo)


def cost(microseconds):
    return pl.CostEstimate(
        flops=int(microseconds * 1e9), bytes_accessed=int(microseconds * 3.5e6), transcendentals=0
    )


def full(shape):
    return pl.BlockSpec(shape, lambda i: (0,) * len(shape))


def planes(shape, per):
    return pl.BlockSpec((per,) + shape[1:], lambda i: (i,) + (0,) * (len(shape) - 1))


def shape_of(*dims, dtype=F32):
    return jax.ShapeDtypeStruct(dims, dtype)


def spread(ref, band, lanes, radius, flip):
    base = jnp.zeros(lanes.shape, F32)
    for k in range(2 * radius + 1):
        base = jnp.where(lanes == (2 * radius - k if flip else k), ref[band, k], base)
    return base


def iotas(rows, lanes):
    shape = (rows, lanes)
    return (
        lax.broadcasted_iota(jnp.int32, shape, 0),
        lax.broadcasted_iota(jnp.int32, shape, 1),
    )


def column_matrix(base, radius, h_ref, l_ref, p):
    columns = h_ref.shape[1]
    sub, lane = iotas(16, 128)
    rolled = {}
    sums = [None] * (columns // 128)
    for first in range(0, columns, 16):
        key = first % 128
        if key not in rolled:
            rolled[key] = pltpu.roll(base, (key - radius) % 128, 1, stride=1, stride_axis=0)
        for block in range(columns // 128):
            left = block * 128
            here = (p, slice(first, first + 16), slice(left, left + 128))
            if left > first + 15 + radius or left + 127 < first - radius:
                zero = jnp.zeros((16, 128), BF16)
                h_ref[here] = zero
                l_ref[here] = zero
                continue
            inside = jnp.abs(lane - sub + (left - first)) <= radius
            tile = jnp.where(inside, rolled[key], 0.0)
            h_ref[here], l_ref[here] = split(tile)
            sums[block] = tile if sums[block] is None else sums[block] + tile
    return [jnp.sum(s, axis=0, keepdims=True) for s in sums]


def row_matrix(base, rows, shift, width):
    return jnp.concatenate(
        [
            pltpu.roll(base, (first + shift) % width, 1, stride=1, stride_axis=0)
            for first in range(0, rows, 16)
        ],
        axis=0,
    )


def store_sends(v, plane, n, radius, low_ref, high_ref):
    @pl.when(plane < radius)
    def _():
        low_ref[jnp.minimum(plane, radius - 1)] = v

    @pl.when(plane >= n - radius)
    def _():
        high_ref[jnp.maximum(plane - (n - radius), 0)] = v


def own_rows(est, wx_ref, ah_ref, al_ref, p, inner):
    rows = est.shape[0]
    est_hi, est_lo = split(est)
    u = blur_rows(wx_ref[p, 0, :inner, :rows], wx_ref[p, 1, :inner, :rows], est_hi, est_lo)
    return blur_columns(u, ah_ref[p], al_ref[p])


def first_kernel(
    per, n, radius, halo, place_ref, band_ref, tx_ref, ty_ref, est_ref,
    ah_ref, al_ref, wx_ref, low_ref, high_ref,
):
    rows, width = wx_ref.shape[2], wx_ref.shape[3]
    _, lane = iotas(16, 128)
    _, wide = iotas(16, width)
    row, lanes = iotas(rows, width)
    keep = (place_ref[2] == 0) | ((row < rows - radius) == (lanes < rows))
    for p in range(per):
        plane = pl.program_id(0) * per + p
        band = band_ref[plane]
        column_matrix(spread(ty_ref, band, lane, radius, True), radius, ah_ref, al_ref, p)
        matrix = row_matrix(spread(tx_ref, band, wide, radius, False), rows, 0, width)
        wx_ref[p, 0], wx_ref[p, 1] = split(jnp.where(keep, matrix, 0.0))
        v = own_rows(est_ref[p], wx_ref, ah_ref, al_ref, p, rows - halo)
        store_sends(v, plane, n, radius, low_ref, high_ref)


def first_blur(place, band_index, taps_x, taps_y, est, halo, width, per):
    n, rows, columns = est.shape
    radius = taps_x.shape[1] // 2
    a = shape_of(n, columns, columns, dtype=BF16)
    w = shape_of(n, 2, rows, width, dtype=BF16)
    send = shape_of(radius, rows - halo, columns)
    return pl.pallas_call(
        functools.partial(first_kernel, per, n, radius, halo),
        grid=(n // per,),
        in_specs=[SMEM] * 4 + [planes(est.shape, per)],
        out_specs=[planes(x.shape, per) for x in (a, a, w)] + [full(send.shape)] * 2,
        out_shape=[a, a, w, send, send],
        compiler_params=PARAMS,
        cost_estimate=cost(1.0),
    )(place, band_index, taps_x, taps_y, est)


def second_kernel(
    per, n, radius, halo, depth, place_ref, band_ref, tx_ref, ty_ref, tz_ref, after_ref,
    obs_ref, next_ref, ah_ref, al_ref, wx_ref, rn_ref, shifted_ref,
):
    rows, width = wx_ref.shape[2], wx_ref.shape[3]
    _, lane = iotas(16, 128)
    _, wide = iotas(16, width)
    _, lanes = iotas(rows, width)
    lower = (place_ref[1] == 0) | (lanes >= rows - radius - (rows - halo))
    upper = (place_ref[2] == 0) | (lanes < rows - radius + halo)
    keep = ((lanes < halo) & lower) | ((lanes >= halo) & upper)
    for p in range(per):
        plane = pl.program_id(0) * per + p
        band = band_ref[plane]
        sums = column_matrix(
            spread(ty_ref, band, lane, radius, False), radius, ah_ref, al_ref, p
        )
        matrix = row_matrix(
            spread(tx_ref, band, wide, radius, True), rows, halo - 2 * radius, width
        )
        matrix = jnp.where(keep, matrix, 0.0)
        wx_ref[p, 0], wx_ref[p, 1] = split(matrix)
        along_x = jnp.sum(matrix, axis=1, keepdims=True)
        along_z = jnp.float32(0.0)
        z = place_ref[0] + plane
        for k in range(2 * radius + 1):
            source = z - k + radius
            inside = (source >= 0) & (source < depth)
            along_z = along_z + jnp.where(inside, tz_ref[k], 0.0)
        for block, along_y in enumerate(sums):
            rn_ref[p, :, block * 128 : block * 128 + 128] = 1.0 / (
                along_x * (along_y * along_z)
            )
        shifted_ref[p, : rows - radius] = obs_ref[p, radius:]
        shifted_ref[p, rows - radius :] = next_ref[p, :radius]


def second_weights(
    place, band_index, taps_x, taps_y, taps_z, after, obs, beyond, halo, width, depth, per
):
    n, rows, columns = obs.shape
    radius = taps_x.shape[1] // 2
    a = shape_of(n, columns, columns, dtype=BF16)
    w = shape_of(n, 2, rows, width, dtype=BF16)
    field = shape_of(*obs.shape)
    return pl.pallas_call(
        functools.partial(second_kernel, per, n, radius, halo, depth),
        grid=(n // per,),
        in_specs=[SMEM] * 5 + [ANY] + [planes(x.shape, per) for x in (obs, beyond)],
        out_specs=[planes(x.shape, per) for x in (a, a, w, field, field)],
        out_shape=[a, a, w, field, field],
        compiler_params=PARAMS,
        cost_estimate=cost(1.0),
    )(place, band_index, taps_x, taps_y, taps_z, after, obs, beyond)


def edge_kernel(
    per, n, radius, halo, est_ref, next_ref, wx_ref, ah_ref, al_ref, low_ref, high_ref
):
    rows = est_ref.shape[1]
    inner, used = rows - halo, rows + halo
    for p in range(per):
        plane = pl.program_id(0) * per + p
        v_hi, v_lo = split(jnp.concatenate([est_ref[p], next_ref[p]], axis=0))
        u = blur_rows(wx_ref[p, 0, inner:, :used], wx_ref[p, 1, inner:, :used], v_hi, v_lo)
        v = blur_columns(u, ah_ref[p], al_ref[p])
        store_sends(v, plane, n, radius, low_ref, high_ref)


def edge_blur(est, beyond, wx, ah, al, radius, per):
    n, _, columns = est.shape
    halo = beyond.shape[1]
    send = shape_of(radius, halo, columns)
    args = (est, beyond, wx, ah, al)
    return pl.pallas_call(
        functools.partial(edge_kernel, per, n, radius, halo),
        grid=(n // per,),
        in_specs=[planes(x.shape, per) for x in args],
        out_specs=[full(send.shape)] * 2,
        out_shape=[send] * 2,
        compiler_params=PARAMS,
        cost_estimate=cost(1.0),
    )(*args)


def depth_sum(n, radius, flip, tz_ref, refs, rows, lanes):
    low_ref, high_ref, zlo_ref, zhi_ref = refs
    last = 2 * radius
    taps = [tz_ref[last - k if flip else k] for k in range(last + 1)]
    total = [None] * n
    for j in range(-radius, n + radius):
        if j < 0:
            piece = zlo_ref[j + radius, rows, lanes]
        elif j < radius:
            piece = low_ref[j, rows, lanes]
        elif j < n:
            piece = high_ref[j - (n - radius), rows, lanes]
        else:
            piece = zhi_ref[j - n, rows, lanes]
        for i in range(max(0, j - radius), min(n, j + radius + 1)):
            term = taps[j - i + radius] * piece
            total[i] = term if total[i] is None else total[i] + term
    return total


def tiles(count, columns, body):
    def step(t, carry):
        for left in range(0, columns, 128):
            body(t * 8, slice(left, left + 128))
        return carry

    lax.fori_loop(0, count // 8, step, 0)


def at(start, offset):
    return pl.ds(pl.multiple_of(start + offset, 8), 8)


def ratio_kernel(n, radius, skip, obs_skip, tz_ref, obs_ref, *refs):
    rlow_ref, rhigh_ref = refs[-2:]
    _, count, columns = rlow_ref.shape

    def body(start, lanes):
        total = depth_sum(n, radius, False, tz_ref, refs[:4], at(start, skip), lanes)
        rows = at(start, 0)
        for i in range(n):
            ratio = obs_ref[i, at(start, obs_skip), lanes] / total[i]
            if i < radius:
                rlow_ref[i, rows, lanes] = ratio
            if i >= n - radius:
                rhigh_ref[i - (n - radius), rows, lanes] = ratio

    tiles(count, columns, body)


def depth_ratio(taps_z, obs, chunk, skip, obs_skip, count, after=None, micro=1.0):
    n, _, columns = obs.shape
    radius = taps_z.shape[0] // 2
    send = shape_of(radius, count, columns)
    extra = [] if after is None else [after]
    return pl.pallas_call(
        functools.partial(ratio_kernel, n, radius, skip, obs_skip),
        in_specs=[SMEM] + [VMEM] * 5 + [ANY] * len(extra),
        out_specs=[VMEM] * 2,
        out_shape=[send] * 2,
        compiler_params=PARAMS,
        cost_estimate=cost(micro),
    )(taps_z, obs, *chunk, *extra)


def back_kernel(n, radius, tz_ref, *refs):
    out_ref = refs[-1]
    _, count, columns = out_ref.shape

    def body(start, lanes):
        rows = at(start, 0)
        total = depth_sum(n, radius, True, tz_ref, refs[:4], rows, lanes)
        for i in range(n):
            out_ref[i, rows, lanes] = total[i]

    tiles(count, columns, body)


def depth_back(taps_z, chunk, n, after, micro=1.0):
    radius, count, columns = chunk[0].shape
    return pl.pallas_call(
        functools.partial(back_kernel, n, radius),
        in_specs=[SMEM] + [VMEM] * 4 + [ANY],
        out_specs=VMEM,
        out_shape=shape_of(n, count, columns),
        compiler_params=PARAMS,
        cost_estimate=cost(micro),
    )(taps_z, *chunk, after)


def update_kernel(per, n, radius, last, *refs):
    pieces, edge_ref, refs = refs[:4], refs[3], refs[4:]
    est_ref, rn_ref, wa_ref, bh_ref, bl_ref = refs[:5]
    refs = refs[5:]
    rows = est_ref.shape[1]
    halo = edge_ref.shape[1]
    if last:
        (out_ref,) = refs
    else:
        wx_ref, ah_ref, al_ref, out_ref, top_ref, low_ref, high_ref = refs
    for p in range(per):
        plane = pl.program_id(0) * per + p
        c = jnp.concatenate([piece[p] for piece in pieces], axis=0)
        c_hi, c_lo = split(c)
        used = rows + halo
        u = blur_rows(wa_ref[p, 0, :, :used], wa_ref[p, 1, :, :used], c_hi, c_lo)
        u = blur_columns(u, bh_ref[p], bl_ref[p])
        est = est_ref[p] * u * rn_ref[p]
        out_ref[p] = est
        if not last:
            top_ref[p] = est[:halo]
            v = own_rows(est, wx_ref, ah_ref, al_ref, p, rows - halo)
            store_sends(v, plane, n, radius, low_ref, high_ref)


def update(pieces, est, rn, adjoint, forward, radius, per):
    n, rows, columns = est.shape
    halo = pieces[0].shape[1]
    last = forward is None
    args = [*pieces, est, rn, *adjoint] + ([] if last else [*forward])
    out_specs, out_shape = [planes(est.shape, per)], [shape_of(*est.shape)]
    if not last:
        top = shape_of(n, halo, columns)
        send = shape_of(radius, rows - halo, columns)
        out_specs += [planes(top.shape, per)] + [full(send.shape)] * 2
        out_shape += [top, send, send]
    return pl.pallas_call(
        functools.partial(update_kernel, per, n, radius, last),
        grid=(n // per,),
        in_specs=[planes(x.shape, per) for x in args],
        out_specs=out_specs,
        out_shape=out_shape,
        compiler_params=PARAMS,
        cost_estimate=cost(1.0),
    )(*args)


def depth_exchange(low, high):
    count = lax.axis_size("slab")
    forward = [(i, i + 1) for i in range(count - 1)]
    backward = [(i + 1, i) for i in range(count - 1)]
    zlo = lax.ppermute(high, "slab", forward)
    zhi = lax.ppermute(low, "slab", backward)
    return low, high, zlo, zhi


def ring(x, step):
    count = lax.axis_size("row")
    return lax.ppermute(x, "row", [(i, (i + step) % count) for i in range(count)])


def on_device(observed, band_index, taps_x, taps_y, taps_z):
    n, rows, columns = observed.shape
    radius = taps_z.shape[0] // 2
    halo = up(2 * radius, 16)
    inner = rows - halo
    half = up(inner // 2, 16)
    width = up(rows + halo, 128)
    per = 4 if n % 4 == 0 else 1
    depth = n * lax.axis_size("slab")
    row = lax.axis_index("row")
    last_row = row == lax.axis_size("row") - 1
    place = jnp.stack([lax.axis_index("slab") * n, row == 0, last_row]).astype(jnp.int32)

    beyond = ring(observed[:, :halo], -1)
    ah, al, wx, low, high = first_blur(
        place, band_index, taps_x, taps_y, observed, halo, width, per
    )
    est, adjoint = observed, None
    for step in range(ITERS):
        v_inner = depth_exchange(low, high)
        low, high = edge_blur(est, beyond, wx, ah, al, radius, per)
        v_edge = depth_exchange(low, high)
        if adjoint is None:
            bh, bl, wa, rn, shifted = second_weights(
                place, band_index, taps_x, taps_y, taps_z, low, observed, beyond, halo,
                width, depth, per,
            )
            adjoint = (wa, bh, bl)
        r_first = depth_exchange(
            *depth_ratio(taps_z, shifted, v_inner, 0, 0, half, after=low)
        )
        r_edge = depth_exchange(*depth_ratio(taps_z, shifted, v_edge, 0, inner, halo, after=r_first[0]))
        r_second = depth_exchange(
            *depth_ratio(
                taps_z, shifted, v_inner, half, half, inner - half, after=r_edge[0]
            )
        )
        c_first = depth_back(taps_z, r_first, n, after=r_second[0], micro=5.0)
        c_edge = depth_back(taps_z, r_edge, n, after=c_first, micro=1.0)
        before = ring(c_edge, 1)
        c_second = depth_back(taps_z, r_second, n, after=c_edge, micro=100.0)
        last = step == ITERS - 1
        out = update(
            (before, c_first, c_second, c_edge), est, rn, adjoint,
            None if last else (wx, ah, al), radius, per,
        )
        est = out[0]
        if not last:
            top, low, high = out[1:]
            beyond = ring(top, -1)
    return est


def solution(mesh):
    in_specs = (P(("grp", "slab"), "row", None), P("slab"), P(), P(), P())
    out_specs = P(("grp", "slab"), "row", None)
    return jax.shard_map(
        on_device, mesh=mesh, in_specs=in_specs, out_specs=out_specs, check_vma=False
    )
```

```python
import functools

import jax
import jax.numpy as jnp
from jax import lax
from jax.experimental import pallas as pl
from jax.experimental.pallas import tpu as pltpu
from jax.sharding import PartitionSpec as P

ITERS = 2
F32 = jnp.float32
BF16 = jnp.bfloat16
PARAMS = pltpu.CompilerParams(vmem_limit_bytes=16 * 1024 * 1024)
SMEM = pl.BlockSpec(memory_space=pltpu.SMEM)
VMEM = pl.BlockSpec(memory_space=pltpu.VMEM)
ANY = pl.BlockSpec(memory_space=pl.ANY)


def up(value, step):
    return -(-value // step) * step


def split(x):
    hi = x.astype(BF16)
    return hi, (x - hi.astype(F32)).astype(BF16)


def mm(a, b):
    return jnp.dot(a, b, preferred_element_type=F32)


def blur_rows(w_hi, w_lo, v_hi, v_lo):
    count = w_hi.shape[0]
    both = mm(jnp.concatenate([w_hi, w_lo], axis=0), v_hi)
    return both[:count] + both[count:] + mm(w_hi, v_lo)


def blur_columns(u, a_hi, a_lo):
    count = u.shape[0]
    u_hi, u_lo = split(u)
    both = mm(jnp.concatenate([u_hi, u_lo], axis=0), a_hi)
    return both[:count] + both[count:] + mm(u_hi, a_lo)


def cost(microseconds):
    return pl.CostEstimate(
        flops=int(microseconds * 1e9), bytes_accessed=int(microseconds * 3.5e6), transcendentals=0
    )


def shape_of(*dims, dtype=F32):
    return jax.ShapeDtypeStruct(dims, dtype)


def spread(ref, band, lanes, radius, flip):
    base = jnp.zeros(lanes.shape, F32)
    for k in range(2 * radius + 1):
        base = jnp.where(lanes == (2 * radius - k if flip else k), ref[band, k], base)
    return base


def iotas(rows, lanes):
    shape = (rows, lanes)
    return (
        lax.broadcasted_iota(jnp.int32, shape, 0),
        lax.broadcasted_iota(jnp.int32, shape, 1),
    )


def column_matrix(base, radius, h_ref, l_ref, p):
    columns = h_ref.shape[1]
    sub, lane = iotas(16, 128)
    rolled = {}
    sums = [None] * (columns // 128)
    for first in range(0, columns, 16):
        key = first % 128
        if key not in rolled:
            rolled[key] = pltpu.roll(base, (key - radius) % 128, 1, stride=1, stride_axis=0)
        for block in range(columns // 128):
            left = block * 128
            here = (p, slice(first, first + 16), slice(left, left + 128))
            if left > first + 15 + radius or left + 127 < first - radius:
                zero = jnp.zeros((16, 128), BF16)
                h_ref[here] = zero
                l_ref[here] = zero
                continue
            inside = jnp.abs(lane - sub + (left - first)) <= radius
            tile = jnp.where(inside, rolled[key], 0.0)
            h_ref[here], l_ref[here] = split(tile)
            sums[block] = tile if sums[block] is None else sums[block] + tile
    return [jnp.sum(s, axis=0, keepdims=True) for s in sums]


def row_matrix(base, rows, shift, width):
    return jnp.concatenate(
        [
            pltpu.roll(base, (first + shift) % width, 1, stride=1, stride_axis=0)
            for first in range(0, rows, 16)
        ],
        axis=0,
    )


def store_sends(v, plane, n, radius, low_ref, high_ref):
    if plane < radius:
        low_ref[plane] = v
    if plane >= n - radius:
        high_ref[plane - (n - radius)] = v


def own_rows(est, wx_ref, ah_ref, al_ref, p, inner):
    rows = est.shape[0]
    w = blur_columns(est, ah_ref[p], al_ref[p])
    w_hi, w_lo = split(w)
    v = blur_rows(wx_ref[p, 0, :inner, :rows], wx_ref[p, 1, :inner, :rows], w_hi, w_lo)
    return w, v


def row_place():
    row = lax.axis_index("row")
    return row == 0, row == lax.axis_size("row") - 1


def first_kernel(
    n, radius, halo, band_ref, tx_ref, ty_ref, est_ref,
    ah_ref, al_ref, wx_ref, w_ref, low_ref, high_ref,
):
    rows, width = wx_ref.shape[2], wx_ref.shape[3]
    _, lane = iotas(16, 128)
    _, wide = iotas(16, width)
    row, lanes = iotas(rows, width)
    keep = jnp.logical_not(row_place()[1]) | ((row < rows - radius) == (lanes < rows))
    for p in range(n):
        band = band_ref[p]
        column_matrix(spread(ty_ref, band, lane, radius, True), radius, ah_ref, al_ref, p)
        matrix = row_matrix(spread(tx_ref, band, wide, radius, False), rows, 0, width)
        wx_ref[p, 0], wx_ref[p, 1] = split(jnp.where(keep, matrix, 0.0))
        w_ref[p], v = own_rows(est_ref[p], wx_ref, ah_ref, al_ref, p, rows - halo)
        store_sends(v, p, n, radius, low_ref, high_ref)


def first_blur(band_index, taps_x, taps_y, est, halo, width):
    n, rows, columns = est.shape
    radius = taps_x.shape[1] // 2
    a = shape_of(n, columns, columns, dtype=BF16)
    w = shape_of(n, 2, rows, width, dtype=BF16)
    send = shape_of(radius, rows - halo, columns)
    return pl.pallas_call(
        functools.partial(first_kernel, n, radius, halo),
        in_specs=[SMEM] * 3 + [VMEM],
        out_specs=[VMEM] * 6,
        out_shape=[a, a, w, shape_of(*est.shape), send, send],
        compiler_params=PARAMS,
        cost_estimate=cost(1.0),
    )(band_index, taps_x, taps_y, est)


def second_kernel(
    n, radius, halo, band_ref, tx_ref, ty_ref, tz_ref, after_ref,
    obs_ref, next_ref, ah_ref, al_ref, wx_ref, rn_ref, shifted_ref,
):
    rows, width = wx_ref.shape[2], wx_ref.shape[3]
    first_row, last_row = row_place()
    below = lax.axis_index("slab") * n
    depth = lax.axis_size("slab") * n
    _, lane = iotas(16, 128)
    _, wide = iotas(16, width)
    _, lanes = iotas(rows, width)
    lower = jnp.logical_not(first_row) | (lanes >= halo - radius)
    upper = jnp.logical_not(last_row) | (lanes < rows - radius + halo)
    keep = ((lanes < halo) & lower) | ((lanes >= halo) & upper)
    for p in range(n):
        band = band_ref[p]
        sums = column_matrix(
            spread(ty_ref, band, lane, radius, False), radius, ah_ref, al_ref, p
        )
        matrix = row_matrix(
            spread(tx_ref, band, wide, radius, True), rows, halo - 2 * radius, width
        )
        matrix = jnp.where(keep, matrix, 0.0)
        wx_ref[p, 0], wx_ref[p, 1] = split(matrix)
        along_x = jnp.sum(matrix, axis=1, keepdims=True)
        along_z = jnp.float32(0.0)
        z = below + p
        for k in range(2 * radius + 1):
            source = z - k + radius
            inside = (source >= 0) & (source < depth)
            along_z = along_z + jnp.where(inside, tz_ref[k], 0.0)
        for block, along_y in enumerate(sums):
            rn_ref[p, :, block * 128 : block * 128 + 128] = 1.0 / (
                along_x * (along_y * along_z)
            )
        shifted_ref[p, : rows - radius] = obs_ref[p, radius:]
        shifted_ref[p, rows - radius :] = next_ref[p, :radius]


def second_weights(band_index, taps_x, taps_y, taps_z, after, obs, beyond, width):
    n, rows, columns = obs.shape
    halo = beyond.shape[1]
    radius = taps_x.shape[1] // 2
    a = shape_of(n, columns, columns, dtype=BF16)
    w = shape_of(n, 2, rows, width, dtype=BF16)
    field = shape_of(*obs.shape)
    return pl.pallas_call(
        functools.partial(second_kernel, n, radius, halo),
        in_specs=[SMEM] * 4 + [ANY] + [VMEM] * 2,
        out_specs=[VMEM] * 5,
        out_shape=[a, a, w, field, field],
        compiler_params=PARAMS,
        cost_estimate=cost(1.0),
    )(band_index, taps_x, taps_y, taps_z, after, obs, beyond)


def edge_kernel(n, radius, blurred, w_ref, next_ref, wx_ref, *refs):
    rows, halo = w_ref.shape[1], next_ref.shape[1]
    inner, used = rows - halo, rows + halo
    if not blurred:
        ah_ref, al_ref = refs[:2]
    for p in range(n):
        beyond = next_ref[p]
        if not blurred:
            beyond = blur_columns(beyond, ah_ref[p], al_ref[p])
        w_hi, w_lo = split(jnp.concatenate([w_ref[p], beyond], axis=0))
        v = blur_rows(wx_ref[p, 0, inner:, :used], wx_ref[p, 1, inner:, :used], w_hi, w_lo)
        store_sends(v, p, n, radius, *refs[-2:])


def edge_blur(w, beyond, wx, columns_matrix, radius):
    n, _, columns = w.shape
    halo = beyond.shape[1]
    send = shape_of(radius, halo, columns)
    args = (w, beyond, wx, *columns_matrix)
    return pl.pallas_call(
        functools.partial(edge_kernel, n, radius, not columns_matrix),
        in_specs=[VMEM] * len(args),
        out_specs=[VMEM] * 2,
        out_shape=[send] * 2,
        compiler_params=PARAMS,
        cost_estimate=cost(1.0),
    )(*args)


def depth_sum(n, radius, flip, tz_ref, refs, rows, lanes):
    low_ref, high_ref, zlo_ref, zhi_ref = refs
    last = 2 * radius
    taps = [tz_ref[last - k if flip else k] for k in range(last + 1)]
    total = [None] * n
    for j in range(-radius, n + radius):
        if j < 0:
            piece = zlo_ref[j + radius, rows, lanes]
        elif j < radius:
            piece = low_ref[j, rows, lanes]
        elif j < n:
            piece = high_ref[j - (n - radius), rows, lanes]
        else:
            piece = zhi_ref[j - n, rows, lanes]
        for i in range(max(0, j - radius), min(n, j + radius + 1)):
            term = taps[j - i + radius] * piece
            total[i] = term if total[i] is None else total[i] + term
    return total


def tiles(count, columns, body):
    def step(t, carry):
        for left in range(0, columns, 128):
            body(t * 8, slice(left, left + 128))
        return carry

    lax.fori_loop(0, count // 8, step, 0)


def at(start, offset):
    return pl.ds(pl.multiple_of(start + offset, 8), 8)


def ratio_kernel(n, radius, skip, obs_skip, tz_ref, obs_ref, *refs):
    rlow_ref, rhigh_ref = refs[-2:]
    _, count, columns = rlow_ref.shape

    def body(start, lanes):
        total = depth_sum(n, radius, False, tz_ref, refs[:4], at(start, skip), lanes)
        rows = at(start, 0)
        for i in range(n):
            ratio = obs_ref[i, at(start, obs_skip), lanes] / total[i]
            if i < radius:
                rlow_ref[i, rows, lanes] = ratio
            if i >= n - radius:
                rhigh_ref[i - (n - radius), rows, lanes] = ratio

    tiles(count, columns, body)


def depth_ratio(taps_z, obs, chunk, skip, obs_skip, count, after=None, micro=1.0):
    n, _, columns = obs.shape
    radius = taps_z.shape[0] // 2
    send = shape_of(radius, count, columns)
    extra = [] if after is None else [after]
    return pl.pallas_call(
        functools.partial(ratio_kernel, n, radius, skip, obs_skip),
        in_specs=[SMEM] + [VMEM] * 5 + [ANY] * len(extra),
        out_specs=[VMEM] * 2,
        out_shape=[send] * 2,
        compiler_params=PARAMS,
        cost_estimate=cost(micro),
    )(taps_z, obs, *chunk, *extra)


def back_kernel(n, radius, tz_ref, *refs):
    out_ref = refs[-1]
    _, count, columns = out_ref.shape

    def body(start, lanes):
        rows = at(start, 0)
        total = depth_sum(n, radius, True, tz_ref, refs[:4], rows, lanes)
        for i in range(n):
            out_ref[i, rows, lanes] = total[i]

    tiles(count, columns, body)


def depth_back(taps_z, chunk, n, after, micro=1.0):
    radius, count, columns = chunk[0].shape
    return pl.pallas_call(
        functools.partial(back_kernel, n, radius),
        in_specs=[SMEM] + [VMEM] * 4 + [ANY],
        out_specs=VMEM,
        out_shape=shape_of(n, count, columns),
        compiler_params=PARAMS,
        cost_estimate=cost(micro),
    )(taps_z, *chunk, after)


def update_kernel(n, radius, last, *refs):
    pieces, edge_ref, refs = refs[:4], refs[3], refs[4:]
    est_ref, rn_ref, wa_ref, bh_ref, bl_ref = refs[:5]
    refs = refs[5:]
    rows = est_ref.shape[1]
    halo = edge_ref.shape[1]
    used = rows + halo
    if last:
        (out_ref,) = refs
    else:
        wx_ref, ah_ref, al_ref, out_ref, w_ref, top_ref, low_ref, high_ref = refs
    for p in range(n):
        c = jnp.concatenate([piece[p] for piece in pieces], axis=0)
        c_hi, c_lo = split(c)
        u = blur_rows(wa_ref[p, 0, :, :used], wa_ref[p, 1, :, :used], c_hi, c_lo)
        u = blur_columns(u, bh_ref[p], bl_ref[p])
        est = est_ref[p] * u * rn_ref[p]
        out_ref[p] = est
        if not last:
            w, v = own_rows(est, wx_ref, ah_ref, al_ref, p, rows - halo)
            w_ref[p] = w
            top_ref[p] = w[:halo]
            store_sends(v, p, n, radius, low_ref, high_ref)


def update(pieces, est, rn, adjoint, forward, radius):
    n, rows, columns = est.shape
    halo = pieces[0].shape[1]
    last = forward is None
    args = [*pieces, est, rn, *adjoint] + ([] if last else [*forward])
    out_shape = [shape_of(*est.shape)]
    if not last:
        send = shape_of(radius, rows - halo, columns)
        out_shape += [shape_of(*est.shape), shape_of(n, halo, columns), send, send]
    return pl.pallas_call(
        functools.partial(update_kernel, n, radius, last),
        in_specs=[VMEM] * len(args),
        out_specs=[VMEM] * len(out_shape),
        out_shape=out_shape,
        compiler_params=PARAMS,
        cost_estimate=cost(1.0),
    )(*args)


def depth_exchange(low, high):
    count = lax.axis_size("slab")
    forward = [(i, i + 1) for i in range(count - 1)]
    backward = [(i + 1, i) for i in range(count - 1)]
    zlo = lax.ppermute(high, "slab", forward)
    zhi = lax.ppermute(low, "slab", backward)
    return low, high, zlo, zhi


def ring(x, step):
    count = lax.axis_size("row")
    return lax.ppermute(x, "row", [(i, (i + step) % count) for i in range(count)])


def on_device(observed, band_index, taps_x, taps_y, taps_z):
    n, rows, columns = observed.shape
    radius = taps_z.shape[0] // 2
    halo = up(2 * radius, 16)
    inner = rows - halo
    half = up(inner // 2, 16)
    width = up(rows + halo, 128)
    beyond = ring(observed[:, :halo], -1)
    ah, al, wx, w, low, high = first_blur(
        band_index, taps_x, taps_y, observed, halo, width
    )
    est, adjoint = observed, None
    for step in range(ITERS):
        v_inner = depth_exchange(low, high)
        low, high = edge_blur(w, beyond, wx, () if step else (ah, al), radius)
        v_edge = depth_exchange(low, high)
        if adjoint is None:
            bh, bl, wa, rn, shifted = second_weights(
                band_index, taps_x, taps_y, taps_z, low, observed, beyond, width
            )
            adjoint = (wa, bh, bl)
        r_first = depth_exchange(
            *depth_ratio(taps_z, shifted, v_inner, 0, 0, half, after=low)
        )
        r_edge = depth_exchange(*depth_ratio(taps_z, shifted, v_edge, 0, inner, halo, after=r_first[0]))
        r_second = depth_exchange(
            *depth_ratio(
                taps_z, shifted, v_inner, half, half, inner - half, after=r_edge[0]
            )
        )
        c_first = depth_back(taps_z, r_first, n, after=r_second[0], micro=5.0)
        c_edge = depth_back(taps_z, r_edge, n, after=c_first, micro=1.0)
        before = ring(c_edge, 1)
        c_second = depth_back(taps_z, r_second, n, after=c_edge, micro=100.0)
        last = step == ITERS - 1
        out = update(
            (before, c_first, c_second, c_edge), est, rn, adjoint,
            None if last else (wx, ah, al), radius,
        )
        est = out[0]
        if not last:
            w, top, low, high = out[1:]
            beyond = ring(top, -1)
    return est


def solution(mesh):
    in_specs = (P(("grp", "slab"), "row", None), P("slab"), P(), P(), P())
    out_specs = P(("grp", "slab"), "row", None)
    return jax.shard_map(
        on_device, mesh=mesh, in_specs=in_specs, out_specs=out_specs, check_vma=False
    )
```

```python
import functools

import jax
import jax.numpy as jnp
from jax import lax
from jax.experimental import pallas as pl
from jax.experimental.pallas import tpu as pltpu
from jax.sharding import PartitionSpec as P

ITERS = 2
F32 = jnp.float32
BF16 = jnp.bfloat16
PARAMS = pltpu.CompilerParams(vmem_limit_bytes=16 * 1024 * 1024)
SMEM = pl.BlockSpec(memory_space=pltpu.SMEM)
VMEM = pl.BlockSpec(memory_space=pltpu.VMEM)
ANY = pl.BlockSpec(memory_space=pl.ANY)


def up(value, step):
    return -(-value // step) * step


def split(x):
    hi = x.astype(BF16)
    return hi, (x - hi.astype(F32)).astype(BF16)


def mm(a, b):
    return jnp.dot(a, b, preferred_element_type=F32)


def blur_rows(w_hi, w_lo, v_hi, v_lo):
    count = w_hi.shape[0]
    both = mm(jnp.concatenate([w_hi, w_lo], axis=0), v_hi)
    return both[:count] + both[count:] + mm(w_hi, v_lo)


def blur_columns(u, a_hi, a_lo):
    count = u.shape[0]
    u_hi, u_lo = split(u)
    both = mm(jnp.concatenate([u_hi, u_lo], axis=0), a_hi)
    return both[:count] + both[count:] + mm(u_hi, a_lo)


def cost(microseconds):
    return pl.CostEstimate(
        flops=int(microseconds * 1e9), bytes_accessed=int(microseconds * 3.5e6), transcendentals=0
    )


def shape_of(*dims, dtype=F32):
    return jax.ShapeDtypeStruct(dims, dtype)


def spread(ref, band, lanes, radius, flip):
    base = jnp.zeros(lanes.shape, F32)
    for k in range(2 * radius + 1):
        base = jnp.where(lanes == (2 * radius - k if flip else k), ref[band, k], base)
    return base


def iotas(rows, lanes):
    shape = (rows, lanes)
    return (
        lax.broadcasted_iota(jnp.int32, shape, 0),
        lax.broadcasted_iota(jnp.int32, shape, 1),
    )


def column_matrix(base, radius, h_ref, l_ref, p):
    columns = h_ref.shape[1]
    sub, lane = iotas(16, 128)
    rolled = {}
    sums = [None] * (columns // 128)
    for first in range(0, columns, 16):
        key = first % 128
        if key not in rolled:
            rolled[key] = pltpu.roll(base, (key - radius) % 128, 1, stride=1, stride_axis=0)
        for block in range(columns // 128):
            left = block * 128
            here = (p, slice(first, first + 16), slice(left, left + 128))
            if left > first + 15 + radius or left + 127 < first - radius:
                zero = jnp.zeros((16, 128), BF16)
                h_ref[here] = zero
                l_ref[here] = zero
                continue
            inside = jnp.abs(lane - sub + (left - first)) <= radius
            tile = jnp.where(inside, rolled[key], 0.0)
            h_ref[here], l_ref[here] = split(tile)
            sums[block] = tile if sums[block] is None else sums[block] + tile
    return [jnp.sum(s, axis=0, keepdims=True) for s in sums]


def row_matrix(base, rows, shift, width):
    return jnp.concatenate(
        [
            pltpu.roll(base, (first + shift) % width, 1, stride=1, stride_axis=0)
            for first in range(0, rows, 16)
        ],
        axis=0,
    )


def store_sends(v, plane, n, radius, low_ref, high_ref):
    if plane < radius:
        low_ref[plane] = v
    if plane >= n - radius:
        high_ref[plane - (n - radius)] = v


def all_columns(source, a_refs, out_ref):
    for p in range(out_ref.shape[0]):
        out_ref[p] = blur_columns(source(p), a_refs[0][p], a_refs[1][p])


def own_rows(w_ref, wx_ref, low_ref, high_ref):
    n, rows, _ = w_ref.shape
    radius, inner, _ = low_ref.shape
    for p in range(n):
        w_hi, w_lo = split(w_ref[p])
        v = blur_rows(wx_ref[p, 0, :inner, :rows], wx_ref[p, 1, :inner, :rows], w_hi, w_lo)
        store_sends(v, p, n, radius, low_ref, high_ref)


def row_place():
    row = lax.axis_index("row")
    return row == 0, row == lax.axis_size("row") - 1


def first_kernel(
    n, radius, band_hbm, tx_hbm, ty_hbm, est_hbm,
    ah_ref, al_ref, wx_ref, w_ref, low_ref, high_ref,
    band_ref, tx_ref, ty_ref, est_ref, sems,
):
    pairs = ((band_hbm, band_ref), (tx_hbm, tx_ref), (ty_hbm, ty_ref), (est_hbm, est_ref))
    copies = [pltpu.make_async_copy(a, b, sems.at[k]) for k, (a, b) in enumerate(pairs)]
    for copy in copies:
        copy.start()
    rows, width = wx_ref.shape[2], wx_ref.shape[3]
    _, lane = iotas(16, 128)
    _, wide = iotas(16, width)
    row, lanes = iotas(rows, width)
    keep = jnp.logical_not(row_place()[1]) | ((row < rows - radius) == (lanes < rows))
    for copy in copies:
        copy.wait()
    for p in range(n):
        band = band_ref[p]
        column_matrix(spread(ty_ref, band, lane, radius, True), radius, ah_ref, al_ref, p)
        matrix = row_matrix(spread(tx_ref, band, wide, radius, False), rows, 0, width)
        wx_ref[p, 0], wx_ref[p, 1] = split(jnp.where(keep, matrix, 0.0))
    all_columns(lambda p: est_ref[p], (ah_ref, al_ref), w_ref)
    own_rows(w_ref, wx_ref, low_ref, high_ref)


def first_blur(band_index, taps_x, taps_y, est, halo, width):
    n, rows, columns = est.shape
    radius = taps_x.shape[1] // 2
    a = shape_of(n, columns, columns, dtype=BF16)
    w = shape_of(n, 2, rows, width, dtype=BF16)
    send = shape_of(radius, rows - halo, columns)
    return pl.pallas_call(
        functools.partial(first_kernel, n, radius),
        in_specs=[pl.BlockSpec(memory_space=pltpu.HBM)] * 4,
        scratch_shapes=[
            pltpu.SMEM(band_index.shape, jnp.int32),
            pltpu.SMEM(taps_x.shape, F32),
            pltpu.SMEM(taps_y.shape, F32),
            pltpu.VMEM(est.shape, F32),
            pltpu.SemaphoreType.DMA((4,)),
        ],
        out_specs=[VMEM] * 6,
        out_shape=[a, a, w, shape_of(*est.shape), send, send],
        compiler_params=PARAMS,
        cost_estimate=cost(1.0),
    )(band_index, taps_x, taps_y, est)


def second_kernel(
    n, radius, halo, band_ref, tx_ref, ty_ref, tz_ref, after_ref,
    obs_ref, next_ref, ah_ref, al_ref, wx_ref, rn_ref, shifted_ref,
):
    rows, width = wx_ref.shape[2], wx_ref.shape[3]
    first_row, last_row = row_place()
    below = lax.axis_index("slab") * n
    depth = lax.axis_size("slab") * n
    _, lane = iotas(16, 128)
    _, wide = iotas(16, width)
    _, lanes = iotas(rows, width)
    lower = jnp.logical_not(first_row) | (lanes >= halo - radius)
    upper = jnp.logical_not(last_row) | (lanes < rows - radius + halo)
    keep = ((lanes < halo) & lower) | ((lanes >= halo) & upper)
    for p in range(n):
        band = band_ref[p]
        sums = column_matrix(
            spread(ty_ref, band, lane, radius, False), radius, ah_ref, al_ref, p
        )
        matrix = row_matrix(
            spread(tx_ref, band, wide, radius, True), rows, halo - 2 * radius, width
        )
        matrix = jnp.where(keep, matrix, 0.0)
        wx_ref[p, 0], wx_ref[p, 1] = split(matrix)
        along_x = jnp.sum(matrix, axis=1, keepdims=True)
        along_z = jnp.float32(0.0)
        z = below + p
        for k in range(2 * radius + 1):
            source = z - k + radius
            inside = (source >= 0) & (source < depth)
            along_z = along_z + jnp.where(inside, tz_ref[k], 0.0)
        for block, along_y in enumerate(sums):
            rn_ref[p, :, block * 128 : block * 128 + 128] = 1.0 / (
                along_x * (along_y * along_z)
            )
        shifted_ref[p, : rows - radius] = obs_ref[p, radius:]
        shifted_ref[p, rows - radius :] = next_ref[p, :radius]


def second_weights(band_index, taps_x, taps_y, taps_z, after, obs, beyond, width):
    n, rows, columns = obs.shape
    halo = beyond.shape[1]
    radius = taps_x.shape[1] // 2
    a = shape_of(n, columns, columns, dtype=BF16)
    w = shape_of(n, 2, rows, width, dtype=BF16)
    field = shape_of(*obs.shape)
    return pl.pallas_call(
        functools.partial(second_kernel, n, radius, halo),
        in_specs=[SMEM] * 4 + [ANY] + [VMEM] * 2,
        out_specs=[VMEM] * 5,
        out_shape=[a, a, w, field, field],
        compiler_params=PARAMS,
        cost_estimate=cost(1.0),
    )(band_index, taps_x, taps_y, taps_z, after, obs, beyond)


def edge_kernel(n, radius, blurred, w_ref, next_ref, wx_ref, *refs):
    rows, halo = w_ref.shape[1], next_ref.shape[1]
    inner, used = rows - halo, rows + halo
    beyond_ref = next_ref
    if not blurred:
        beyond_ref, refs = refs[-1], refs[:-1]
        all_columns(lambda p: next_ref[p], refs[:2], beyond_ref)
    for p in range(n):
        w_hi, w_lo = split(jnp.concatenate([w_ref[p], beyond_ref[p]], axis=0))
        v = blur_rows(wx_ref[p, 0, inner:, :used], wx_ref[p, 1, inner:, :used], w_hi, w_lo)
        store_sends(v, p, n, radius, *refs[-2:])


def edge_blur(w, beyond, wx, columns_matrix, radius):
    n, _, columns = w.shape
    halo = beyond.shape[1]
    send = shape_of(radius, halo, columns)
    args = (w, beyond, wx, *columns_matrix)
    return pl.pallas_call(
        functools.partial(edge_kernel, n, radius, not columns_matrix),
        in_specs=[VMEM] * len(args),
        out_specs=[VMEM] * 2,
        out_shape=[send] * 2,
        scratch_shapes=[pltpu.VMEM(beyond.shape, F32)] if columns_matrix else [],
        compiler_params=PARAMS,
        cost_estimate=cost(1.0),
    )(*args)


def depth_sum(n, radius, flip, tz_ref, refs, rows, lanes):
    low_ref, high_ref, zlo_ref, zhi_ref = refs
    last = 2 * radius
    taps = [tz_ref[last - k if flip else k] for k in range(last + 1)]
    total = [None] * n
    for j in range(-radius, n + radius):
        if j < 0:
            piece = zlo_ref[j + radius, rows, lanes]
        elif j < radius:
            piece = low_ref[j, rows, lanes]
        elif j < n:
            piece = high_ref[j - (n - radius), rows, lanes]
        else:
            piece = zhi_ref[j - n, rows, lanes]
        for i in range(max(0, j - radius), min(n, j + radius + 1)):
            term = taps[j - i + radius] * piece
            total[i] = term if total[i] is None else total[i] + term
    return total


def tiles(count, columns, body):
    def step(t, carry):
        for left in range(0, columns, 128):
            body(t * 8, slice(left, left + 128))
        return carry

    lax.fori_loop(0, count // 8, step, 0)


def at(start, offset):
    return pl.ds(pl.multiple_of(start + offset, 8), 8)


def ratio_kernel(n, radius, skip, obs_skip, tz_ref, obs_ref, *refs):
    rlow_ref, rhigh_ref = refs[-2:]
    _, count, columns = rlow_ref.shape

    def body(start, lanes):
        total = depth_sum(n, radius, False, tz_ref, refs[:4], at(start, skip), lanes)
        rows = at(start, 0)
        for i in range(n):
            ratio = obs_ref[i, at(start, obs_skip), lanes] / total[i]
            if i < radius:
                rlow_ref[i, rows, lanes] = ratio
            if i >= n - radius:
                rhigh_ref[i - (n - radius), rows, lanes] = ratio

    tiles(count, columns, body)


def depth_ratio(taps_z, obs, chunk, skip, obs_skip, count, after=None, micro=1.0):
    n, _, columns = obs.shape
    radius = taps_z.shape[0] // 2
    send = shape_of(radius, count, columns)
    extra = [] if after is None else [after]
    return pl.pallas_call(
        functools.partial(ratio_kernel, n, radius, skip, obs_skip),
        in_specs=[SMEM] + [VMEM] * 5 + [ANY] * len(extra),
        out_specs=[VMEM] * 2,
        out_shape=[send] * 2,
        compiler_params=PARAMS,
        cost_estimate=cost(micro),
    )(taps_z, obs, *chunk, *extra)


def back_kernel(n, radius, tz_ref, *refs):
    out_ref = refs[-1]
    _, count, columns = out_ref.shape

    def body(start, lanes):
        rows = at(start, 0)
        total = depth_sum(n, radius, True, tz_ref, refs[:4], rows, lanes)
        for i in range(n):
            out_ref[i, rows, lanes] = total[i]

    tiles(count, columns, body)


def depth_back(taps_z, chunk, n, after, micro=1.0):
    radius, count, columns = chunk[0].shape
    return pl.pallas_call(
        functools.partial(back_kernel, n, radius),
        in_specs=[SMEM] + [VMEM] * 4 + [ANY],
        out_specs=VMEM,
        out_shape=shape_of(n, count, columns),
        compiler_params=PARAMS,
        cost_estimate=cost(micro),
    )(taps_z, *chunk, after)


def update_kernel(n, last, *refs):
    pieces, edge_ref, refs = refs[:4], refs[3], refs[4:]
    est_ref, rn_ref, wa_ref, bh_ref, bl_ref = refs[:5]
    refs = refs[5:]
    rows = est_ref.shape[1]
    halo = edge_ref.shape[1]
    used = rows + halo
    u_ref, refs = refs[-1], refs[:-1]
    if last:
        (out_ref,) = refs
    else:
        wx_ref, ah_ref, al_ref, out_ref, w_ref, top_ref, low_ref, high_ref = refs
    for p in range(n):
        c_hi, c_lo = split(jnp.concatenate([piece[p] for piece in pieces], axis=0))
        u_ref[p] = blur_rows(wa_ref[p, 0, :, :used], wa_ref[p, 1, :, :used], c_hi, c_lo)
    for p in range(n):
        u = blur_columns(u_ref[p], bh_ref[p], bl_ref[p])
        out_ref[p] = est_ref[p] * u * rn_ref[p]
    if not last:
        all_columns(lambda p: out_ref[p], (ah_ref, al_ref), w_ref)
        for p in range(n):
            top_ref[p] = w_ref[p, :halo]
        own_rows(w_ref, wx_ref, low_ref, high_ref)


def update(pieces, est, rn, adjoint, forward, radius):
    n, rows, columns = est.shape
    halo = pieces[0].shape[1]
    last = forward is None
    args = [*pieces, est, rn, *adjoint] + ([] if last else [*forward])
    out_shape = [shape_of(*est.shape)]
    if not last:
        send = shape_of(radius, rows - halo, columns)
        out_shape += [shape_of(*est.shape), shape_of(n, halo, columns), send, send]
    return pl.pallas_call(
        functools.partial(update_kernel, n, last),
        in_specs=[VMEM] * len(args),
        out_specs=[VMEM] * len(out_shape),
        out_shape=out_shape,
        scratch_shapes=[pltpu.VMEM(est.shape, F32)],
        compiler_params=PARAMS,
        cost_estimate=cost(1.0),
    )(*args)


def depth_exchange(low, high):
    count = lax.axis_size("slab")
    forward = [(i, i + 1) for i in range(count - 1)]
    backward = [(i + 1, i) for i in range(count - 1)]
    zlo = lax.ppermute(high, "slab", forward)
    zhi = lax.ppermute(low, "slab", backward)
    return low, high, zlo, zhi


def ring(x, step):
    count = lax.axis_size("row")
    return lax.ppermute(x, "row", [(i, (i + step) % count) for i in range(count)])


def on_device(observed, band_index, taps_x, taps_y, taps_z):
    n, rows, columns = observed.shape
    radius = taps_z.shape[0] // 2
    halo = up(2 * radius, 16)
    inner = rows - halo
    half = up(inner // 2, 16)
    width = up(rows + halo, 128)
    beyond = ring(observed[:, :halo], -1)
    ah, al, wx, w, low, high = first_blur(
        band_index, taps_x, taps_y, observed, halo, width
    )
    est, adjoint = observed, None
    for step in range(ITERS):
        v_inner = depth_exchange(low, high)
        low, high = edge_blur(w, beyond, wx, () if step else (ah, al), radius)
        v_edge = depth_exchange(low, high)
        if adjoint is None:
            bh, bl, wa, rn, shifted = second_weights(
                band_index, taps_x, taps_y, taps_z, low, observed, beyond, width
            )
            adjoint = (wa, bh, bl)
        r_first = depth_exchange(
            *depth_ratio(taps_z, shifted, v_inner, 0, 0, half, after=low)
        )
        r_edge = depth_exchange(*depth_ratio(taps_z, shifted, v_edge, 0, inner, halo, after=r_first[0]))
        r_second = depth_exchange(
            *depth_ratio(
                taps_z, shifted, v_inner, half, half, inner - half, after=r_edge[0]
            )
        )
        c_first = depth_back(taps_z, r_first, n, after=r_second[0], micro=5.0)
        c_edge = depth_back(taps_z, r_edge, n, after=c_first, micro=1.0)
        before = ring(c_edge, 1)
        c_second = depth_back(taps_z, r_second, n, after=c_edge, micro=100.0)
        last = step == ITERS - 1
        out = update(
            (before, c_first, c_second, c_edge), est, rn, adjoint,
            None if last else (wx, ah, al), radius,
        )
        est = out[0]
        if not last:
            w, top, low, high = out[1:]
            beyond = ring(top, -1)
    return est


def solution(mesh):
    in_specs = (P(("grp", "slab"), "row", None), P("slab"), P(), P(), P())
    out_specs = P(("grp", "slab"), "row", None)
    return jax.shard_map(
        on_device, mesh=mesh, in_specs=in_specs, out_specs=out_specs, check_vma=False
    )
```

```python
import functools

import jax
import jax.numpy as jnp
from jax import lax
from jax.experimental import pallas as pl
from jax.experimental.pallas import tpu as pltpu
from jax.sharding import PartitionSpec as P

ITERS = 2
F32 = jnp.float32
BF16 = jnp.bfloat16
PARAMS = pltpu.CompilerParams(vmem_limit_bytes=16 * 1024 * 1024)
SMEM = pl.BlockSpec(memory_space=pltpu.SMEM)
VMEM = pl.BlockSpec(memory_space=pltpu.VMEM)
ANY = pl.BlockSpec(memory_space=pl.ANY)


def up(value, step):
    return -(-value // step) * step


def split(x):
    hi = x.astype(BF16)
    return hi, (x - hi.astype(F32)).astype(BF16)


def mm(a, b):
    return jnp.dot(a, b, preferred_element_type=F32)


def blur_rows(w_hi, w_lo, v_hi, v_lo):
    count = w_hi.shape[0]
    both = mm(jnp.concatenate([w_hi, w_lo], axis=0), v_hi)
    return both[:count] + both[count:] + mm(w_hi, v_lo)


def blur_columns(u, a_hi, a_lo):
    count = u.shape[0]
    u_hi, u_lo = split(u)
    both = mm(jnp.concatenate([u_hi, u_lo], axis=0), a_hi)
    return both[:count] + both[count:] + mm(u_hi, a_lo)


def cost(microseconds):
    return pl.CostEstimate(
        flops=int(microseconds * 1e9), bytes_accessed=int(microseconds * 3.5e6), transcendentals=0
    )


def shape_of(*dims, dtype=F32):
    return jax.ShapeDtypeStruct(dims, dtype)


def spread(ref, band, lanes, radius, flip):
    base = jnp.zeros(lanes.shape, F32)
    for k in range(2 * radius + 1):
        base = jnp.where(lanes == (2 * radius - k if flip else k), ref[band, k], base)
    return base


def iotas(rows, lanes):
    shape = (rows, lanes)
    return (
        lax.broadcasted_iota(jnp.int32, shape, 0),
        lax.broadcasted_iota(jnp.int32, shape, 1),
    )


def column_matrix(base, radius, h_ref, l_ref, p):
    columns = h_ref.shape[1]
    sub, lane = iotas(16, 128)
    rolled = {}
    sums = [None] * (columns // 128)
    for first in range(0, columns, 16):
        key = first % 128
        if key not in rolled:
            rolled[key] = pltpu.roll(base, (key - radius) % 128, 1, stride=1, stride_axis=0)
        for block in range(columns // 128):
            left = block * 128
            here = (p, slice(first, first + 16), slice(left, left + 128))
            if left > first + 15 + radius or left + 127 < first - radius:
                zero = jnp.zeros((16, 128), BF16)
                h_ref[here] = zero
                l_ref[here] = zero
                continue
            inside = jnp.abs(lane - sub + (left - first)) <= radius
            tile = jnp.where(inside, rolled[key], 0.0)
            h_ref[here], l_ref[here] = split(tile)
            sums[block] = tile if sums[block] is None else sums[block] + tile
    return [jnp.sum(s, axis=0, keepdims=True) for s in sums]


def row_matrix(base, rows, shift, width):
    return jnp.concatenate(
        [
            pltpu.roll(base, (first + shift) % width, 1, stride=1, stride_axis=0)
            for first in range(0, rows, 16)
        ],
        axis=0,
    )


def store_sends(v, plane, n, radius, low_ref, high_ref):
    if plane < radius:
        low_ref[plane] = v
    if plane >= n - radius:
        high_ref[plane - (n - radius)] = v


def all_columns(source, a_refs, out_ref):
    for p in range(out_ref.shape[0]):
        out_ref[p] = blur_columns(source(p), a_refs[0][p], a_refs[1][p])


def own_rows(w_ref, wx_ref, low_ref, high_ref):
    n, rows, _ = w_ref.shape
    radius, inner, _ = low_ref.shape
    for p in range(n):
        w_hi, w_lo = split(w_ref[p])
        v = blur_rows(wx_ref[p, 0, :inner, :rows], wx_ref[p, 1, :inner, :rows], w_hi, w_lo)
        store_sends(v, p, n, radius, low_ref, high_ref)


def row_place():
    row = lax.axis_index("row")
    return row == 0, row == lax.axis_size("row") - 1


def first_kernel(
    n, radius, band_hbm, tx_hbm, ty_hbm, est_hbm,
    ah_ref, al_ref, wx_ref, w_ref,
    band_ref, tx_ref, ty_ref, est_ref, sems,
):
    pairs = ((band_hbm, band_ref), (tx_hbm, tx_ref), (ty_hbm, ty_ref), (est_hbm, est_ref))
    copies = [pltpu.make_async_copy(a, b, sems.at[k]) for k, (a, b) in enumerate(pairs)]
    for copy in copies:
        copy.start()
    rows, width = wx_ref.shape[2], wx_ref.shape[3]
    _, lane = iotas(16, 128)
    _, wide = iotas(16, width)
    row, lanes = iotas(rows, width)
    keep = jnp.logical_not(row_place()[1]) | ((row < rows - radius) == (lanes < rows))
    for copy in copies:
        copy.wait()
    for p in range(n):
        band = band_ref[p]
        column_matrix(spread(ty_ref, band, lane, radius, True), radius, ah_ref, al_ref, p)
        matrix = row_matrix(spread(tx_ref, band, wide, radius, False), rows, 0, width)
        wx_ref[p, 0], wx_ref[p, 1] = split(jnp.where(keep, matrix, 0.0))
    all_columns(lambda p: est_ref[p], (ah_ref, al_ref), w_ref)


def first_blur(band_index, taps_x, taps_y, est, width):
    n, rows, columns = est.shape
    radius = taps_x.shape[1] // 2
    a = shape_of(n, columns, columns, dtype=BF16)
    w = shape_of(n, 2, rows, width, dtype=BF16)
    return pl.pallas_call(
        functools.partial(first_kernel, n, radius),
        in_specs=[pl.BlockSpec(memory_space=pltpu.HBM)] * 4,
        scratch_shapes=[
            pltpu.SMEM(band_index.shape, jnp.int32),
            pltpu.SMEM(taps_x.shape, F32),
            pltpu.SMEM(taps_y.shape, F32),
            pltpu.VMEM(est.shape, F32),
            pltpu.SemaphoreType.DMA((4,)),
        ],
        out_specs=[VMEM] * 4,
        out_shape=[a, a, w, shape_of(*est.shape)],
        compiler_params=PARAMS,
        cost_estimate=cost(1.0),
    )(band_index, taps_x, taps_y, est)


def second_kernel(
    n, radius, halo, band_ref, tx_ref, ty_ref, tz_ref, after_ref,
    obs_ref, next_ref, ah_ref, al_ref, wx_ref, rn_ref, shifted_ref,
):
    rows, width = wx_ref.shape[2], wx_ref.shape[3]
    first_row, last_row = row_place()
    below = lax.axis_index("slab") * n
    depth = lax.axis_size("slab") * n
    _, lane = iotas(16, 128)
    _, wide = iotas(16, width)
    _, lanes = iotas(rows, width)
    lower = jnp.logical_not(first_row) | (lanes >= halo - radius)
    upper = jnp.logical_not(last_row) | (lanes < rows - radius + halo)
    keep = ((lanes < halo) & lower) | ((lanes >= halo) & upper)
    for p in range(n):
        band = band_ref[p]
        sums = column_matrix(
            spread(ty_ref, band, lane, radius, False), radius, ah_ref, al_ref, p
        )
        matrix = row_matrix(
            spread(tx_ref, band, wide, radius, True), rows, halo - 2 * radius, width
        )
        matrix = jnp.where(keep, matrix, 0.0)
        wx_ref[p, 0], wx_ref[p, 1] = split(matrix)
        along_x = jnp.sum(matrix, axis=1, keepdims=True)
        along_z = jnp.float32(0.0)
        z = below + p
        for k in range(2 * radius + 1):
            source = z - k + radius
            inside = (source >= 0) & (source < depth)
            along_z = along_z + jnp.where(inside, tz_ref[k], 0.0)
        for block, along_y in enumerate(sums):
            rn_ref[p, :, block * 128 : block * 128 + 128] = 1.0 / (
                along_x * (along_y * along_z)
            )
        shifted_ref[p, : rows - radius] = obs_ref[p, radius:]
        shifted_ref[p, rows - radius :] = next_ref[p, :radius]


def second_weights(band_index, taps_x, taps_y, taps_z, after, obs, beyond, width):
    n, rows, columns = obs.shape
    halo = beyond.shape[1]
    radius = taps_x.shape[1] // 2
    a = shape_of(n, columns, columns, dtype=BF16)
    w = shape_of(n, 2, rows, width, dtype=BF16)
    field = shape_of(*obs.shape)
    return pl.pallas_call(
        functools.partial(second_kernel, n, radius, halo),
        in_specs=[SMEM] * 4 + [ANY] + [VMEM] * 2,
        out_specs=[VMEM] * 5,
        out_shape=[a, a, w, field, field],
        compiler_params=PARAMS,
        cost_estimate=cost(1.0),
    )(band_index, taps_x, taps_y, taps_z, after, obs, beyond)


def inner_kernel(w_ref, wx_ref, after_ref, low_ref, high_ref):
    own_rows(w_ref, wx_ref, low_ref, high_ref)


def inner_blur(w, wx, halo, radius, after):
    _, rows, columns = w.shape
    send = shape_of(radius, rows - halo, columns)
    return pl.pallas_call(
        inner_kernel,
        in_specs=[VMEM] * 2 + [ANY],
        out_specs=[VMEM] * 2,
        out_shape=[send] * 2,
        compiler_params=PARAMS,
        cost_estimate=cost(1.0),
    )(w, wx, after)


def edge_kernel(n, radius, blurred, w_ref, next_ref, wx_ref, *refs):
    rows, halo = w_ref.shape[1], next_ref.shape[1]
    inner, used = rows - halo, rows + halo
    beyond_ref = next_ref
    if not blurred:
        beyond_ref, refs = refs[-1], refs[:-1]
        all_columns(lambda p: next_ref[p], refs[:2], beyond_ref)
    for p in range(n):
        w_hi, w_lo = split(jnp.concatenate([w_ref[p], beyond_ref[p]], axis=0))
        v = blur_rows(wx_ref[p, 0, inner:, :used], wx_ref[p, 1, inner:, :used], w_hi, w_lo)
        store_sends(v, p, n, radius, *refs[-2:])


def edge_blur(w, beyond, wx, columns_matrix, radius):
    n, _, columns = w.shape
    halo = beyond.shape[1]
    send = shape_of(radius, halo, columns)
    args = (w, beyond, wx, *columns_matrix)
    return pl.pallas_call(
        functools.partial(edge_kernel, n, radius, not columns_matrix),
        in_specs=[VMEM] * len(args),
        out_specs=[VMEM] * 2,
        out_shape=[send] * 2,
        scratch_shapes=[pltpu.VMEM(beyond.shape, F32)] if columns_matrix else [],
        compiler_params=PARAMS,
        cost_estimate=cost(1.0),
    )(*args)


def depth_sum(n, radius, flip, tz_ref, refs, rows, lanes):
    low_ref, high_ref, zlo_ref, zhi_ref = refs
    last = 2 * radius
    taps = [tz_ref[last - k if flip else k] for k in range(last + 1)]
    total = [None] * n
    for j in range(-radius, n + radius):
        if j < 0:
            piece = zlo_ref[j + radius, rows, lanes]
        elif j < radius:
            piece = low_ref[j, rows, lanes]
        elif j < n:
            piece = high_ref[j - (n - radius), rows, lanes]
        else:
            piece = zhi_ref[j - n, rows, lanes]
        for i in range(max(0, j - radius), min(n, j + radius + 1)):
            term = taps[j - i + radius] * piece
            total[i] = term if total[i] is None else total[i] + term
    return total


def tiles(count, columns, body):
    def step(t, carry):
        for left in range(0, columns, 128):
            body(t * 8, slice(left, left + 128))
        return carry

    lax.fori_loop(0, count // 8, step, 0)


def at(start, offset):
    return pl.ds(pl.multiple_of(start + offset, 8), 8)


def ratio_kernel(n, radius, skip, tz_ref, obs_ref, *refs):
    rlow_ref, rhigh_ref = refs[-2:]
    _, count, columns = rlow_ref.shape

    def body(start, lanes):
        rows = at(start, 0)
        total = depth_sum(n, radius, False, tz_ref, refs[:4], rows, lanes)
        for i in range(n):
            ratio = obs_ref[i, at(start, skip), lanes] / total[i]
            if i < radius:
                rlow_ref[i, rows, lanes] = ratio
            if i >= n - radius:
                rhigh_ref[i - (n - radius), rows, lanes] = ratio

    tiles(count, columns, body)


def depth_ratio(taps_z, obs, chunk, skip, count, after, micro=1.0):
    n, _, columns = obs.shape
    radius = taps_z.shape[0] // 2
    send = shape_of(radius, count, columns)
    return pl.pallas_call(
        functools.partial(ratio_kernel, n, radius, skip),
        in_specs=[SMEM] + [VMEM] * 5 + [ANY],
        out_specs=[VMEM] * 2,
        out_shape=[send] * 2,
        compiler_params=PARAMS,
        cost_estimate=cost(micro),
    )(taps_z, obs, *chunk, after)


def back_kernel(n, radius, tz_ref, *refs):
    out_ref = refs[-1]
    _, count, columns = out_ref.shape

    def body(start, lanes):
        rows = at(start, 0)
        total = depth_sum(n, radius, True, tz_ref, refs[:4], rows, lanes)
        for i in range(n):
            out_ref[i, rows, lanes] = total[i]

    tiles(count, columns, body)


def depth_back(taps_z, chunk, n, after, micro=1.0):
    radius, count, columns = chunk[0].shape
    return pl.pallas_call(
        functools.partial(back_kernel, n, radius),
        in_specs=[SMEM] + [VMEM] * 4 + [ANY],
        out_specs=VMEM,
        out_shape=shape_of(n, count, columns),
        compiler_params=PARAMS,
        cost_estimate=cost(micro),
    )(taps_z, *chunk, after)


def update_kernel(n, last, *refs):
    pieces, edge_ref, refs = refs[:3], refs[2], refs[3:]
    est_ref, rn_ref, wa_ref, bh_ref, bl_ref = refs[:5]
    refs = refs[5:]
    rows = est_ref.shape[1]
    halo = edge_ref.shape[1]
    used = rows + halo
    u_ref, refs = refs[-1], refs[:-1]
    if last:
        (out_ref,) = refs
    else:
        wx_ref, ah_ref, al_ref, out_ref, w_ref, top_ref, low_ref, high_ref = refs
    for p in range(n):
        c_hi, c_lo = split(jnp.concatenate([piece[p] for piece in pieces], axis=0))
        u_ref[p] = blur_rows(wa_ref[p, 0, :, :used], wa_ref[p, 1, :, :used], c_hi, c_lo)
    for p in range(n):
        u = blur_columns(u_ref[p], bh_ref[p], bl_ref[p])
        out_ref[p] = est_ref[p] * u * rn_ref[p]
    if not last:
        all_columns(lambda p: out_ref[p], (ah_ref, al_ref), w_ref)
        for p in range(n):
            top_ref[p] = w_ref[p, :halo]
        own_rows(w_ref, wx_ref, low_ref, high_ref)


def update(pieces, est, rn, adjoint, forward, radius):
    n, rows, columns = est.shape
    halo = pieces[0].shape[1]
    last = forward is None
    args = [*pieces, est, rn, *adjoint] + ([] if last else [*forward])
    out_shape = [shape_of(*est.shape)]
    if not last:
        send = shape_of(radius, rows - halo, columns)
        out_shape += [shape_of(*est.shape), shape_of(n, halo, columns), send, send]
    return pl.pallas_call(
        functools.partial(update_kernel, n, last),
        in_specs=[VMEM] * len(args),
        out_specs=[VMEM] * len(out_shape),
        out_shape=out_shape,
        scratch_shapes=[pltpu.VMEM(est.shape, F32)],
        compiler_params=PARAMS,
        cost_estimate=cost(1.0),
    )(*args)


def depth_exchange(low, high):
    count = lax.axis_size("slab")
    forward = [(i, i + 1) for i in range(count - 1)]
    backward = [(i + 1, i) for i in range(count - 1)]
    zlo = lax.ppermute(high, "slab", forward)
    zhi = lax.ppermute(low, "slab", backward)
    return low, high, zlo, zhi


def ring(x, step):
    count = lax.axis_size("row")
    return lax.ppermute(x, "row", [(i, (i + step) % count) for i in range(count)])


def on_device(observed, band_index, taps_x, taps_y, taps_z):
    n, rows, columns = observed.shape
    radius = taps_z.shape[0] // 2
    halo = up(2 * radius, 16)
    inner = rows - halo
    width = up(rows + halo, 128)
    beyond = ring(observed[:, :halo], -1)
    ah, al, wx, w = first_blur(band_index, taps_x, taps_y, observed, width)
    est, adjoint = observed, None
    for step in range(ITERS):
        if step:
            v_inner = depth_exchange(*inner_sends)
            edge_sends = edge_blur(w, beyond, wx, (), radius)
            v_edge = depth_exchange(*edge_sends)
            after = edge_sends[0]
        else:
            edge_sends = edge_blur(w, beyond, wx, (ah, al), radius)
            v_edge = depth_exchange(*edge_sends)
            inner_sends = inner_blur(w, wx, halo, radius, edge_sends[0])
            v_inner = depth_exchange(*inner_sends)
            bh, bl, wa, rn, shifted = second_weights(
                band_index, taps_x, taps_y, taps_z, inner_sends[0], observed, beyond, width
            )
            adjoint = (wa, bh, bl)
            after = inner_sends[0]
        r_edge = depth_exchange(
            *depth_ratio(taps_z, shifted, v_edge, inner, halo, after)
        )
        r_inner = depth_exchange(
            *depth_ratio(taps_z, shifted, v_inner, 0, inner, r_edge[0])
        )
        c_edge = depth_back(taps_z, r_edge, n, r_inner[0])
        before = ring(c_edge, 1)
        c_inner = depth_back(taps_z, r_inner, n, c_edge, 100.0)
        last = step == ITERS - 1
        out = update(
            (before, c_inner, c_edge), est, rn, adjoint,
            None if last else (wx, ah, al), radius,
        )
        est = out[0]
        if not last:
            w, top, *inner_sends = out[1:]
            beyond = ring(top, -1)
    return est


def solution(mesh):
    in_specs = (P(("grp", "slab"), "row", None), P("slab"), P(), P(), P())
    out_specs = P(("grp", "slab"), "row", None)
    return jax.shard_map(
        on_device, mesh=mesh, in_specs=in_specs, out_specs=out_specs, check_vma=False
    )
```

```python
import functools

import jax
import jax.numpy as jnp
from jax import lax
from jax.experimental import pallas as pl
from jax.experimental.pallas import tpu as pltpu
from jax.sharding import PartitionSpec as P

ITERS = 2
F32 = jnp.float32
BF16 = jnp.bfloat16
PARAMS = pltpu.CompilerParams(vmem_limit_bytes=16 * 1024 * 1024)
SMEM = pl.BlockSpec(memory_space=pltpu.SMEM)
VMEM = pl.BlockSpec(memory_space=pltpu.VMEM)
ANY = pl.BlockSpec(memory_space=pl.ANY)


def up(value, step):
    return -(-value // step) * step


def split(x):
    hi = x.astype(BF16)
    return hi, (x - hi.astype(F32)).astype(BF16)


def mm(a, b):
    return jnp.dot(a, b, preferred_element_type=F32)


def blur_rows(w_hi, w_lo, v_hi, v_lo):
    count = w_hi.shape[0]
    both = mm(jnp.concatenate([w_hi, w_lo], axis=0), v_hi)
    return both[:count] + both[count:] + mm(w_hi, v_lo)


def blur_columns(u, a_hi, a_lo):
    count = u.shape[0]
    u_hi, u_lo = split(u)
    both = mm(jnp.concatenate([u_hi, u_lo], axis=0), a_hi)
    return both[:count] + both[count:] + mm(u_hi, a_lo)


def cost(microseconds):
    return pl.CostEstimate(
        flops=int(microseconds * 1e9), bytes_accessed=int(microseconds * 3.5e6), transcendentals=0
    )


def shape_of(*dims, dtype=F32):
    return jax.ShapeDtypeStruct(dims, dtype)


def spread(ref, band, lanes, radius, flip):
    base = jnp.zeros(lanes.shape, F32)
    for k in range(2 * radius + 1):
        base = jnp.where(lanes == (2 * radius - k if flip else k), ref[band, k], base)
    return base


def iotas(rows, lanes):
    shape = (rows, lanes)
    return (
        lax.broadcasted_iota(jnp.int32, shape, 0),
        lax.broadcasted_iota(jnp.int32, shape, 1),
    )


def column_matrix(base, radius, h_ref, l_ref, p):
    columns = h_ref.shape[1]
    sub, lane = iotas(16, 128)
    rolled = {}
    sums = [None] * (columns // 128)
    for first in range(0, columns, 16):
        key = first % 128
        if key not in rolled:
            rolled[key] = pltpu.roll(base, (key - radius) % 128, 1, stride=1, stride_axis=0)
        for block in range(columns // 128):
            left = block * 128
            here = (p, slice(first, first + 16), slice(left, left + 128))
            if left > first + 15 + radius or left + 127 < first - radius:
                zero = jnp.zeros((16, 128), BF16)
                h_ref[here] = zero
                l_ref[here] = zero
                continue
            inside = jnp.abs(lane - sub + (left - first)) <= radius
            tile = jnp.where(inside, rolled[key], 0.0)
            h_ref[here], l_ref[here] = split(tile)
            sums[block] = tile if sums[block] is None else sums[block] + tile
    return [jnp.sum(s, axis=0, keepdims=True) for s in sums]


def row_matrix(base, rows, shift, width):
    return jnp.concatenate(
        [
            pltpu.roll(base, (first + shift) % width, 1, stride=1, stride_axis=0)
            for first in range(0, rows, 16)
        ],
        axis=0,
    )


def store_sends(v, plane, n, radius, low_ref, high_ref):
    if plane < radius:
        low_ref[plane] = v
    if plane >= n - radius:
        high_ref[plane - (n - radius)] = v


def all_columns(source, a_refs, out_ref):
    for p in range(out_ref.shape[0]):
        out_ref[p] = blur_columns(source(p), a_refs[0][p], a_refs[1][p])


def own_rows(w_ref, wx_ref, low_ref, high_ref, first=0):
    n, rows, _ = w_ref.shape
    radius, count, _ = low_ref.shape
    part = slice(first, first + count)
    for p in range(n):
        w_hi, w_lo = split(w_ref[p])
        v = blur_rows(wx_ref[p, 0, part, :rows], wx_ref[p, 1, part, :rows], w_hi, w_lo)
        store_sends(v, p, n, radius, low_ref, high_ref)


def row_place():
    row = lax.axis_index("row")
    return row == 0, row == lax.axis_size("row") - 1


def first_kernel(
    n, radius, band_hbm, tx_hbm, ty_hbm, est_hbm,
    ah_ref, al_ref, wx_ref, w_ref,
    band_ref, tx_ref, ty_ref, est_ref, sems,
):
    pairs = ((band_hbm, band_ref), (tx_hbm, tx_ref), (ty_hbm, ty_ref), (est_hbm, est_ref))
    copies = [pltpu.make_async_copy(a, b, sems.at[k]) for k, (a, b) in enumerate(pairs)]
    for copy in copies:
        copy.start()
    rows, width = wx_ref.shape[2], wx_ref.shape[3]
    _, lane = iotas(16, 128)
    _, wide = iotas(16, width)
    row, lanes = iotas(rows, width)
    keep = jnp.logical_not(row_place()[1]) | ((row < rows - radius) == (lanes < rows))
    for copy in copies:
        copy.wait()
    for p in range(n):
        band = band_ref[p]
        column_matrix(spread(ty_ref, band, lane, radius, True), radius, ah_ref, al_ref, p)
        matrix = row_matrix(spread(tx_ref, band, wide, radius, False), rows, 0, width)
        wx_ref[p, 0], wx_ref[p, 1] = split(jnp.where(keep, matrix, 0.0))
    all_columns(lambda p: est_ref[p], (ah_ref, al_ref), w_ref)


def first_blur(band_index, taps_x, taps_y, est, width):
    n, rows, columns = est.shape
    radius = taps_x.shape[1] // 2
    a = shape_of(n, columns, columns, dtype=BF16)
    w = shape_of(n, 2, rows, width, dtype=BF16)
    return pl.pallas_call(
        functools.partial(first_kernel, n, radius),
        in_specs=[pl.BlockSpec(memory_space=pltpu.HBM)] * 4,
        scratch_shapes=[
            pltpu.SMEM(band_index.shape, jnp.int32),
            pltpu.SMEM(taps_x.shape, F32),
            pltpu.SMEM(taps_y.shape, F32),
            pltpu.VMEM(est.shape, F32),
            pltpu.SemaphoreType.DMA((4,)),
        ],
        out_specs=[VMEM] * 4,
        out_shape=[a, a, w, shape_of(*est.shape)],
        compiler_params=PARAMS,
        cost_estimate=cost(1.0),
    )(band_index, taps_x, taps_y, est)


def second_kernel(
    n, radius, halo, band_ref, tx_ref, ty_ref, tz_ref, after_ref,
    obs_ref, next_ref, ah_ref, al_ref, wx_ref, rn_ref, shifted_ref,
):
    rows, width = wx_ref.shape[2], wx_ref.shape[3]
    first_row, last_row = row_place()
    below = lax.axis_index("slab") * n
    depth = lax.axis_size("slab") * n
    _, lane = iotas(16, 128)
    _, wide = iotas(16, width)
    _, lanes = iotas(rows, width)
    lower = jnp.logical_not(first_row) | (lanes >= halo - radius)
    upper = jnp.logical_not(last_row) | (lanes < rows - radius + halo)
    keep = ((lanes < halo) & lower) | ((lanes >= halo) & upper)
    for p in range(n):
        band = band_ref[p]
        sums = column_matrix(
            spread(ty_ref, band, lane, radius, False), radius, ah_ref, al_ref, p
        )
        matrix = row_matrix(
            spread(tx_ref, band, wide, radius, True), rows, halo - 2 * radius, width
        )
        matrix = jnp.where(keep, matrix, 0.0)
        wx_ref[p, 0], wx_ref[p, 1] = split(matrix)
        along_x = jnp.sum(matrix, axis=1, keepdims=True)
        along_z = jnp.float32(0.0)
        z = below + p
        for k in range(2 * radius + 1):
            source = z - k + radius
            inside = (source >= 0) & (source < depth)
            along_z = along_z + jnp.where(inside, tz_ref[k], 0.0)
        for block, along_y in enumerate(sums):
            rn_ref[p, :, block * 128 : block * 128 + 128] = 1.0 / (
                along_x * (along_y * along_z)
            )
        shifted_ref[p, : rows - radius] = obs_ref[p, radius:]
        shifted_ref[p, rows - radius :] = next_ref[p, :radius]


def second_weights(band_index, taps_x, taps_y, taps_z, after, obs, beyond, width):
    n, rows, columns = obs.shape
    halo = beyond.shape[1]
    radius = taps_x.shape[1] // 2
    a = shape_of(n, columns, columns, dtype=BF16)
    w = shape_of(n, 2, rows, width, dtype=BF16)
    field = shape_of(*obs.shape)
    return pl.pallas_call(
        functools.partial(second_kernel, n, radius, halo),
        in_specs=[SMEM] * 4 + [ANY] + [VMEM] * 2,
        out_specs=[VMEM] * 5,
        out_shape=[a, a, w, field, field],
        compiler_params=PARAMS,
        cost_estimate=cost(1.0),
    )(band_index, taps_x, taps_y, taps_z, after, obs, beyond)


def inner_kernel(first, w_ref, wx_ref, *refs):
    own_rows(w_ref, wx_ref, *refs[-2:], first)


def inner_blur(w, wx, first, count, radius, after, micro):
    send = shape_of(radius, count, w.shape[2])
    return pl.pallas_call(
        functools.partial(inner_kernel, first),
        in_specs=[VMEM] * 2 + [ANY] * len(after),
        out_specs=[VMEM] * 2,
        out_shape=[send] * 2,
        compiler_params=PARAMS,
        cost_estimate=cost(micro),
    )(w, wx, *after)


def edge_kernel(n, radius, blurred, w_ref, next_ref, wx_ref, *refs):
    rows, halo = w_ref.shape[1], next_ref.shape[1]
    inner, used = rows - halo, rows + halo
    beyond_ref = next_ref
    if not blurred:
        beyond_ref, refs = refs[-1], refs[:-1]
        all_columns(lambda p: next_ref[p], refs[:2], beyond_ref)
    for p in range(n):
        w_hi, w_lo = split(jnp.concatenate([w_ref[p], beyond_ref[p]], axis=0))
        v = blur_rows(wx_ref[p, 0, inner:, :used], wx_ref[p, 1, inner:, :used], w_hi, w_lo)
        store_sends(v, p, n, radius, *refs[-2:])


def edge_blur(w, beyond, wx, columns_matrix, radius):
    n, _, columns = w.shape
    halo = beyond.shape[1]
    send = shape_of(radius, halo, columns)
    args = (w, beyond, wx, *columns_matrix)
    return pl.pallas_call(
        functools.partial(edge_kernel, n, radius, not columns_matrix),
        in_specs=[VMEM] * len(args),
        out_specs=[VMEM] * 2,
        out_shape=[send] * 2,
        scratch_shapes=[pltpu.VMEM(beyond.shape, F32)] if columns_matrix else [],
        compiler_params=PARAMS,
        cost_estimate=cost(1.0),
    )(*args)


def depth_sum(n, radius, flip, tz_ref, refs, rows, lanes):
    low_ref, high_ref, zlo_ref, zhi_ref = refs
    last = 2 * radius
    taps = [tz_ref[last - k if flip else k] for k in range(last + 1)]
    total = [None] * n
    for j in range(-radius, n + radius):
        if j < 0:
            piece = zlo_ref[j + radius, rows, lanes]
        elif j < radius:
            piece = low_ref[j, rows, lanes]
        elif j < n:
            piece = high_ref[j - (n - radius), rows, lanes]
        else:
            piece = zhi_ref[j - n, rows, lanes]
        for i in range(max(0, j - radius), min(n, j + radius + 1)):
            term = taps[j - i + radius] * piece
            total[i] = term if total[i] is None else total[i] + term
    return total


def tiles(count, columns, body):
    def step(t, carry):
        for left in range(0, columns, 128):
            body(t * 8, slice(left, left + 128))
        return carry

    lax.fori_loop(0, count // 8, step, 0)


def at(start, offset):
    return pl.ds(pl.multiple_of(start + offset, 8), 8)


def ratio_kernel(n, radius, skip, tz_ref, obs_ref, *refs):
    rlow_ref, rhigh_ref = refs[-2:]
    columns = obs_ref.shape[2]

    def run(own, first):
        def body(start, lanes):
            total = depth_sum(n, radius, False, tz_ref, own, at(start, 0), lanes)
            rows = at(start, first)
            for i in range(n):
                ratio = obs_ref[i, at(start, skip + first), lanes] / total[i]
                if i < radius:
                    rlow_ref[i, rows, lanes] = ratio
                if i >= n - radius:
                    rhigh_ref[i - (n - radius), rows, lanes] = ratio

        tiles(own[0].shape[1], columns, body)

    first = 0
    while first < rlow_ref.shape[1]:
        run(refs[:4], first)
        first += refs[0].shape[1]
        refs = refs[4:]


def depth_ratio(taps_z, obs, chunks, skip, after):
    n, _, columns = obs.shape
    radius = taps_z.shape[0] // 2
    send = shape_of(radius, sum(chunk[0].shape[1] for chunk in chunks), columns)
    return pl.pallas_call(
        functools.partial(ratio_kernel, n, radius, skip),
        in_specs=[SMEM] + [VMEM] * (1 + 4 * len(chunks)) + [ANY] * len(after),
        out_specs=[VMEM] * 2,
        out_shape=[send] * 2,
        compiler_params=PARAMS,
        cost_estimate=cost(1.0),
    )(taps_z, obs, *(x for chunk in chunks for x in chunk), *after)


def back_kernel(n, radius, tz_ref, *refs):
    out_ref = refs[-1]
    _, count, columns = out_ref.shape

    def body(start, lanes):
        rows = at(start, 0)
        total = depth_sum(n, radius, True, tz_ref, refs[:4], rows, lanes)
        for i in range(n):
            out_ref[i, rows, lanes] = total[i]

    tiles(count, columns, body)


def depth_back(taps_z, chunk, n, after, micro=1.0):
    radius, count, columns = chunk[0].shape
    return pl.pallas_call(
        functools.partial(back_kernel, n, radius),
        in_specs=[SMEM] + [VMEM] * 4 + [ANY],
        out_specs=VMEM,
        out_shape=shape_of(n, count, columns),
        compiler_params=PARAMS,
        cost_estimate=cost(micro),
    )(taps_z, *chunk, after)


def update_kernel(n, last, *refs):
    pieces, edge_ref, refs = refs[:3], refs[2], refs[3:]
    est_ref, rn_ref, wa_ref, bh_ref, bl_ref = refs[:5]
    refs = refs[5:]
    rows = est_ref.shape[1]
    halo = edge_ref.shape[1]
    used = rows + halo
    u_ref, refs = refs[-1], refs[:-1]
    if last:
        (out_ref,) = refs
    else:
        wx_ref, ah_ref, al_ref, out_ref, w_ref, top_ref, low_ref, high_ref = refs
    for p in range(n):
        c_hi, c_lo = split(jnp.concatenate([piece[p] for piece in pieces], axis=0))
        u_ref[p] = blur_rows(wa_ref[p, 0, :, :used], wa_ref[p, 1, :, :used], c_hi, c_lo)
    for p in range(n):
        u = blur_columns(u_ref[p], bh_ref[p], bl_ref[p])
        out_ref[p] = est_ref[p] * u * rn_ref[p]
    if not last:
        all_columns(lambda p: out_ref[p], (ah_ref, al_ref), w_ref)
        for p in range(n):
            top_ref[p] = w_ref[p, :halo]
        own_rows(w_ref, wx_ref, low_ref, high_ref)


def update(pieces, est, rn, adjoint, forward, count, radius):
    n, rows, columns = est.shape
    halo = pieces[0].shape[1]
    last = forward is None
    args = [*pieces, est, rn, *adjoint] + ([] if last else [*forward])
    out_shape = [shape_of(*est.shape)]
    if not last:
        send = shape_of(radius, count, columns)
        out_shape += [shape_of(*est.shape), shape_of(n, halo, columns), send, send]
    return pl.pallas_call(
        functools.partial(update_kernel, n, last),
        in_specs=[VMEM] * len(args),
        out_specs=[VMEM] * len(out_shape),
        out_shape=out_shape,
        scratch_shapes=[pltpu.VMEM(est.shape, F32)],
        compiler_params=PARAMS,
        cost_estimate=cost(1.0),
    )(*args)


def depth_exchange(low, high):
    count = lax.axis_size("slab")
    forward = [(i, i + 1) for i in range(count - 1)]
    backward = [(i + 1, i) for i in range(count - 1)]
    zlo = lax.ppermute(high, "slab", forward)
    zhi = lax.ppermute(low, "slab", backward)
    return low, high, zlo, zhi


def ring(x, step):
    count = lax.axis_size("row")
    return lax.ppermute(x, "row", [(i, (i + step) % count) for i in range(count)])


def on_device(observed, band_index, taps_x, taps_y, taps_z):
    n, rows, columns = observed.shape
    radius = taps_z.shape[0] // 2
    halo = up(2 * radius, 16)
    inner = rows - halo
    half = up(inner // 2, 16)
    width = up(rows + halo, 128)
    beyond = ring(observed[:, :halo], -1)
    ah, al, wx, w = first_blur(band_index, taps_x, taps_y, observed, width)
    est, adjoint = observed, None
    for step in range(ITERS):
        if step:
            v_first = depth_exchange(*first_sends)
            edge_sends = edge_blur(w, beyond, wx, (), radius)
            v_edge = depth_exchange(*edge_sends)
            after = (edge_sends[0],) + v_first[2:]
            inner_sends = inner_blur(w, wx, half, inner - half, radius, after, 20.0)
            v_inner = [v_first, depth_exchange(*inner_sends)]
        else:
            edge_sends = edge_blur(w, beyond, wx, (ah, al), radius)
            v_edge = depth_exchange(*edge_sends)
            inner_sends = inner_blur(w, wx, 0, inner, radius, (edge_sends[0],), 1.0)
            v_inner = [depth_exchange(*inner_sends)]
            bh, bl, wa, rn, shifted = second_weights(
                band_index, taps_x, taps_y, taps_z, inner_sends[0], observed, beyond, width
            )
            adjoint = (wa, bh, bl)
        r_edge = depth_exchange(
            *depth_ratio(taps_z, shifted, [v_edge], inner, (inner_sends[0],))
        )
        r_inner = depth_exchange(
            *depth_ratio(taps_z, shifted, v_inner, 0, (r_edge[0],))
        )
        c_edge = depth_back(taps_z, r_edge, n, r_inner[0])
        before = ring(c_edge, 1)
        c_inner = depth_back(taps_z, r_inner, n, c_edge, 100.0)
        last = step == ITERS - 1
        out = update(
            (before, c_inner, c_edge), est, rn, adjoint,
            None if last else (wx, ah, al), half, radius,
        )
        est = out[0]
        if not last:
            w, top, *first_sends = out[1:]
            beyond = ring(top, -1)
    return est


def solution(mesh):
    in_specs = (P(("grp", "slab"), "row", None), P("slab"), P(), P(), P())
    out_specs = P(("grp", "slab"), "row", None)
    return jax.shard_map(
        on_device, mesh=mesh, in_specs=in_specs, out_specs=out_specs, check_vma=False
    )
```

```python
import functools

import jax
import jax.numpy as jnp
from jax import lax
from jax.experimental import pallas as pl
from jax.experimental.pallas import tpu as pltpu
from jax.sharding import PartitionSpec as P

ITERS = 2
F32 = jnp.float32
BF16 = jnp.bfloat16
PARAMS = pltpu.CompilerParams(vmem_limit_bytes=16 * 1024 * 1024)
SMEM = pl.BlockSpec(memory_space=pltpu.SMEM)
VMEM = pl.BlockSpec(memory_space=pltpu.VMEM)
ANY = pl.BlockSpec(memory_space=pl.ANY)


def up(value, step):
    return -(-value // step) * step


def split(x):
    hi = x.astype(BF16)
    return hi, (x - hi.astype(F32)).astype(BF16)


def mm(a, b):
    return jnp.dot(a, b, preferred_element_type=F32)


def blur_rows(w_hi, w_lo, v_hi, v_lo):
    count = w_hi.shape[0]
    both = mm(jnp.concatenate([w_hi, w_lo], axis=0), v_hi)
    return both[:count] + both[count:] + mm(w_hi, v_lo)


def blur_columns(u, a_hi, a_lo):
    count = u.shape[0]
    u_hi, u_lo = split(u)
    both = mm(jnp.concatenate([u_hi, u_lo], axis=0), a_hi)
    return both[:count] + both[count:] + mm(u_hi, a_lo)


def cost(microseconds):
    return pl.CostEstimate(
        flops=int(microseconds * 1e9), bytes_accessed=int(microseconds * 3.5e6), transcendentals=0
    )


def shape_of(*dims, dtype=F32):
    return jax.ShapeDtypeStruct(dims, dtype)


def spread(ref, band, lanes, radius, flip):
    base = jnp.zeros(lanes.shape, F32)
    for k in range(2 * radius + 1):
        base = jnp.where(lanes == (2 * radius - k if flip else k), ref[band, k], base)
    return base


def iotas(rows, lanes):
    shape = (rows, lanes)
    return (
        lax.broadcasted_iota(jnp.int32, shape, 0),
        lax.broadcasted_iota(jnp.int32, shape, 1),
    )


def column_matrix(base, radius, h_ref, l_ref, p):
    columns = h_ref.shape[1]
    sub, lane = iotas(16, 128)
    rolled = {}
    sums = [None] * (columns // 128)
    for first in range(0, columns, 16):
        key = first % 128
        if key not in rolled:
            rolled[key] = pltpu.roll(base, (key - radius) % 128, 1, stride=1, stride_axis=0)
        for block in range(columns // 128):
            left = block * 128
            here = (p, slice(first, first + 16), slice(left, left + 128))
            if left > first + 15 + radius or left + 127 < first - radius:
                zero = jnp.zeros((16, 128), BF16)
                h_ref[here] = zero
                l_ref[here] = zero
                continue
            inside = jnp.abs(lane - sub + (left - first)) <= radius
            tile = jnp.where(inside, rolled[key], 0.0)
            h_ref[here], l_ref[here] = split(tile)
            sums[block] = tile if sums[block] is None else sums[block] + tile
    return [jnp.sum(s, axis=0, keepdims=True) for s in sums]


def row_matrix(base, rows, shift, width):
    return jnp.concatenate(
        [
            pltpu.roll(base, (first + shift) % width, 1, stride=1, stride_axis=0)
            for first in range(0, rows, 16)
        ],
        axis=0,
    )


def store_sends(v, plane, n, radius, low_ref, high_ref):
    if plane < radius:
        low_ref[plane] = v
    if plane >= n - radius:
        high_ref[plane - (n - radius)] = v


def all_columns(source, a_refs, out_ref):
    for p in range(out_ref.shape[0]):
        out_ref[p] = blur_columns(source(p), a_refs[0][p], a_refs[1][p])


def own_rows(w_ref, wx_ref, low_ref, high_ref, first=0):
    n, rows, _ = w_ref.shape
    radius, count, _ = low_ref.shape
    part = slice(first, first + count)
    for p in range(n):
        w_hi, w_lo = split(w_ref[p])
        v = blur_rows(wx_ref[p, 0, part, :rows], wx_ref[p, 1, part, :rows], w_hi, w_lo)
        store_sends(v, p, n, radius, low_ref, high_ref)


def row_place():
    row = lax.axis_index("row")
    return row == 0, row == lax.axis_size("row") - 1


def first_kernel(
    n, radius, band_hbm, tx_hbm, ty_hbm, est_hbm,
    ah_ref, al_ref, wx_ref, w_ref,
    band_ref, tx_ref, ty_ref, est_ref, sems,
):
    pairs = ((band_hbm, band_ref), (tx_hbm, tx_ref), (ty_hbm, ty_ref), (est_hbm, est_ref))
    copies = [pltpu.make_async_copy(a, b, sems.at[k]) for k, (a, b) in enumerate(pairs)]
    for copy in copies:
        copy.start()
    rows, width = wx_ref.shape[2], wx_ref.shape[3]
    _, lane = iotas(16, 128)
    _, wide = iotas(16, width)
    row, lanes = iotas(rows, width)
    keep = jnp.logical_not(row_place()[1]) | ((row < rows - radius) == (lanes < rows))
    for copy in copies:
        copy.wait()
    for p in range(n):
        band = band_ref[p]
        column_matrix(spread(ty_ref, band, lane, radius, True), radius, ah_ref, al_ref, p)
        matrix = row_matrix(spread(tx_ref, band, wide, radius, False), rows, 0, width)
        wx_ref[p, 0], wx_ref[p, 1] = split(jnp.where(keep, matrix, 0.0))
    all_columns(lambda p: est_ref[p], (ah_ref, al_ref), w_ref)


def first_blur(band_index, taps_x, taps_y, est, width):
    n, rows, columns = est.shape
    radius = taps_x.shape[1] // 2
    a = shape_of(n, columns, columns, dtype=BF16)
    w = shape_of(n, 2, rows, width, dtype=BF16)
    return pl.pallas_call(
        functools.partial(first_kernel, n, radius),
        in_specs=[pl.BlockSpec(memory_space=pltpu.HBM)] * 4,
        scratch_shapes=[
            pltpu.SMEM(band_index.shape, jnp.int32),
            pltpu.SMEM(taps_x.shape, F32),
            pltpu.SMEM(taps_y.shape, F32),
            pltpu.VMEM(est.shape, F32),
            pltpu.SemaphoreType.DMA((4,)),
        ],
        out_specs=[VMEM] * 4,
        out_shape=[a, a, w, shape_of(*est.shape)],
        compiler_params=PARAMS,
        cost_estimate=cost(1.0),
    )(band_index, taps_x, taps_y, est)


def second_kernel(
    n, radius, halo, band_ref, tx_ref, ty_ref, tz_ref, after_ref,
    obs_ref, next_ref, ah_ref, al_ref, wx_ref, rn_ref, shifted_ref, taps_ref,
):
    rows, width = wx_ref.shape[2], wx_ref.shape[3]
    first_row, last_row = row_place()
    below = lax.axis_index("slab") * n
    depth = lax.axis_size("slab") * n
    _, lane = iotas(16, 128)
    _, wide = iotas(16, width)
    _, lanes = iotas(rows, width)
    lower = jnp.logical_not(first_row) | (lanes >= halo - radius)
    upper = jnp.logical_not(last_row) | (lanes < rows - radius + halo)
    keep = ((lanes < halo) & lower) | ((lanes >= halo) & upper)
    for k in range(2 * radius + 1):
        taps_ref[k] = jnp.full(taps_ref.shape[1:], tz_ref[k], F32)
    for p in range(n):
        band = band_ref[p]
        sums = column_matrix(
            spread(ty_ref, band, lane, radius, False), radius, ah_ref, al_ref, p
        )
        matrix = row_matrix(
            spread(tx_ref, band, wide, radius, True), rows, halo - 2 * radius, width
        )
        matrix = jnp.where(keep, matrix, 0.0)
        wx_ref[p, 0], wx_ref[p, 1] = split(matrix)
        along_x = jnp.sum(matrix, axis=1, keepdims=True)
        along_z = jnp.float32(0.0)
        z = below + p
        for k in range(2 * radius + 1):
            source = z - k + radius
            inside = (source >= 0) & (source < depth)
            along_z = along_z + jnp.where(inside, tz_ref[k], 0.0)
        for block, along_y in enumerate(sums):
            rn_ref[p, :, block * 128 : block * 128 + 128] = 1.0 / (
                along_x * (along_y * along_z)
            )
        shifted_ref[p, : rows - radius] = obs_ref[p, radius:]
        shifted_ref[p, rows - radius :] = next_ref[p, :radius]


def second_weights(band_index, taps_x, taps_y, taps_z, after, obs, beyond, width):
    n, rows, columns = obs.shape
    halo = beyond.shape[1]
    radius = taps_x.shape[1] // 2
    a = shape_of(n, columns, columns, dtype=BF16)
    w = shape_of(n, 2, rows, width, dtype=BF16)
    field = shape_of(*obs.shape)
    return pl.pallas_call(
        functools.partial(second_kernel, n, radius, halo),
        in_specs=[SMEM] * 4 + [ANY] + [VMEM] * 2,
        out_specs=[VMEM] * 6,
        out_shape=[a, a, w, field, field, shape_of(2 * radius + 1, 8, 128)],
        compiler_params=PARAMS,
        cost_estimate=cost(1.0),
    )(band_index, taps_x, taps_y, taps_z, after, obs, beyond)


def inner_kernel(first, w_ref, wx_ref, *refs):
    own_rows(w_ref, wx_ref, *refs[-2:], first)


def inner_blur(w, wx, first, count, radius, after, micro):
    send = shape_of(radius, count, w.shape[2])
    return pl.pallas_call(
        functools.partial(inner_kernel, first),
        in_specs=[VMEM] * 2 + [ANY] * len(after),
        out_specs=[VMEM] * 2,
        out_shape=[send] * 2,
        compiler_params=PARAMS,
        cost_estimate=cost(micro),
    )(w, wx, *after)


def edge_kernel(n, radius, blurred, w_ref, next_ref, wx_ref, *refs):
    rows, halo = w_ref.shape[1], next_ref.shape[1]
    inner, used = rows - halo, rows + halo
    beyond_ref = next_ref
    if not blurred:
        beyond_ref, refs = refs[-1], refs[:-1]
        all_columns(lambda p: next_ref[p], refs[:2], beyond_ref)
    for p in range(n):
        w_hi, w_lo = split(jnp.concatenate([w_ref[p], beyond_ref[p]], axis=0))
        v = blur_rows(wx_ref[p, 0, inner:, :used], wx_ref[p, 1, inner:, :used], w_hi, w_lo)
        store_sends(v, p, n, radius, *refs[-2:])


def edge_blur(w, beyond, wx, columns_matrix, radius):
    n, _, columns = w.shape
    halo = beyond.shape[1]
    send = shape_of(radius, halo, columns)
    args = (w, beyond, wx, *columns_matrix)
    return pl.pallas_call(
        functools.partial(edge_kernel, n, radius, not columns_matrix),
        in_specs=[VMEM] * len(args),
        out_specs=[VMEM] * 2,
        out_shape=[send] * 2,
        scratch_shapes=[pltpu.VMEM(beyond.shape, F32)] if columns_matrix else [],
        compiler_params=PARAMS,
        cost_estimate=cost(1.0),
    )(*args)


def depth_sum(n, radius, flip, tz_ref, refs, rows, lanes):
    low_ref, high_ref, zlo_ref, zhi_ref = refs
    last = 2 * radius
    taps = [tz_ref[last - k if flip else k] for k in range(last + 1)]
    total = [None] * n
    for j in range(-radius, n + radius):
        if j < 0:
            piece = zlo_ref[j + radius, rows, lanes]
        elif j < radius:
            piece = low_ref[j, rows, lanes]
        elif j < n:
            piece = high_ref[j - (n - radius), rows, lanes]
        else:
            piece = zhi_ref[j - n, rows, lanes]
        for i in range(max(0, j - radius), min(n, j + radius + 1)):
            term = taps[j - i + radius] * piece
            total[i] = term if total[i] is None else total[i] + term
    return total


def tiles(count, columns, body):
    def step(t, carry):
        for left in range(0, columns, 128):
            body(t * 8, slice(left, left + 128))
        return carry

    lax.fori_loop(0, count // 8, step, 0)


def at(start, offset):
    return pl.ds(pl.multiple_of(start + offset, 8), 8)


def ratio_kernel(n, radius, skip, tz_ref, obs_ref, *refs):
    rlow_ref, rhigh_ref = refs[-2:]
    columns = obs_ref.shape[2]

    def run(own, first):
        def body(start, lanes):
            total = depth_sum(n, radius, False, tz_ref, own, at(start, 0), lanes)
            rows = at(start, first)
            for i in range(n):
                ratio = obs_ref[i, at(start, skip + first), lanes] / total[i]
                if i < radius:
                    rlow_ref[i, rows, lanes] = ratio
                if i >= n - radius:
                    rhigh_ref[i - (n - radius), rows, lanes] = ratio

        tiles(own[0].shape[1], columns, body)

    first = 0
    while first < rlow_ref.shape[1]:
        run(refs[:4], first)
        first += refs[0].shape[1]
        refs = refs[4:]


def depth_ratio(taps_z, obs, chunks, skip, after, micro):
    n, _, columns = obs.shape
    radius = chunks[0][0].shape[0]
    send = shape_of(radius, sum(chunk[0].shape[1] for chunk in chunks), columns)
    return pl.pallas_call(
        functools.partial(ratio_kernel, n, radius, skip),
        in_specs=[VMEM] * (2 + 4 * len(chunks)) + [ANY] * len(after),
        out_specs=[VMEM] * 2,
        out_shape=[send] * 2,
        compiler_params=PARAMS,
        cost_estimate=cost(micro),
    )(taps_z, obs, *(x for chunk in chunks for x in chunk), *after)


def back_kernel(n, radius, tz_ref, *refs):
    out_ref = refs[-1]
    _, count, columns = out_ref.shape

    def body(start, lanes):
        rows = at(start, 0)
        total = depth_sum(n, radius, True, tz_ref, refs[:4], rows, lanes)
        for i in range(n):
            out_ref[i, rows, lanes] = total[i]

    tiles(count, columns, body)


def depth_back(taps_z, chunk, n, after, micro=1.0):
    radius, count, columns = chunk[0].shape
    return pl.pallas_call(
        functools.partial(back_kernel, n, radius),
        in_specs=[VMEM] * 5 + [ANY],
        out_specs=VMEM,
        out_shape=shape_of(n, count, columns),
        compiler_params=PARAMS,
        cost_estimate=cost(micro),
    )(taps_z, *chunk, after)


def update_kernel(n, last, count, *refs):
    pieces, edge_ref, refs = refs[:count], refs[count - 1], refs[count:]
    est_ref, rn_ref, wa_ref, bh_ref, bl_ref = refs[:5]
    refs = refs[5:]
    rows = est_ref.shape[1]
    halo = edge_ref.shape[1]
    used = rows + halo
    u_ref, refs = refs[-1], refs[:-1]
    if last:
        (out_ref,) = refs
    else:
        wx_ref, ah_ref, al_ref, out_ref, w_ref, top_ref, low_ref, high_ref = refs
    for p in range(n):
        c_hi, c_lo = split(jnp.concatenate([piece[p] for piece in pieces], axis=0))
        u_ref[p] = blur_rows(wa_ref[p, 0, :, :used], wa_ref[p, 1, :, :used], c_hi, c_lo)
    for p in range(n):
        u = blur_columns(u_ref[p], bh_ref[p], bl_ref[p])
        out_ref[p] = est_ref[p] * u * rn_ref[p]
    if not last:
        all_columns(lambda p: out_ref[p], (ah_ref, al_ref), w_ref)
        for p in range(n):
            top_ref[p] = w_ref[p, :halo]
        own_rows(w_ref, wx_ref, low_ref, high_ref)


def update(pieces, est, rn, adjoint, forward, count, radius):
    n, rows, columns = est.shape
    halo = pieces[0].shape[1]
    last = forward is None
    args = [*pieces, est, rn, *adjoint] + ([] if last else [*forward])
    out_shape = [shape_of(*est.shape)]
    if not last:
        send = shape_of(radius, count, columns)
        out_shape += [shape_of(*est.shape), shape_of(n, halo, columns), send, send]
    return pl.pallas_call(
        functools.partial(update_kernel, n, last, len(pieces)),
        in_specs=[VMEM] * len(args),
        out_specs=[VMEM] * len(out_shape),
        out_shape=out_shape,
        scratch_shapes=[pltpu.VMEM(est.shape, F32)],
        compiler_params=PARAMS,
        cost_estimate=cost(1.0),
    )(*args)


def depth_exchange(low, high):
    count = lax.axis_size("slab")
    forward = [(i, i + 1) for i in range(count - 1)]
    backward = [(i + 1, i) for i in range(count - 1)]
    zlo = lax.ppermute(high, "slab", forward)
    zhi = lax.ppermute(low, "slab", backward)
    return low, high, zlo, zhi


def ring(x, step):
    count = lax.axis_size("row")
    return lax.ppermute(x, "row", [(i, (i + step) % count) for i in range(count)])


def on_device(observed, band_index, taps_x, taps_y, taps_z):
    n, rows, columns = observed.shape
    radius = taps_z.shape[0] // 2
    halo = up(2 * radius, 16)
    inner = rows - halo
    half = up(inner // 2, 16)
    width = up(rows + halo, 128)
    beyond = ring(observed[:, :halo], -1)
    ah, al, wx, w = first_blur(band_index, taps_x, taps_y, observed, width)
    est, adjoint = observed, None
    for step in range(ITERS):
        if step:
            v_first = depth_exchange(*first_sends)
            edge_sends = edge_blur(w, beyond, wx, (), radius)
            v_edge = depth_exchange(*edge_sends)
            r_sends = depth_ratio(taps, shifted, [v_first], 0, (edge_sends[0],), 1.0)
            r_inner = [depth_exchange(*r_sends)]
            after = (r_sends[0],)
            inner_sends = inner_blur(w, wx, half, inner - half, radius, after, 1.0)
            v_inner = depth_exchange(*inner_sends)
        else:
            edge_sends = edge_blur(w, beyond, wx, (ah, al), radius)
            v_edge = depth_exchange(*edge_sends)
            after = (edge_sends[0],)
            inner_sends = inner_blur(w, wx, 0, inner, radius, after, 1.0)
            v_inner = depth_exchange(*inner_sends)
            r_inner = []
            bh, bl, wa, rn, shifted, taps = second_weights(
                band_index, taps_x, taps_y, taps_z, inner_sends[0], observed, beyond, width
            )
            adjoint = (wa, bh, bl)
        after = (inner_sends[0],)
        r_edge = depth_exchange(
            *depth_ratio(taps, shifted, [v_edge], inner, after, 1.0 if step else 1.0)
        )
        r_sends = depth_ratio(
            taps, shifted, [v_inner], half if step else 0, (r_edge[0],), 1.0
        )
        r_inner.append(depth_exchange(*r_sends))
        after = r_sends[0]
        c_inner = []
        if step:
            c_inner.append(depth_back(taps, r_inner[0], n, after, 5.0))
            after = c_inner[0]
        c_edge = depth_back(taps, r_edge, n, after, 1.0 if step else 1.0)
        before = ring(c_edge, 1)
        c_inner.append(depth_back(taps, r_inner[-1], n, c_edge, 100.0))
        last = step == ITERS - 1
        out = update(
            (before, *c_inner, c_edge), est, rn, adjoint,
            None if last else (wx, ah, al), half, radius,
        )
        est = out[0]
        if not last:
            w, top, *first_sends = out[1:]
            beyond = ring(top, -1)
    return est


def solution(mesh):
    in_specs = (P(("grp", "slab"), "row", None), P("slab"), P(), P(), P())
    out_specs = P(("grp", "slab"), "row", None)
    return jax.shard_map(
        on_device, mesh=mesh, in_specs=in_specs, out_specs=out_specs, check_vma=False
    )
```

```python
import functools

import jax
import jax.numpy as jnp
from jax import lax
from jax.experimental import pallas as pl
from jax.experimental.pallas import tpu as pltpu
from jax.sharding import PartitionSpec as P

ITERS = 2
F32 = jnp.float32
BF16 = jnp.bfloat16
PARAMS = pltpu.CompilerParams(vmem_limit_bytes=16 * 1024 * 1024)
SMEM = pl.BlockSpec(memory_space=pltpu.SMEM)
VMEM = pl.BlockSpec(memory_space=pltpu.VMEM)
ANY = pl.BlockSpec(memory_space=pl.ANY)


def up(value, step):
    return -(-value // step) * step


def split(x):
    hi = x.astype(BF16)
    return hi, (x - hi.astype(F32)).astype(BF16)


def mm(a, b):
    return jnp.dot(a, b, preferred_element_type=F32)


def blur_rows(w_hi, w_lo, v_hi, v_lo):
    count = w_hi.shape[0]
    both = mm(jnp.concatenate([w_hi, w_lo], axis=0), v_hi)
    return both[:count] + both[count:] + mm(w_hi, v_lo)


def blur_columns(u, a_hi, a_lo):
    count = u.shape[0]
    u_hi, u_lo = split(u)
    both = mm(jnp.concatenate([u_hi, u_lo], axis=0), a_hi)
    return both[:count] + both[count:] + mm(u_hi, a_lo)


def cost(microseconds):
    return pl.CostEstimate(
        flops=int(microseconds * 1e9), bytes_accessed=int(microseconds * 3.5e6), transcendentals=0
    )


def shape_of(*dims, dtype=F32):
    return jax.ShapeDtypeStruct(dims, dtype)


def spread(ref, band, lanes, radius, flip):
    base = jnp.zeros(lanes.shape, F32)
    for k in range(2 * radius + 1):
        base = jnp.where(lanes == (2 * radius - k if flip else k), ref[band, k], base)
    return base


def iotas(rows, lanes):
    shape = (rows, lanes)
    return (
        lax.broadcasted_iota(jnp.int32, shape, 0),
        lax.broadcasted_iota(jnp.int32, shape, 1),
    )


def column_matrix(base, radius, h_ref, l_ref, p):
    columns = h_ref.shape[1]
    sub, lane = iotas(16, 128)
    rolled = {}
    sums = [None] * (columns // 128)
    for first in range(0, columns, 16):
        key = first % 128
        if key not in rolled:
            rolled[key] = pltpu.roll(base, (key - radius) % 128, 1, stride=1, stride_axis=0)
        for block in range(columns // 128):
            left = block * 128
            here = (p, slice(first, first + 16), slice(left, left + 128))
            if left > first + 15 + radius or left + 127 < first - radius:
                zero = jnp.zeros((16, 128), BF16)
                h_ref[here] = zero
                l_ref[here] = zero
                continue
            inside = jnp.abs(lane - sub + (left - first)) <= radius
            tile = jnp.where(inside, rolled[key], 0.0)
            h_ref[here], l_ref[here] = split(tile)
            sums[block] = tile if sums[block] is None else sums[block] + tile
    return [jnp.sum(s, axis=0, keepdims=True) for s in sums]


def row_matrix(base, rows, shift, width):
    return jnp.concatenate(
        [
            pltpu.roll(base, (first + shift) % width, 1, stride=1, stride_axis=0)
            for first in range(0, rows, 16)
        ],
        axis=0,
    )


def store_sends(v, plane, n, radius, low_ref, high_ref):
    if plane < radius:
        low_ref[plane] = v
    if plane >= n - radius:
        high_ref[plane - (n - radius)] = v


def all_columns(source, a_refs, out_ref):
    for p in range(out_ref.shape[0]):
        out_ref[p] = blur_columns(source(p), a_refs[0][p], a_refs[1][p])


def own_rows(w_ref, wx_ref, low_ref, high_ref, first=0):
    n, rows, _ = w_ref.shape
    radius, count, _ = low_ref.shape
    part = slice(first, first + count)
    for p in range(n):
        w_hi, w_lo = split(w_ref[p])
        v = blur_rows(wx_ref[p, 0, part, :rows], wx_ref[p, 1, part, :rows], w_hi, w_lo)
        store_sends(v, p, n, radius, low_ref, high_ref)


def row_place():
    row = lax.axis_index("row")
    return row == 0, row == lax.axis_size("row") - 1


def first_kernel(
    n, radius, band_hbm, tx_hbm, ty_hbm, est_hbm,
    ah_ref, al_ref, wx_ref, w_ref,
    band_ref, tx_ref, ty_ref, est_ref, sems,
):
    pairs = ((band_hbm, band_ref), (tx_hbm, tx_ref), (ty_hbm, ty_ref), (est_hbm, est_ref))
    copies = [pltpu.make_async_copy(a, b, sems.at[k]) for k, (a, b) in enumerate(pairs)]
    for copy in copies:
        copy.start()
    rows, width = wx_ref.shape[2], wx_ref.shape[3]
    _, lane = iotas(16, 128)
    _, wide = iotas(16, width)
    row, lanes = iotas(rows, width)
    keep = jnp.logical_not(row_place()[1]) | ((row < rows - radius) == (lanes < rows))
    for copy in copies:
        copy.wait()
    for p in range(n):
        band = band_ref[p]
        column_matrix(spread(ty_ref, band, lane, radius, True), radius, ah_ref, al_ref, p)
        matrix = row_matrix(spread(tx_ref, band, wide, radius, False), rows, 0, width)
        wx_ref[p, 0], wx_ref[p, 1] = split(jnp.where(keep, matrix, 0.0))
    all_columns(lambda p: est_ref[p], (ah_ref, al_ref), w_ref)


def first_blur(band_index, taps_x, taps_y, est, width):
    n, rows, columns = est.shape
    radius = taps_x.shape[1] // 2
    a = shape_of(n, columns, columns, dtype=BF16)
    w = shape_of(n, 2, rows, width, dtype=BF16)
    return pl.pallas_call(
        functools.partial(first_kernel, n, radius),
        in_specs=[pl.BlockSpec(memory_space=pltpu.HBM)] * 4,
        scratch_shapes=[
            pltpu.SMEM(band_index.shape, jnp.int32),
            pltpu.SMEM(taps_x.shape, F32),
            pltpu.SMEM(taps_y.shape, F32),
            pltpu.VMEM(est.shape, F32),
            pltpu.SemaphoreType.DMA((4,)),
        ],
        out_specs=[VMEM] * 4,
        out_shape=[a, a, w, shape_of(*est.shape)],
        compiler_params=PARAMS,
        cost_estimate=cost(1.0),
    )(band_index, taps_x, taps_y, est)


def second_kernel(
    n, radius, halo, band_ref, tx_ref, ty_ref, tz_ref, after_ref,
    obs_ref, next_ref, ah_ref, al_ref, wx_ref, rn_ref, shifted_ref, taps_ref,
):
    rows, width = wx_ref.shape[2], wx_ref.shape[3]
    first_row, last_row = row_place()
    below = lax.axis_index("slab") * n
    depth = lax.axis_size("slab") * n
    _, lane = iotas(16, 128)
    _, wide = iotas(16, width)
    _, lanes = iotas(rows, width)
    lower = jnp.logical_not(first_row) | (lanes >= halo - radius)
    upper = jnp.logical_not(last_row) | (lanes < rows - radius + halo)
    keep = ((lanes < halo) & lower) | ((lanes >= halo) & upper)
    for k in range(2 * radius + 1):
        taps_ref[k] = jnp.full(taps_ref.shape[1:], tz_ref[k], F32)
    for p in range(n):
        band = band_ref[p]
        sums = column_matrix(
            spread(ty_ref, band, lane, radius, False), radius, ah_ref, al_ref, p
        )
        matrix = row_matrix(
            spread(tx_ref, band, wide, radius, True), rows, halo - 2 * radius, width
        )
        matrix = jnp.where(keep, matrix, 0.0)
        wx_ref[p, 0], wx_ref[p, 1] = split(matrix)
        along_x = jnp.sum(matrix, axis=1, keepdims=True)
        along_z = jnp.float32(0.0)
        z = below + p
        for k in range(2 * radius + 1):
            source = z - k + radius
            inside = (source >= 0) & (source < depth)
            along_z = along_z + jnp.where(inside, tz_ref[k], 0.0)
        for block, along_y in enumerate(sums):
            rn_ref[p, :, block * 128 : block * 128 + 128] = 1.0 / (
                along_x * (along_y * along_z)
            )
        shifted_ref[p, : rows - radius] = obs_ref[p, radius:]
        shifted_ref[p, rows - radius :] = next_ref[p, :radius]


def second_weights(band_index, taps_x, taps_y, taps_z, after, obs, beyond, width):
    n, rows, columns = obs.shape
    halo = beyond.shape[1]
    radius = taps_x.shape[1] // 2
    a = shape_of(n, columns, columns, dtype=BF16)
    w = shape_of(n, 2, rows, width, dtype=BF16)
    field = shape_of(*obs.shape)
    return pl.pallas_call(
        functools.partial(second_kernel, n, radius, halo),
        in_specs=[SMEM] * 4 + [ANY] + [VMEM] * 2,
        out_specs=[VMEM] * 6,
        out_shape=[a, a, w, field, field, shape_of(2 * radius + 1, 8, 128)],
        compiler_params=PARAMS,
        cost_estimate=cost(1.0),
    )(band_index, taps_x, taps_y, taps_z, after, obs, beyond)


def inner_kernel(first, w_ref, wx_ref, *refs):
    own_rows(w_ref, wx_ref, *refs[-2:], first)


def inner_blur(w, wx, first, count, radius, after, micro):
    send = shape_of(radius, count, w.shape[2])
    return pl.pallas_call(
        functools.partial(inner_kernel, first),
        in_specs=[VMEM] * 2 + [ANY] * len(after),
        out_specs=[VMEM] * 2,
        out_shape=[send] * 2,
        compiler_params=PARAMS,
        cost_estimate=cost(micro),
    )(w, wx, *after)


def edge_kernel(n, radius, blurred, w_ref, next_ref, wx_ref, *refs):
    rows, halo = w_ref.shape[1], next_ref.shape[1]
    inner, used = rows - halo, rows + halo
    beyond_ref = next_ref
    if not blurred:
        beyond_ref, refs = refs[-1], refs[:-1]
        all_columns(lambda p: next_ref[p], refs[:2], beyond_ref)
    for p in range(n):
        w_hi, w_lo = split(jnp.concatenate([w_ref[p], beyond_ref[p]], axis=0))
        v = blur_rows(wx_ref[p, 0, inner:, :used], wx_ref[p, 1, inner:, :used], w_hi, w_lo)
        store_sends(v, p, n, radius, *refs[-2:])


def edge_blur(w, beyond, wx, columns_matrix, radius):
    n, _, columns = w.shape
    halo = beyond.shape[1]
    send = shape_of(radius, halo, columns)
    args = (w, beyond, wx, *columns_matrix)
    return pl.pallas_call(
        functools.partial(edge_kernel, n, radius, not columns_matrix),
        in_specs=[VMEM] * len(args),
        out_specs=[VMEM] * 2,
        out_shape=[send] * 2,
        scratch_shapes=[pltpu.VMEM(beyond.shape, F32)] if columns_matrix else [],
        compiler_params=PARAMS,
        cost_estimate=cost(1.0),
    )(*args)


def depth_sum(n, radius, flip, tz_ref, refs, rows, lanes):
    low_ref, high_ref, zlo_ref, zhi_ref = refs
    last = 2 * radius
    taps = [tz_ref[last - k if flip else k] for k in range(last + 1)]
    total = [None] * n
    for j in range(-radius, n + radius):
        if j < 0:
            piece = zlo_ref[j + radius, rows, lanes]
        elif j < radius:
            piece = low_ref[j, rows, lanes]
        elif j < n:
            piece = high_ref[j - (n - radius), rows, lanes]
        else:
            piece = zhi_ref[j - n, rows, lanes]
        for i in range(max(0, j - radius), min(n, j + radius + 1)):
            term = taps[j - i + radius] * piece
            total[i] = term if total[i] is None else total[i] + term
    return total


def tiles(count, columns, body):
    def step(t, carry):
        for left in range(0, columns, 128):
            body(t * 8, slice(left, left + 128))
        return carry

    lax.fori_loop(0, count // 8, step, 0)


def at(start, offset):
    return pl.ds(pl.multiple_of(start + offset, 8), 8)


def ratio_kernel(n, radius, skip, tz_ref, obs_ref, *refs):
    rlow_ref, rhigh_ref = refs[-2:]
    columns = obs_ref.shape[2]

    def run(own, first):
        def body(start, lanes):
            total = depth_sum(n, radius, False, tz_ref, own, at(start, 0), lanes)
            rows = at(start, first)
            for i in range(n):
                ratio = obs_ref[i, at(start, skip + first), lanes] / total[i]
                if i < radius:
                    rlow_ref[i, rows, lanes] = ratio
                if i >= n - radius:
                    rhigh_ref[i - (n - radius), rows, lanes] = ratio

        tiles(own[0].shape[1], columns, body)

    first = 0
    while first < rlow_ref.shape[1]:
        run(refs[:4], first)
        first += refs[0].shape[1]
        refs = refs[4:]


def depth_ratio(taps_z, obs, chunks, skip, after, micro):
    n, _, columns = obs.shape
    radius = chunks[0][0].shape[0]
    send = shape_of(radius, sum(chunk[0].shape[1] for chunk in chunks), columns)
    return pl.pallas_call(
        functools.partial(ratio_kernel, n, radius, skip),
        in_specs=[VMEM] * (2 + 4 * len(chunks)) + [ANY] * len(after),
        out_specs=[VMEM] * 2,
        out_shape=[send] * 2,
        compiler_params=PARAMS,
        cost_estimate=cost(micro),
    )(taps_z, obs, *(x for chunk in chunks for x in chunk), *after)


def back_kernel(n, radius, tz_ref, *refs):
    out_ref = refs[-1]
    _, count, columns = out_ref.shape

    def body(start, lanes):
        rows = at(start, 0)
        total = depth_sum(n, radius, True, tz_ref, refs[:4], rows, lanes)
        for i in range(n):
            out_ref[i, rows, lanes] = total[i]

    tiles(count, columns, body)


def depth_back(taps_z, chunk, n, after, micro=1.0):
    radius, count, columns = chunk[0].shape
    return pl.pallas_call(
        functools.partial(back_kernel, n, radius),
        in_specs=[VMEM] * 5 + [ANY],
        out_specs=VMEM,
        out_shape=shape_of(n, count, columns),
        compiler_params=PARAMS,
        cost_estimate=cost(micro),
    )(taps_z, *chunk, after)


def adjoint_rows(pieces, wa_ref, b_refs, est_ref, rn_ref, part, u_ref, store):
    n = est_ref.shape[0]
    used = sum(piece.shape[1] for piece in pieces)
    for p in range(n):
        c_hi, c_lo = split(jnp.concatenate([piece[p] for piece in pieces], axis=0))
        w_hi, w_lo = wa_ref[p, 0, part, :used], wa_ref[p, 1, part, :used]
        u_ref[p] = blur_rows(w_hi, w_lo, c_hi, c_lo)
    for p in range(n):
        u = blur_columns(u_ref[p], b_refs[0][p], b_refs[1][p])
        store(p, est_ref[p, part] * u * rn_ref[p, part])


def update_kernel(count, *refs):
    pieces, refs = refs[:count], refs[count:]
    est_ref, rn_ref, wa_ref, bh_ref, bl_ref, wx_ref, ah_ref, al_ref = refs[:8]
    out_ref, w_ref, top_ref, low_ref, high_ref, u_ref = refs[8:]
    n, rows, _ = est_ref.shape

    def store(p, value):
        out_ref[p] = value

    part = slice(0, rows)
    adjoint_rows(pieces, wa_ref, (bh_ref, bl_ref), est_ref, rn_ref, part, u_ref, store)
    all_columns(lambda p: out_ref[p], (ah_ref, al_ref), w_ref)
    for p in range(n):
        top_ref[p] = w_ref[p, : top_ref.shape[1]]
    own_rows(w_ref, wx_ref, low_ref, high_ref)


def update(pieces, est, rn, adjoint, forward, count, radius):
    n, rows, columns = est.shape
    halo = pieces[0].shape[1]
    args = [*pieces, est, rn, *adjoint, *forward]
    send = shape_of(radius, count, columns)
    field = shape_of(*est.shape)
    return pl.pallas_call(
        functools.partial(update_kernel, len(pieces)),
        in_specs=[VMEM] * len(args),
        out_specs=[VMEM] * 5,
        out_shape=[field, field, shape_of(n, halo, columns), send, send],
        scratch_shapes=[pltpu.VMEM(est.shape, F32)],
        compiler_params=PARAMS,
        cost_estimate=cost(1.0),
    )(*args)


def far_kernel(count, *refs):
    pieces, refs = refs[:count], refs[count:]
    est_ref, rn_ref, wa_ref, bh_ref, bl_ref, far_ref, zero_ref, u_ref = refs
    rows, halo = est_ref.shape[1], zero_ref.shape[1]
    zero_ref[...] = jnp.zeros(zero_ref.shape, F32)

    def store(p, value):
        far_ref[p] = value

    pieces = (zero_ref, *pieces)
    part = slice(halo, rows)
    adjoint_rows(pieces, wa_ref, (bh_ref, bl_ref), est_ref, rn_ref, part, u_ref, store)


def far_rows(pieces, halo, est, rn, adjoint):
    n, rows, columns = est.shape
    args = [*pieces, est, rn, *adjoint]
    far = (n, rows - halo, columns)
    return pl.pallas_call(
        functools.partial(far_kernel, len(pieces)),
        in_specs=[VMEM] * len(args),
        out_specs=VMEM,
        out_shape=shape_of(*far),
        scratch_shapes=[pltpu.VMEM((n, halo, columns), F32), pltpu.VMEM(far, F32)],
        compiler_params=PARAMS,
        cost_estimate=cost(100.0),
    )(*args)


def near_kernel(count, *refs):
    pieces, refs = refs[:count], refs[count:]
    est_ref, rn_ref, wa_ref, bh_ref, bl_ref, far_ref, out_ref, u_ref = refs
    halo = u_ref.shape[1]
    out_ref[:, halo:] = far_ref[...]

    def store(p, value):
        out_ref[p, :halo] = value

    part = slice(0, halo)
    adjoint_rows(pieces, wa_ref, (bh_ref, bl_ref), est_ref, rn_ref, part, u_ref, store)


def near_rows(pieces, est, rn, adjoint, far):
    n, _, columns = est.shape
    args = [*pieces, est, rn, *adjoint, far]
    return pl.pallas_call(
        functools.partial(near_kernel, len(pieces)),
        in_specs=[VMEM] * len(args),
        out_specs=VMEM,
        out_shape=shape_of(*est.shape),
        scratch_shapes=[pltpu.VMEM((n, pieces[0].shape[1], columns), F32)],
        compiler_params=PARAMS,
        cost_estimate=cost(1.0),
    )(*args)


def depth_exchange(low, high):
    count = lax.axis_size("slab")
    forward = [(i, i + 1) for i in range(count - 1)]
    backward = [(i + 1, i) for i in range(count - 1)]
    zlo = lax.ppermute(high, "slab", forward)
    zhi = lax.ppermute(low, "slab", backward)
    return low, high, zlo, zhi


def ring(x, step):
    count = lax.axis_size("row")
    return lax.ppermute(x, "row", [(i, (i + step) % count) for i in range(count)])


def on_device(observed, band_index, taps_x, taps_y, taps_z):
    n, rows, columns = observed.shape
    radius = taps_z.shape[0] // 2
    halo = up(2 * radius, 16)
    inner = rows - halo
    half = up(inner // 2, 16)
    width = up(rows + halo, 128)
    beyond = ring(observed[:, :halo], -1)
    ah, al, wx, w = first_blur(band_index, taps_x, taps_y, observed, width)
    est, adjoint = observed, None
    for step in range(ITERS):
        if step:
            v_first = depth_exchange(*first_sends)
            edge_sends = edge_blur(w, beyond, wx, (), radius)
            v_edge = depth_exchange(*edge_sends)
            r_sends = depth_ratio(taps, shifted, [v_first], 0, (edge_sends[0],), 20.0)
            r_inner = [depth_exchange(*r_sends)]
            after = (r_sends[0],)
            inner_sends = inner_blur(w, wx, half, inner - half, radius, after, 1.0)
            v_inner = depth_exchange(*inner_sends)
        else:
            edge_sends = edge_blur(w, beyond, wx, (ah, al), radius)
            v_edge = depth_exchange(*edge_sends)
            after = (edge_sends[0],)
            inner_sends = inner_blur(w, wx, 0, inner, radius, after, 1.0)
            v_inner = depth_exchange(*inner_sends)
            r_inner = []
            bh, bl, wa, rn, shifted, taps = second_weights(
                band_index, taps_x, taps_y, taps_z, inner_sends[0], observed, beyond, width
            )
            adjoint = (wa, bh, bl)
        after = (inner_sends[0],)
        r_edge = depth_exchange(
            *depth_ratio(taps, shifted, [v_edge], inner, after, 1.0 if step else 1.0)
        )
        after, c_inner = r_edge[0], []
        if step:
            after = depth_back(taps, r_inner[0], n, after, 5.0)
            c_inner.append(after)
        r_sends = depth_ratio(
            taps, shifted, [v_inner], half if step else 0, (after,), 1.0 if step else 1.0
        )
        r_inner.append(depth_exchange(*r_sends))
        after = r_sends[0]
        c_edge = depth_back(taps, r_edge, n, after, 1.0 if step else 1.0)
        before = ring(c_edge, 1)
        c_inner.append(depth_back(taps, r_inner[-1], n, c_edge, 100.0))
        own = (*c_inner, c_edge)
        if step == ITERS - 1:
            far = far_rows(own, halo, est, rn, adjoint)
            return near_rows((before, *own), est, rn, adjoint, far)
        est, w, top, *first_sends = update(
            (before, *own), est, rn, adjoint, (wx, ah, al), half, radius
        )
        beyond = ring(top, -1)


def solution(mesh):
    in_specs = (P(("grp", "slab"), "row", None), P("slab"), P(), P(), P())
    out_specs = P(("grp", "slab"), "row", None)
    return jax.shard_map(
        on_device, mesh=mesh, in_specs=in_specs, out_specs=out_specs, check_vma=False
    )
```

```python
import functools

import jax
import jax.numpy as jnp
from jax import lax
from jax.experimental import pallas as pl
from jax.experimental.pallas import tpu as pltpu
from jax.sharding import PartitionSpec as P

ITERS = 2
GROUPS = 4
F32 = jnp.float32
BF16 = jnp.bfloat16
PARAMS = pltpu.CompilerParams(vmem_limit_bytes=16 * 1024 * 1024)
SMEM = pl.BlockSpec(memory_space=pltpu.SMEM)
VMEM = pl.BlockSpec(memory_space=pltpu.VMEM)
ANY = pl.BlockSpec(memory_space=pl.ANY)


def up(value, step):
    return -(-value // step) * step


def split(x):
    hi = x.astype(BF16)
    return hi, (x - hi.astype(F32)).astype(BF16)


def mm(a, b):
    return jnp.dot(a, b, preferred_element_type=F32)


def blur_rows(w_hi, w_lo, v_hi, v_lo):
    count = w_hi.shape[0]
    both = mm(jnp.concatenate([w_hi, w_lo], axis=0), v_hi)
    return both[:count] + both[count:] + mm(w_hi, v_lo)


def blur_columns(u, a_hi, a_lo):
    count = u.shape[0]
    u_hi, u_lo = split(u)
    both = mm(jnp.concatenate([u_hi, u_lo], axis=0), a_hi)
    return both[:count] + both[count:] + mm(u_hi, a_lo)


def cost(microseconds):
    return pl.CostEstimate(
        flops=int(microseconds * 1e9), bytes_accessed=int(microseconds * 3.5e6), transcendentals=0
    )


def shape_of(*dims, dtype=F32):
    return jax.ShapeDtypeStruct(dims, dtype)


def spread(ref, band, lanes, radius, flip):
    base = jnp.zeros(lanes.shape, F32)
    for k in range(2 * radius + 1):
        base = jnp.where(lanes == (2 * radius - k if flip else k), ref[band, k], base)
    return base


def iotas(rows, lanes):
    shape = (rows, lanes)
    return (
        lax.broadcasted_iota(jnp.int32, shape, 0),
        lax.broadcasted_iota(jnp.int32, shape, 1),
    )


def column_matrix(base, radius, h_ref, l_ref, p):
    columns = h_ref.shape[1]
    sub, lane = iotas(16, 128)
    rolled = {}
    sums = [None] * (columns // 128)
    for first in range(0, columns, 16):
        key = first % 128
        if key not in rolled:
            rolled[key] = pltpu.roll(base, (key - radius) % 128, 1, stride=1, stride_axis=0)
        for block in range(columns // 128):
            left = block * 128
            here = (p, slice(first, first + 16), slice(left, left + 128))
            if left > first + 15 + radius or left + 127 < first - radius:
                zero = jnp.zeros((16, 128), BF16)
                h_ref[here] = zero
                l_ref[here] = zero
                continue
            inside = jnp.abs(lane - sub + (left - first)) <= radius
            tile = jnp.where(inside, rolled[key], 0.0)
            h_ref[here], l_ref[here] = split(tile)
            sums[block] = tile if sums[block] is None else sums[block] + tile
    return [jnp.sum(s, axis=0, keepdims=True) for s in sums]


def row_matrix(base, rows, shift, width):
    return jnp.concatenate(
        [
            pltpu.roll(base, (first + shift) % width, 1, stride=1, stride_axis=0)
            for first in range(0, rows, 16)
        ],
        axis=0,
    )


def store_sends(v, plane, n, radius, low_ref, high_ref):
    if plane < radius:
        low_ref[plane] = v
    if plane >= n - radius:
        high_ref[plane - (n - radius)] = v


def all_columns(source, a_refs, out_ref):
    for p in range(out_ref.shape[0]):
        out_ref[p] = blur_columns(source(p), a_refs[0][p], a_refs[1][p])


def own_rows(w_ref, wx_ref, low_ref, high_ref, first=0):
    n, rows, _ = w_ref.shape
    radius, count, _ = low_ref.shape
    part = slice(first, first + count)
    for p in range(n):
        w_hi, w_lo = split(w_ref[p])
        v = blur_rows(wx_ref[p, 0, part, :rows], wx_ref[p, 1, part, :rows], w_hi, w_lo)
        store_sends(v, p, n, radius, low_ref, high_ref)


def row_place():
    row = lax.axis_index("row")
    return row == 0, row == lax.axis_size("row") - 1


def first_kernel(
    n, radius, band_hbm, tx_hbm, ty_hbm, est_hbm,
    ah_ref, al_ref, wx_ref, w_ref,
    band_ref, tx_ref, ty_ref, est_ref, sems,
):
    pairs = ((band_hbm, band_ref), (tx_hbm, tx_ref), (ty_hbm, ty_ref), (est_hbm, est_ref))
    copies = [pltpu.make_async_copy(a, b, sems.at[k]) for k, (a, b) in enumerate(pairs)]
    for copy in copies:
        copy.start()
    rows, width = wx_ref.shape[2], wx_ref.shape[3]
    _, lane = iotas(16, 128)
    _, wide = iotas(16, width)
    row, lanes = iotas(rows, width)
    keep = jnp.logical_not(row_place()[1]) | ((row < rows - radius) == (lanes < rows))
    for copy in copies:
        copy.wait()
    for p in range(n):
        band = band_ref[p]
        column_matrix(spread(ty_ref, band, lane, radius, True), radius, ah_ref, al_ref, p)
        matrix = row_matrix(spread(tx_ref, band, wide, radius, False), rows, 0, width)
        wx_ref[p, 0], wx_ref[p, 1] = split(jnp.where(keep, matrix, 0.0))
    all_columns(lambda p: est_ref[p], (ah_ref, al_ref), w_ref)


def first_blur(band_index, taps_x, taps_y, est, width):
    n, rows, columns = est.shape
    radius = taps_x.shape[1] // 2
    a = shape_of(n, columns, columns, dtype=BF16)
    w = shape_of(n, 2, rows, width, dtype=BF16)
    return pl.pallas_call(
        functools.partial(first_kernel, n, radius),
        in_specs=[pl.BlockSpec(memory_space=pltpu.HBM)] * 4,
        scratch_shapes=[
            pltpu.SMEM(band_index.shape, jnp.int32),
            pltpu.SMEM(taps_x.shape, F32),
            pltpu.SMEM(taps_y.shape, F32),
            pltpu.VMEM(est.shape, F32),
            pltpu.SemaphoreType.DMA((4,)),
        ],
        out_specs=[VMEM] * 4,
        out_shape=[a, a, w, shape_of(*est.shape)],
        compiler_params=PARAMS,
        cost_estimate=cost(1.0),
    )(band_index, taps_x, taps_y, est)


def second_kernel(
    n, radius, halo, band_ref, tx_ref, ty_ref, tz_ref, after_ref,
    obs_ref, next_ref, ah_ref, al_ref, wx_ref, rn_ref, shifted_ref, taps_ref,
):
    rows, width = wx_ref.shape[2], wx_ref.shape[3]
    first_row, last_row = row_place()
    below = lax.axis_index("slab") * n
    depth = lax.axis_size("slab") * n
    _, lane = iotas(16, 128)
    _, wide = iotas(16, width)
    _, lanes = iotas(rows, width)
    lower = jnp.logical_not(first_row) | (lanes >= halo - radius)
    upper = jnp.logical_not(last_row) | (lanes < rows - radius + halo)
    keep = ((lanes < halo) & lower) | ((lanes >= halo) & upper)
    for k in range(2 * radius + 1):
        taps_ref[k] = jnp.full(taps_ref.shape[1:], tz_ref[k], F32)
    for p in range(n):
        band = band_ref[p]
        sums = column_matrix(
            spread(ty_ref, band, lane, radius, False), radius, ah_ref, al_ref, p
        )
        matrix = row_matrix(
            spread(tx_ref, band, wide, radius, True), rows, halo - 2 * radius, width
        )
        matrix = jnp.where(keep, matrix, 0.0)
        wx_ref[p, 0], wx_ref[p, 1] = split(matrix)
        along_x = jnp.sum(matrix, axis=1, keepdims=True)
        along_z = jnp.float32(0.0)
        z = below + p
        for k in range(2 * radius + 1):
            source = z - k + radius
            inside = (source >= 0) & (source < depth)
            along_z = along_z + jnp.where(inside, tz_ref[k], 0.0)
        for block, along_y in enumerate(sums):
            rn_ref[p, :, block * 128 : block * 128 + 128] = 1.0 / (
                along_x * (along_y * along_z)
            )
        shifted_ref[p, : rows - radius] = obs_ref[p, radius:]
        shifted_ref[p, rows - radius :] = next_ref[p, :radius]


def second_weights(band_index, taps_x, taps_y, taps_z, after, obs, beyond, width):
    n, rows, columns = obs.shape
    halo = beyond.shape[1]
    radius = taps_x.shape[1] // 2
    a = shape_of(n, columns, columns, dtype=BF16)
    w = shape_of(n, 2, rows, width, dtype=BF16)
    field = shape_of(*obs.shape)
    return pl.pallas_call(
        functools.partial(second_kernel, n, radius, halo),
        in_specs=[SMEM] * 4 + [ANY] + [VMEM] * 2,
        out_specs=[VMEM] * 6,
        out_shape=[a, a, w, field, field, shape_of(2 * radius + 1, 8, 128)],
        compiler_params=PARAMS,
        cost_estimate=cost(1.0),
    )(band_index, taps_x, taps_y, taps_z, after, obs, beyond)


def inner_kernel(first, w_ref, wx_ref, *refs):
    own_rows(w_ref, wx_ref, *refs[-2:], first)


def inner_blur(w, wx, first, count, radius, after, micro):
    send = shape_of(radius, count, w.shape[2])
    return pl.pallas_call(
        functools.partial(inner_kernel, first),
        in_specs=[VMEM] * 2 + [ANY] * len(after),
        out_specs=[VMEM] * 2,
        out_shape=[send] * 2,
        compiler_params=PARAMS,
        cost_estimate=cost(micro),
    )(w, wx, *after)


def edge_kernel(n, radius, blurred, w_ref, next_ref, wx_ref, *refs):
    rows, halo = w_ref.shape[1], next_ref.shape[1]
    inner, used = rows - halo, rows + halo
    beyond_ref = next_ref
    if not blurred:
        beyond_ref, refs = refs[-1], refs[:-1]
        all_columns(lambda p: next_ref[p], refs[:2], beyond_ref)
    for p in range(n):
        w_hi, w_lo = split(jnp.concatenate([w_ref[p], beyond_ref[p]], axis=0))
        v = blur_rows(wx_ref[p, 0, inner:, :used], wx_ref[p, 1, inner:, :used], w_hi, w_lo)
        store_sends(v, p, n, radius, *refs[-2:])


def edge_blur(w, beyond, wx, columns_matrix, radius):
    n, _, columns = w.shape
    halo = beyond.shape[1]
    send = shape_of(radius, halo, columns)
    args = (w, beyond, wx, *columns_matrix)
    return pl.pallas_call(
        functools.partial(edge_kernel, n, radius, not columns_matrix),
        in_specs=[VMEM] * len(args),
        out_specs=[VMEM] * 2,
        out_shape=[send] * 2,
        scratch_shapes=[pltpu.VMEM(beyond.shape, F32)] if columns_matrix else [],
        compiler_params=PARAMS,
        cost_estimate=cost(1.0),
    )(*args)


def depth_sum(n, radius, flip, tz_ref, refs, rows, lanes):
    low_ref, high_ref, zlo_ref, zhi_ref = refs
    last = 2 * radius
    taps = [tz_ref[last - k if flip else k] for k in range(last + 1)]
    total = [None] * n
    for j in range(-radius, n + radius):
        if j < 0:
            piece = zlo_ref[j + radius, rows, lanes]
        elif j < radius:
            piece = low_ref[j, rows, lanes]
        elif j < n:
            piece = high_ref[j - (n - radius), rows, lanes]
        else:
            piece = zhi_ref[j - n, rows, lanes]
        for i in range(max(0, j - radius), min(n, j + radius + 1)):
            term = taps[j - i + radius] * piece
            total[i] = term if total[i] is None else total[i] + term
    return total


def tiles(count, columns, body):
    def step(t, carry):
        for left in range(0, columns, 128):
            body(t * 8, slice(left, left + 128))
        return carry

    lax.fori_loop(0, count // 8, step, 0)


def at(start, offset):
    return pl.ds(pl.multiple_of(start + offset, 8), 8)


def ratio_kernel(n, radius, skip, tz_ref, obs_ref, *refs):
    rlow_ref, rhigh_ref = refs[-2:]
    columns = obs_ref.shape[2]

    def run(own, first):
        def body(start, lanes):
            total = depth_sum(n, radius, False, tz_ref, own, at(start, 0), lanes)
            rows = at(start, first)
            for i in range(n):
                ratio = obs_ref[i, at(start, skip + first), lanes] / total[i]
                if i < radius:
                    rlow_ref[i, rows, lanes] = ratio
                if i >= n - radius:
                    rhigh_ref[i - (n - radius), rows, lanes] = ratio

        tiles(own[0].shape[1], columns, body)

    first = 0
    while first < rlow_ref.shape[1]:
        run(refs[:4], first)
        first += refs[0].shape[1]
        refs = refs[4:]


def depth_ratio(taps_z, obs, chunks, skip, after, micro):
    n, _, columns = obs.shape
    radius = chunks[0][0].shape[0]
    send = shape_of(radius, sum(chunk[0].shape[1] for chunk in chunks), columns)
    return pl.pallas_call(
        functools.partial(ratio_kernel, n, radius, skip),
        in_specs=[VMEM] * (2 + 4 * len(chunks)) + [ANY] * len(after),
        out_specs=[VMEM] * 2,
        out_shape=[send] * 2,
        compiler_params=PARAMS,
        cost_estimate=cost(micro),
    )(taps_z, obs, *(x for chunk in chunks for x in chunk), *after)


def back_kernel(n, radius, swapped, tz_ref, *refs):
    out_ref = refs[-1]
    if swapped:
        refs = (*refs[:2], refs[3], refs[2])
    _, count, columns = out_ref.shape

    def body(start, lanes):
        rows = at(start, 0)
        total = depth_sum(n, radius, True, tz_ref, refs[:4], rows, lanes)
        for i in range(n):
            out_ref[i, rows, lanes] = total[i]

    tiles(count, columns, body)


def depth_back(taps_z, chunk, n, after, micro=1.0, swapped=False):
    radius, count, columns = chunk[0].shape
    if swapped:
        chunk = (*chunk[:2], chunk[3], chunk[2])
    return pl.pallas_call(
        functools.partial(back_kernel, n, radius, swapped),
        in_specs=[VMEM] * 5 + [ANY],
        out_specs=VMEM,
        out_shape=shape_of(n, count, columns),
        compiler_params=PARAMS,
        cost_estimate=cost(micro),
    )(taps_z, *chunk, after)


def update_kernel(n, last, count, *refs):
    pieces, edge_ref, refs = refs[:count], refs[count - 1], refs[count:]
    est_ref, rn_ref, wa_ref, bh_ref, bl_ref = refs[:5]
    refs = refs[5:]
    rows = est_ref.shape[1]
    halo = edge_ref.shape[1]
    used = rows + halo
    if last:
        out_ref, u_ref, sems = refs
    else:
        wx_ref, ah_ref, al_ref, out_ref, w_ref, top_ref, low_ref, high_ref, u_ref = refs
    for p in range(n):
        c_hi, c_lo = split(jnp.concatenate([piece[p] for piece in pieces], axis=0))
        u_ref[p] = blur_rows(wa_ref[p, 0, :, :used], wa_ref[p, 1, :, :used], c_hi, c_lo)
    if last:
        copies = []
        group = up(n, GROUPS) // GROUPS
        for first in range(0, n, group):
            part = pl.ds(first, min(group, n - first))
            for p in range(first, min(first + group, n)):
                u = blur_columns(u_ref[p], bh_ref[p], bl_ref[p])
                u_ref[p] = est_ref[p] * u * rn_ref[p]
            copies.append(
                pltpu.make_async_copy(
                    u_ref.at[part], out_ref.at[part], sems.at[len(copies)]
                )
            )
            copies[-1].start()
        for copy in copies:
            copy.wait()
        return
    for p in range(n):
        u = blur_columns(u_ref[p], bh_ref[p], bl_ref[p])
        out_ref[p] = est_ref[p] * u * rn_ref[p]
    all_columns(lambda p: out_ref[p], (ah_ref, al_ref), w_ref)
    for p in range(n):
        top_ref[p] = w_ref[p, :halo]
    own_rows(w_ref, wx_ref, low_ref, high_ref)


def update(pieces, est, rn, adjoint, forward, count, radius):
    n, rows, columns = est.shape
    halo = pieces[0].shape[1]
    last = forward is None
    sems = pltpu.SemaphoreType.DMA((GROUPS,))
    args = [*pieces, est, rn, *adjoint] + ([] if last else [*forward])
    out_shape = [shape_of(*est.shape)]
    if not last:
        send = shape_of(radius, count, columns)
        out_shape += [shape_of(*est.shape), shape_of(n, halo, columns), send, send]
    return pl.pallas_call(
        functools.partial(update_kernel, n, last, len(pieces)),
        in_specs=[VMEM] * len(args),
        out_specs=[ANY] if last else [VMEM] * len(out_shape),
        out_shape=out_shape,
        scratch_shapes=[pltpu.VMEM(est.shape, F32)] + [sems] * last,
        compiler_params=PARAMS,
        cost_estimate=cost(1.0),
    )(*args)


def depth_exchange(low, high):
    count = lax.axis_size("slab")
    forward = [(i, i + 1) for i in range(count - 1)]
    backward = [(i + 1, i) for i in range(count - 1)]
    zlo = lax.ppermute(high, "slab", forward)
    zhi = lax.ppermute(low, "slab", backward)
    return low, high, zlo, zhi


def ring(x, step):
    count = lax.axis_size("row")
    return lax.ppermute(x, "row", [(i, (i + step) % count) for i in range(count)])


def on_device(observed, band_index, taps_x, taps_y, taps_z):
    n, rows, columns = observed.shape
    radius = taps_z.shape[0] // 2
    halo = up(2 * radius, 16)
    inner = rows - halo
    half = up(inner // 2, 16)
    width = up(rows + halo, 128)
    beyond = ring(observed[:, :halo], -1)
    ah, al, wx, w = first_blur(band_index, taps_x, taps_y, observed, width)
    est, adjoint = observed, None
    for step in range(ITERS):
        if step:
            v_first = depth_exchange(*first_sends)
            edge_sends = edge_blur(w, beyond, wx, (), radius)
            v_edge = depth_exchange(*edge_sends)
            r_sends = depth_ratio(taps, shifted, [v_first], 0, (edge_sends[0],), 1.0)
            r_inner = [depth_exchange(*r_sends)]
            after = (r_sends[0],)
            inner_sends = inner_blur(w, wx, half, inner - half, radius, after, 1.0)
            v_inner = depth_exchange(*inner_sends)
        else:
            edge_sends = edge_blur(w, beyond, wx, (ah, al), radius)
            v_edge = depth_exchange(*edge_sends)
            after = (edge_sends[0],)
            inner_sends = inner_blur(w, wx, 0, inner, radius, after, 1.0)
            v_inner = depth_exchange(*inner_sends)
            r_inner = []
            bh, bl, wa, rn, shifted, taps = second_weights(
                band_index, taps_x, taps_y, taps_z, inner_sends[0], observed, beyond, width
            )
            adjoint = (wa, bh, bl)
        after = (inner_sends[0],)
        r_edge = depth_exchange(
            *depth_ratio(taps, shifted, [v_edge], inner, after, 1.0),
        )
        r_sends = depth_ratio(
            taps, shifted, [v_inner], half if step else 0, (r_edge[0],), 1.0
        )
        r_inner.append(depth_exchange(*r_sends))
        after = r_sends[0]
        c_inner = []
        if step:
            c_inner.append(depth_back(taps, r_inner[0], n, after, 5.0))
            after = c_inner[0]
        c_edge = depth_back(taps, r_edge, n, after, 1.0, step > 0)
        before = ring(c_edge, 1)
        c_inner.append(depth_back(taps, r_inner[-1], n, c_edge, 100.0))
        last = step == ITERS - 1
        out = update(
            (before, *c_inner, c_edge), est, rn, adjoint,
            None if last else (wx, ah, al), half, radius,
        )
        est = out[0]
        if not last:
            w, top, *first_sends = out[1:]
            beyond = ring(top, -1)
    return est


def solution(mesh):
    in_specs = (P(("grp", "slab"), "row", None), P("slab"), P(), P(), P())
    out_specs = P(("grp", "slab"), "row", None)
    return jax.shard_map(
        on_device, mesh=mesh, in_specs=in_specs, out_specs=out_specs, check_vma=False
    )
```

```python
import functools

import jax
import jax.numpy as jnp
from jax import lax
from jax.experimental import pallas as pl
from jax.experimental.pallas import tpu as pltpu
from jax.sharding import PartitionSpec as P

ITERS = 2
GROUPS = 4
F32 = jnp.float32
BF16 = jnp.bfloat16
PARAMS = pltpu.CompilerParams(vmem_limit_bytes=16 * 1024 * 1024)
SMEM = pl.BlockSpec(memory_space=pltpu.SMEM)
VMEM = pl.BlockSpec(memory_space=pltpu.VMEM)
ANY = pl.BlockSpec(memory_space=pl.ANY)


def up(value, step):
    return -(-value // step) * step


def split(x):
    hi = x.astype(BF16)
    return hi, (x - hi.astype(F32)).astype(BF16)


def mm(a, b):
    return jnp.dot(a, b, preferred_element_type=F32)


def blur_rows(w_hi, w_lo, v_hi, v_lo):
    count = w_hi.shape[0]
    both = mm(jnp.concatenate([w_hi, w_lo], axis=0), v_hi)
    return both[:count] + both[count:] + mm(w_hi, v_lo)


def blur_columns(u, a_hi, a_lo):
    count = u.shape[0]
    u_hi, u_lo = split(u)
    both = mm(jnp.concatenate([u_hi, u_lo], axis=0), a_hi)
    return both[:count] + both[count:] + mm(u_hi, a_lo)


def cost(microseconds):
    return pl.CostEstimate(
        flops=int(microseconds * 1e9), bytes_accessed=int(microseconds * 3.5e6), transcendentals=0
    )


def shape_of(*dims, dtype=F32):
    return jax.ShapeDtypeStruct(dims, dtype)


def spread(ref, band, lanes, radius, flip):
    base = jnp.zeros(lanes.shape, F32)
    for k in range(2 * radius + 1):
        base = jnp.where(lanes == (2 * radius - k if flip else k), ref[band, k], base)
    return base


def iotas(rows, lanes):
    shape = (rows, lanes)
    return (
        lax.broadcasted_iota(jnp.int32, shape, 0),
        lax.broadcasted_iota(jnp.int32, shape, 1),
    )


def column_matrix(base, radius, h_ref, l_ref, p):
    columns = h_ref.shape[1]
    sub, lane = iotas(16, 128)
    rolled = {}
    sums = [None] * (columns // 128)
    for first in range(0, columns, 16):
        key = first % 128
        if key not in rolled:
            rolled[key] = pltpu.roll(base, (key - radius) % 128, 1, stride=1, stride_axis=0)
        for block in range(columns // 128):
            left = block * 128
            here = (p, slice(first, first + 16), slice(left, left + 128))
            if left > first + 15 + radius or left + 127 < first - radius:
                zero = jnp.zeros((16, 128), BF16)
                h_ref[here] = zero
                l_ref[here] = zero
                continue
            inside = jnp.abs(lane - sub + (left - first)) <= radius
            tile = jnp.where(inside, rolled[key], 0.0)
            h_ref[here], l_ref[here] = split(tile)
            sums[block] = tile if sums[block] is None else sums[block] + tile
    return [jnp.sum(s, axis=0, keepdims=True) for s in sums]


def row_matrix(base, rows, shift, width):
    return jnp.concatenate(
        [
            pltpu.roll(base, (first + shift) % width, 1, stride=1, stride_axis=0)
            for first in range(0, rows, 16)
        ],
        axis=0,
    )


def store_sends(v, plane, n, radius, low_ref, high_ref):
    if plane < radius:
        low_ref[plane] = v
    if plane >= n - radius:
        high_ref[plane - (n - radius)] = v


def all_columns(source, a_refs, out_ref):
    for p in range(out_ref.shape[0]):
        out_ref[p] = blur_columns(source(p), a_refs[0][p], a_refs[1][p])


def own_rows(w_ref, wx_ref, low_ref, high_ref, first=0):
    n, rows, _ = w_ref.shape
    radius, count, _ = low_ref.shape
    part = slice(first, first + count)
    for p in range(n):
        w_hi, w_lo = split(w_ref[p])
        v = blur_rows(wx_ref[p, 0, part, :rows], wx_ref[p, 1, part, :rows], w_hi, w_lo)
        store_sends(v, p, n, radius, low_ref, high_ref)


def row_place():
    row = lax.axis_index("row")
    return row == 0, row == lax.axis_size("row") - 1


def first_kernel(
    n, radius, band_hbm, tx_hbm, ty_hbm, est_hbm,
    ah_ref, al_ref, wx_ref, w_ref,
    band_ref, tx_ref, ty_ref, est_ref, sems,
):
    pairs = ((band_hbm, band_ref), (tx_hbm, tx_ref), (ty_hbm, ty_ref), (est_hbm, est_ref))
    copies = [pltpu.make_async_copy(a, b, sems.at[k]) for k, (a, b) in enumerate(pairs)]
    for copy in copies:
        copy.start()
    rows, width = wx_ref.shape[2], wx_ref.shape[3]
    _, lane = iotas(16, 128)
    _, wide = iotas(16, width)
    row, lanes = iotas(rows, width)
    keep = jnp.logical_not(row_place()[1]) | ((row < rows - radius) == (lanes < rows))
    for copy in copies:
        copy.wait()
    for p in range(n):
        band = band_ref[p]
        column_matrix(spread(ty_ref, band, lane, radius, True), radius, ah_ref, al_ref, p)
        matrix = row_matrix(spread(tx_ref, band, wide, radius, False), rows, 0, width)
        wx_ref[p, 0], wx_ref[p, 1] = split(jnp.where(keep, matrix, 0.0))
    all_columns(lambda p: est_ref[p], (ah_ref, al_ref), w_ref)


def first_blur(band_index, taps_x, taps_y, est, width):
    n, rows, columns = est.shape
    radius = taps_x.shape[1] // 2
    a = shape_of(n, columns, columns, dtype=BF16)
    w = shape_of(n, 2, rows, width, dtype=BF16)
    return pl.pallas_call(
        functools.partial(first_kernel, n, radius),
        in_specs=[pl.BlockSpec(memory_space=pltpu.HBM)] * 4,
        scratch_shapes=[
            pltpu.SMEM(band_index.shape, jnp.int32),
            pltpu.SMEM(taps_x.shape, F32),
            pltpu.SMEM(taps_y.shape, F32),
            pltpu.VMEM(est.shape, F32),
            pltpu.SemaphoreType.DMA((4,)),
        ],
        out_specs=[VMEM] * 4,
        out_shape=[a, a, w, shape_of(*est.shape)],
        compiler_params=PARAMS,
        cost_estimate=cost(1.0),
    )(band_index, taps_x, taps_y, est)


def second_kernel(
    n, radius, halo, band_ref, tx_ref, ty_ref, tz_ref, after_ref,
    obs_ref, next_ref, ah_ref, al_ref, wx_ref, rn_ref, shifted_ref, taps_ref,
):
    rows, width = wx_ref.shape[2], wx_ref.shape[3]
    first_row, last_row = row_place()
    below = lax.axis_index("slab") * n
    depth = lax.axis_size("slab") * n
    _, lane = iotas(16, 128)
    _, wide = iotas(16, width)
    _, lanes = iotas(rows, width)
    lower = jnp.logical_not(first_row) | (lanes >= halo - radius)
    upper = jnp.logical_not(last_row) | (lanes < rows - radius + halo)
    keep = ((lanes < halo) & lower) | ((lanes >= halo) & upper)
    for k in range(2 * radius + 1):
        taps_ref[k] = jnp.full(taps_ref.shape[1:], tz_ref[k], F32)
    for p in range(n):
        band = band_ref[p]
        sums = column_matrix(
            spread(ty_ref, band, lane, radius, False), radius, ah_ref, al_ref, p
        )
        matrix = row_matrix(
            spread(tx_ref, band, wide, radius, True), rows, halo - 2 * radius, width
        )
        matrix = jnp.where(keep, matrix, 0.0)
        wx_ref[p, 0], wx_ref[p, 1] = split(matrix)
        along_x = jnp.sum(matrix, axis=1, keepdims=True)
        along_z = jnp.float32(0.0)
        z = below + p
        for k in range(2 * radius + 1):
            source = z - k + radius
            inside = (source >= 0) & (source < depth)
            along_z = along_z + jnp.where(inside, tz_ref[k], 0.0)
        for block, along_y in enumerate(sums):
            rn_ref[p, :, block * 128 : block * 128 + 128] = 1.0 / (
                along_x * (along_y * along_z)
            )
        shifted_ref[p, : rows - radius] = obs_ref[p, radius:]
        shifted_ref[p, rows - radius :] = next_ref[p, :radius]


def second_weights(band_index, taps_x, taps_y, taps_z, after, obs, beyond, width):
    n, rows, columns = obs.shape
    halo = beyond.shape[1]
    radius = taps_x.shape[1] // 2
    a = shape_of(n, columns, columns, dtype=BF16)
    w = shape_of(n, 2, rows, width, dtype=BF16)
    field = shape_of(*obs.shape)
    return pl.pallas_call(
        functools.partial(second_kernel, n, radius, halo),
        in_specs=[SMEM] * 4 + [ANY] + [VMEM] * 2,
        out_specs=[VMEM] * 6,
        out_shape=[a, a, w, field, field, shape_of(2 * radius + 1, 8, 128)],
        compiler_params=PARAMS,
        cost_estimate=cost(1.0),
    )(band_index, taps_x, taps_y, taps_z, after, obs, beyond)


def inner_kernel(first, w_ref, wx_ref, *refs):
    own_rows(w_ref, wx_ref, *refs[-2:], first)


def inner_blur(w, wx, first, count, radius, after, micro):
    send = shape_of(radius, count, w.shape[2])
    return pl.pallas_call(
        functools.partial(inner_kernel, first),
        in_specs=[VMEM] * 2 + [ANY] * len(after),
        out_specs=[VMEM] * 2,
        out_shape=[send] * 2,
        compiler_params=PARAMS,
        cost_estimate=cost(micro),
    )(w, wx, *after)


def edge_kernel(n, radius, blurred, w_ref, next_ref, wx_ref, *refs):
    rows, halo = w_ref.shape[1], next_ref.shape[1]
    inner, used = rows - halo, rows + halo
    beyond_ref = next_ref
    if not blurred:
        beyond_ref, refs = refs[-1], refs[:-1]
        all_columns(lambda p: next_ref[p], refs[:2], beyond_ref)
    for p in range(n):
        w_hi, w_lo = split(jnp.concatenate([w_ref[p], beyond_ref[p]], axis=0))
        v = blur_rows(wx_ref[p, 0, inner:, :used], wx_ref[p, 1, inner:, :used], w_hi, w_lo)
        store_sends(v, p, n, radius, *refs[-2:])


def edge_blur(w, beyond, wx, columns_matrix, radius):
    n, _, columns = w.shape
    halo = beyond.shape[1]
    send = shape_of(radius, halo, columns)
    args = (w, beyond, wx, *columns_matrix)
    return pl.pallas_call(
        functools.partial(edge_kernel, n, radius, not columns_matrix),
        in_specs=[VMEM] * len(args),
        out_specs=[VMEM] * 2,
        out_shape=[send] * 2,
        scratch_shapes=[pltpu.VMEM(beyond.shape, F32)] if columns_matrix else [],
        compiler_params=PARAMS,
        cost_estimate=cost(1.0),
    )(*args)


def depth_sum(n, radius, flip, tz_ref, refs, rows, lanes):
    low_ref, high_ref, zlo_ref, zhi_ref = refs
    last = 2 * radius
    taps = [tz_ref[last - k if flip else k] for k in range(last + 1)]
    total = [None] * n
    for j in range(-radius, n + radius):
        if j < 0:
            piece = zlo_ref[j + radius, rows, lanes]
        elif j < radius:
            piece = low_ref[j, rows, lanes]
        elif j < n:
            piece = high_ref[j - (n - radius), rows, lanes]
        else:
            piece = zhi_ref[j - n, rows, lanes]
        for i in range(max(0, j - radius), min(n, j + radius + 1)):
            term = taps[j - i + radius] * piece
            total[i] = term if total[i] is None else total[i] + term
    return total


def tiles(count, columns, body):
    def step(t, carry):
        for left in range(0, columns, 128):
            body(t * 8, slice(left, left + 128))
        return carry

    lax.fori_loop(0, count // 8, step, 0)


def at(start, offset):
    return pl.ds(pl.multiple_of(start + offset, 8), 8)


def ratio_kernel(n, radius, skip, tz_ref, obs_ref, *refs):
    rlow_ref, rhigh_ref = refs[-2:]
    columns = obs_ref.shape[2]

    def run(own, first):
        def body(start, lanes):
            total = depth_sum(n, radius, False, tz_ref, own, at(start, 0), lanes)
            rows = at(start, first)
            for i in range(n):
                ratio = obs_ref[i, at(start, skip + first), lanes] / total[i]
                if i < radius:
                    rlow_ref[i, rows, lanes] = ratio
                if i >= n - radius:
                    rhigh_ref[i - (n - radius), rows, lanes] = ratio

        tiles(own[0].shape[1], columns, body)

    first = 0
    while first < rlow_ref.shape[1]:
        run(refs[:4], first)
        first += refs[0].shape[1]
        refs = refs[4:]


def depth_ratio(taps_z, obs, chunks, skip, after, micro):
    n, _, columns = obs.shape
    radius = chunks[0][0].shape[0]
    send = shape_of(radius, sum(chunk[0].shape[1] for chunk in chunks), columns)
    return pl.pallas_call(
        functools.partial(ratio_kernel, n, radius, skip),
        in_specs=[VMEM] * (2 + 4 * len(chunks)) + [ANY] * len(after),
        out_specs=[VMEM] * 2,
        out_shape=[send] * 2,
        compiler_params=PARAMS,
        cost_estimate=cost(micro),
    )(taps_z, obs, *(x for chunk in chunks for x in chunk), *after)


def back_kernel(n, radius, swapped, tz_ref, *refs):
    out_ref = refs[-1]
    if swapped:
        refs = (*refs[:2], refs[3], refs[2])
    _, count, columns = out_ref.shape

    def body(start, lanes):
        rows = at(start, 0)
        total = depth_sum(n, radius, True, tz_ref, refs[:4], rows, lanes)
        for i in range(n):
            out_ref[i, rows, lanes] = total[i]

    tiles(count, columns, body)


def depth_back(taps_z, chunk, n, after, micro=1.0, swapped=False):
    radius, count, columns = chunk[0].shape
    if swapped:
        chunk = (*chunk[:2], chunk[3], chunk[2])
    return pl.pallas_call(
        functools.partial(back_kernel, n, radius, swapped),
        in_specs=[VMEM] * 5 + [ANY],
        out_specs=VMEM,
        out_shape=shape_of(n, count, columns),
        compiler_params=PARAMS,
        cost_estimate=cost(micro),
    )(taps_z, *chunk, after)


def update_kernel(n, last, count, *refs):
    pieces, edge_ref, refs = refs[:count], refs[count - 1], refs[count:]
    est_ref, rn_ref, wa_ref, bh_ref, bl_ref = refs[:5]
    refs = refs[5:]
    rows = est_ref.shape[1]
    halo = edge_ref.shape[1]
    used = rows + halo
    if last:
        out_ref, u_ref, sems = refs
    else:
        wx_ref, ah_ref, al_ref, out_ref, w_ref, top_ref, low_ref, high_ref, u_ref = refs
    for p in range(n):
        c_hi, c_lo = split(jnp.concatenate([piece[p] for piece in pieces], axis=0))
        u_ref[p] = blur_rows(wa_ref[p, 0, :, :used], wa_ref[p, 1, :, :used], c_hi, c_lo)
    if last:
        copies = []
        group = up(n, GROUPS) // GROUPS
        for first in range(0, n, group):
            part = pl.ds(first, min(group, n - first))
            for p in range(first, min(first + group, n)):
                u = blur_columns(u_ref[p], bh_ref[p], bl_ref[p])
                u_ref[p] = est_ref[p] * u * rn_ref[p]
            copies.append(
                pltpu.make_async_copy(
                    u_ref.at[part], out_ref.at[part], sems.at[len(copies)]
                )
            )
            copies[-1].start()
        for copy in copies:
            copy.wait()
        return
    for p in range(n):
        u = blur_columns(u_ref[p], bh_ref[p], bl_ref[p])
        out_ref[p] = est_ref[p] * u * rn_ref[p]
    all_columns(lambda p: out_ref[p], (ah_ref, al_ref), w_ref)
    for p in range(n):
        top_ref[p] = w_ref[p, :halo]
    own_rows(w_ref, wx_ref, low_ref, high_ref)


def update(pieces, est, rn, adjoint, forward, count, radius):
    n, rows, columns = est.shape
    halo = pieces[0].shape[1]
    last = forward is None
    sems = pltpu.SemaphoreType.DMA((GROUPS,))
    args = [*pieces, est, rn, *adjoint] + ([] if last else [*forward])
    out_shape = [shape_of(*est.shape)]
    if not last:
        send = shape_of(radius, count, columns)
        out_shape += [shape_of(*est.shape), shape_of(n, halo, columns), send, send]
    return pl.pallas_call(
        functools.partial(update_kernel, n, last, len(pieces)),
        in_specs=[VMEM] * len(args),
        out_specs=[ANY] if last else [VMEM] * len(out_shape),
        out_shape=out_shape,
        scratch_shapes=[pltpu.VMEM(est.shape, F32)] + [sems] * last,
        compiler_params=PARAMS,
        cost_estimate=cost(1.0),
    )(*args)


def send_up(x):
    steps = range(lax.axis_size("slab") - 1)
    return lax.ppermute(x, "slab", [(i, i + 1) for i in steps])


def send_down(x):
    steps = range(lax.axis_size("slab") - 1)
    return lax.ppermute(x, "slab", [(i + 1, i) for i in steps])


def depth_exchange(low, high):
    return low, high, send_up(high), send_down(low)


def ring(x, step):
    count = lax.axis_size("row")
    return lax.ppermute(x, "row", [(i, (i + step) % count) for i in range(count)])


def on_device(observed, band_index, taps_x, taps_y, taps_z):
    n, rows, columns = observed.shape
    radius = taps_z.shape[0] // 2
    halo = up(2 * radius, 16)
    inner = rows - halo
    half = up(inner // 2, 16)
    width = up(rows + halo, 128)
    beyond = ring(observed[:, :halo], -1)
    ah, al, wx, w = first_blur(band_index, taps_x, taps_y, observed, width)
    est, adjoint = observed, None
    for step in range(ITERS):
        if step:
            v_first = depth_exchange(*first_sends)
            edge_sends = edge_blur(w, beyond, wx, (), radius)
            v_edge = depth_exchange(*edge_sends)
            r_sends = depth_ratio(taps, shifted, [v_first], 0, (edge_sends[0],), 20.0)
            first_low = send_up(r_sends[1])
            r_inner = []
            after = (r_sends[0],)
            inner_sends = inner_blur(w, wx, half, inner - half, radius, after, 1.0)
            v_inner = depth_exchange(*inner_sends)
        else:
            edge_sends = edge_blur(w, beyond, wx, (ah, al), radius)
            v_edge = depth_exchange(*edge_sends)
            after = (edge_sends[0],)
            inner_sends = inner_blur(w, wx, 0, inner, radius, after, 1.0)
            v_inner = depth_exchange(*inner_sends)
            r_inner = []
            bh, bl, wa, rn, shifted, taps = second_weights(
                band_index, taps_x, taps_y, taps_z, inner_sends[0], observed, beyond, width
            )
            adjoint = (wa, bh, bl)
        after = (inner_sends[0],)
        r_edge = depth_exchange(
            *depth_ratio(taps, shifted, [v_edge], inner, after, 1.0),
        )
        after = (r_edge[0],)
        if step:
            again = depth_ratio(taps, shifted, [v_first], 0, after, 20.0)
            r_inner.append((*again, first_low, send_down(again[0])))
            after = (again[0],)
        r_sends = depth_ratio(
            taps, shifted, [v_inner], half if step else 0, after, 1.0
        )
        r_inner.append(depth_exchange(*r_sends))
        after = r_sends[0]
        c_edge = depth_back(taps, r_edge, n, after, 1.0, step > 0)
        before = ring(c_edge, 1)
        after, c_inner = c_edge, []
        if step:
            after = depth_back(taps, r_inner[0], n, after, 1.0)
            c_inner.append(after)
        c_inner.append(depth_back(taps, r_inner[-1], n, after, 100.0))
        last = step == ITERS - 1
        out = update(
            (before, *c_inner, c_edge), est, rn, adjoint,
            None if last else (wx, ah, al), half, radius,
        )
        est = out[0]
        if not last:
            w, top, *first_sends = out[1:]
            beyond = ring(top, -1)
    return est


def solution(mesh):
    in_specs = (P(("grp", "slab"), "row", None), P("slab"), P(), P(), P())
    out_specs = P(("grp", "slab"), "row", None)
    return jax.shard_map(
        on_device, mesh=mesh, in_specs=in_specs, out_specs=out_specs, check_vma=False
    )
```

```python
import functools

import jax
import jax.numpy as jnp
from jax import lax
from jax.experimental import pallas as pl
from jax.experimental.pallas import tpu as pltpu
from jax.sharding import PartitionSpec as P

ITERS = 2
GROUPS = 2
F32 = jnp.float32
BF16 = jnp.bfloat16
PARAMS = pltpu.CompilerParams(vmem_limit_bytes=16 * 1024 * 1024)
SMEM = pl.BlockSpec(memory_space=pltpu.SMEM)
VMEM = pl.BlockSpec(memory_space=pltpu.VMEM)
ANY = pl.BlockSpec(memory_space=pl.ANY)


def up(value, step):
    return -(-value // step) * step


def split(x):
    hi = x.astype(BF16)
    return hi, (x - hi.astype(F32)).astype(BF16)


def mm(a, b):
    return jnp.dot(a, b, preferred_element_type=F32)


def blur_rows(w_hi, w_lo, v_hi, v_lo):
    count = w_hi.shape[0]
    both = mm(jnp.concatenate([w_hi, w_lo], axis=0), v_hi)
    return both[:count] + both[count:] + mm(w_hi, v_lo)


def blur_columns(u, a_hi, a_lo):
    count = u.shape[0]
    u_hi, u_lo = split(u)
    both = mm(jnp.concatenate([u_hi, u_lo], axis=0), a_hi)
    return both[:count] + both[count:] + mm(u_hi, a_lo)


def cost(microseconds):
    return pl.CostEstimate(
        flops=int(microseconds * 1e9), bytes_accessed=int(microseconds * 3.5e6), transcendentals=0
    )


def shape_of(*dims, dtype=F32):
    return jax.ShapeDtypeStruct(dims, dtype)


def spread(ref, band, lanes, radius, flip):
    base = jnp.zeros(lanes.shape, F32)
    for k in range(2 * radius + 1):
        base = jnp.where(lanes == (2 * radius - k if flip else k), ref[band, k], base)
    return base


def iotas(rows, lanes):
    shape = (rows, lanes)
    return (
        lax.broadcasted_iota(jnp.int32, shape, 0),
        lax.broadcasted_iota(jnp.int32, shape, 1),
    )


def column_matrix(base, radius, h_ref, l_ref, p):
    columns = h_ref.shape[1]
    sub, lane = iotas(16, 128)
    rolled = {}
    sums = [None] * (columns // 128)
    for first in range(0, columns, 16):
        key = first % 128
        if key not in rolled:
            rolled[key] = pltpu.roll(base, (key - radius) % 128, 1, stride=1, stride_axis=0)
        for block in range(columns // 128):
            left = block * 128
            here = (p, slice(first, first + 16), slice(left, left + 128))
            if left > first + 15 + radius or left + 127 < first - radius:
                zero = jnp.zeros((16, 128), BF16)
                h_ref[here] = zero
                l_ref[here] = zero
                continue
            inside = jnp.abs(lane - sub + (left - first)) <= radius
            tile = jnp.where(inside, rolled[key], 0.0)
            h_ref[here], l_ref[here] = split(tile)
            sums[block] = tile if sums[block] is None else sums[block] + tile
    return [jnp.sum(s, axis=0, keepdims=True) for s in sums]


def row_matrix(base, rows, shift, width):
    return jnp.concatenate(
        [
            pltpu.roll(base, (first + shift) % width, 1, stride=1, stride_axis=0)
            for first in range(0, rows, 16)
        ],
        axis=0,
    )


def store_sends(v, plane, n, radius, low_ref, high_ref):
    if plane < radius:
        low_ref[plane] = v
    if plane >= n - radius:
        high_ref[plane - (n - radius)] = v


def all_columns(source, a_refs, out_ref):
    for p in range(out_ref.shape[0]):
        out_ref[p] = blur_columns(source(p), a_refs[0][p], a_refs[1][p])


def own_rows(w_ref, wx_ref, low_ref, high_ref, first=0):
    n, rows, _ = w_ref.shape
    radius, count, _ = low_ref.shape
    part = slice(first, first + count)
    for p in range(n):
        w_hi, w_lo = split(w_ref[p])
        v = blur_rows(wx_ref[p, 0, part, :rows], wx_ref[p, 1, part, :rows], w_hi, w_lo)
        store_sends(v, p, n, radius, low_ref, high_ref)


def row_place():
    row = lax.axis_index("row")
    return row == 0, row == lax.axis_size("row") - 1


def first_kernel(
    n, radius, band_hbm, tx_hbm, ty_hbm, est_hbm,
    ah_ref, al_ref, wx_ref, w_ref,
    band_ref, tx_ref, ty_ref, est_ref, sems,
):
    pairs = ((band_hbm, band_ref), (tx_hbm, tx_ref), (ty_hbm, ty_ref), (est_hbm, est_ref))
    copies = [pltpu.make_async_copy(a, b, sems.at[k]) for k, (a, b) in enumerate(pairs)]
    for copy in copies:
        copy.start()
    rows, width = wx_ref.shape[2], wx_ref.shape[3]
    _, lane = iotas(16, 128)
    _, wide = iotas(16, width)
    row, lanes = iotas(rows, width)
    keep = jnp.logical_not(row_place()[1]) | ((row < rows - radius) == (lanes < rows))
    for copy in copies:
        copy.wait()
    for p in range(n):
        band = band_ref[p]
        column_matrix(spread(ty_ref, band, lane, radius, True), radius, ah_ref, al_ref, p)
        matrix = row_matrix(spread(tx_ref, band, wide, radius, False), rows, 0, width)
        wx_ref[p, 0], wx_ref[p, 1] = split(jnp.where(keep, matrix, 0.0))
    all_columns(lambda p: est_ref[p], (ah_ref, al_ref), w_ref)


def first_blur(band_index, taps_x, taps_y, est, width):
    n, rows, columns = est.shape
    radius = taps_x.shape[1] // 2
    a = shape_of(n, columns, columns, dtype=BF16)
    w = shape_of(n, 2, rows, width, dtype=BF16)
    return pl.pallas_call(
        functools.partial(first_kernel, n, radius),
        in_specs=[pl.BlockSpec(memory_space=pltpu.HBM)] * 4,
        scratch_shapes=[
            pltpu.SMEM(band_index.shape, jnp.int32),
            pltpu.SMEM(taps_x.shape, F32),
            pltpu.SMEM(taps_y.shape, F32),
            pltpu.VMEM(est.shape, F32),
            pltpu.SemaphoreType.DMA((4,)),
        ],
        out_specs=[VMEM] * 4,
        out_shape=[a, a, w, shape_of(*est.shape)],
        compiler_params=PARAMS,
        cost_estimate=cost(1.0),
    )(band_index, taps_x, taps_y, est)


def second_kernel(
    n, radius, halo, band_ref, tx_ref, ty_ref, tz_ref, after_ref,
    obs_ref, next_ref, ah_ref, al_ref, wx_ref, rn_ref, shifted_ref, taps_ref,
):
    rows, width = wx_ref.shape[2], wx_ref.shape[3]
    first_row, last_row = row_place()
    below = lax.axis_index("slab") * n
    depth = lax.axis_size("slab") * n
    _, lane = iotas(16, 128)
    _, wide = iotas(16, width)
    _, lanes = iotas(rows, width)
    lower = jnp.logical_not(first_row) | (lanes >= halo - radius)
    upper = jnp.logical_not(last_row) | (lanes < rows - radius + halo)
    keep = ((lanes < halo) & lower) | ((lanes >= halo) & upper)
    for k in range(2 * radius + 1):
        taps_ref[k] = jnp.full(taps_ref.shape[1:], tz_ref[k], F32)
    for p in range(n):
        band = band_ref[p]
        sums = column_matrix(
            spread(ty_ref, band, lane, radius, False), radius, ah_ref, al_ref, p
        )
        matrix = row_matrix(
            spread(tx_ref, band, wide, radius, True), rows, halo - 2 * radius, width
        )
        matrix = jnp.where(keep, matrix, 0.0)
        wx_ref[p, 0], wx_ref[p, 1] = split(matrix)
        along_x = jnp.sum(matrix, axis=1, keepdims=True)
        along_z = jnp.float32(0.0)
        z = below + p
        for k in range(2 * radius + 1):
            source = z - k + radius
            inside = (source >= 0) & (source < depth)
            along_z = along_z + jnp.where(inside, tz_ref[k], 0.0)
        for block, along_y in enumerate(sums):
            rn_ref[p, :, block * 128 : block * 128 + 128] = 1.0 / (
                along_x * (along_y * along_z)
            )
        shifted_ref[p, : rows - radius] = obs_ref[p, radius:]
        shifted_ref[p, rows - radius :] = next_ref[p, :radius]


def second_weights(band_index, taps_x, taps_y, taps_z, after, obs, beyond, width):
    n, rows, columns = obs.shape
    halo = beyond.shape[1]
    radius = taps_x.shape[1] // 2
    a = shape_of(n, columns, columns, dtype=BF16)
    w = shape_of(n, 2, rows, width, dtype=BF16)
    field = shape_of(*obs.shape)
    return pl.pallas_call(
        functools.partial(second_kernel, n, radius, halo),
        in_specs=[SMEM] * 4 + [ANY] + [VMEM] * 2,
        out_specs=[VMEM] * 6,
        out_shape=[a, a, w, field, field, shape_of(2 * radius + 1, 8, 128)],
        compiler_params=PARAMS,
        cost_estimate=cost(1.0),
    )(band_index, taps_x, taps_y, taps_z, after, obs, beyond)


def inner_kernel(first, w_ref, wx_ref, *refs):
    own_rows(w_ref, wx_ref, *refs[-2:], first)


def inner_blur(w, wx, first, count, radius, after, micro):
    send = shape_of(radius, count, w.shape[2])
    return pl.pallas_call(
        functools.partial(inner_kernel, first),
        in_specs=[VMEM] * 2 + [ANY] * len(after),
        out_specs=[VMEM] * 2,
        out_shape=[send] * 2,
        compiler_params=PARAMS,
        cost_estimate=cost(micro),
    )(w, wx, *after)


def edge_kernel(n, radius, blurred, w_ref, next_ref, wx_ref, *refs):
    rows, halo = w_ref.shape[1], next_ref.shape[1]
    inner, used = rows - halo, rows + halo
    beyond_ref = next_ref
    if not blurred:
        beyond_ref, refs = refs[-1], refs[:-1]
        all_columns(lambda p: next_ref[p], refs[:2], beyond_ref)
    for p in range(n):
        w_hi, w_lo = split(jnp.concatenate([w_ref[p], beyond_ref[p]], axis=0))
        v = blur_rows(wx_ref[p, 0, inner:, :used], wx_ref[p, 1, inner:, :used], w_hi, w_lo)
        store_sends(v, p, n, radius, *refs[-2:])


def edge_blur(w, beyond, wx, columns_matrix, radius):
    n, _, columns = w.shape
    halo = beyond.shape[1]
    send = shape_of(radius, halo, columns)
    args = (w, beyond, wx, *columns_matrix)
    return pl.pallas_call(
        functools.partial(edge_kernel, n, radius, not columns_matrix),
        in_specs=[VMEM] * len(args),
        out_specs=[VMEM] * 2,
        out_shape=[send] * 2,
        scratch_shapes=[pltpu.VMEM(beyond.shape, F32)] if columns_matrix else [],
        compiler_params=PARAMS,
        cost_estimate=cost(1.0),
    )(*args)


def depth_sum(n, radius, flip, tz_ref, refs, rows, lanes):
    low_ref, high_ref, zlo_ref, zhi_ref = refs
    last = 2 * radius
    taps = [tz_ref[last - k if flip else k] for k in range(last + 1)]
    total = [None] * n
    for j in range(-radius, n + radius):
        if j < 0:
            piece = zlo_ref[j + radius, rows, lanes]
        elif j < radius:
            piece = low_ref[j, rows, lanes]
        elif j < n:
            piece = high_ref[j - (n - radius), rows, lanes]
        else:
            piece = zhi_ref[j - n, rows, lanes]
        for i in range(max(0, j - radius), min(n, j + radius + 1)):
            term = taps[j - i + radius] * piece
            total[i] = term if total[i] is None else total[i] + term
    return total


def tiles(count, columns, body):
    def step(t, carry):
        for left in range(0, columns, 128):
            body(t * 8, slice(left, left + 128))
        return carry

    lax.fori_loop(0, count // 8, step, 0)


def at(start, offset):
    return pl.ds(pl.multiple_of(start + offset, 8), 8)


def ratio_kernel(n, radius, skip, tz_ref, obs_ref, *refs):
    rlow_ref, rhigh_ref = refs[-2:]
    columns = obs_ref.shape[2]

    def run(own, first):
        def body(start, lanes):
            total = depth_sum(n, radius, False, tz_ref, own, at(start, 0), lanes)
            rows = at(start, first)
            for i in range(n):
                ratio = obs_ref[i, at(start, skip + first), lanes] / total[i]
                if i < radius:
                    rlow_ref[i, rows, lanes] = ratio
                if i >= n - radius:
                    rhigh_ref[i - (n - radius), rows, lanes] = ratio

        tiles(own[0].shape[1], columns, body)

    first = 0
    while first < rlow_ref.shape[1]:
        run(refs[:4], first)
        first += refs[0].shape[1]
        refs = refs[4:]


def depth_ratio(taps_z, obs, chunks, skip, after, micro):
    n, _, columns = obs.shape
    radius = chunks[0][0].shape[0]
    send = shape_of(radius, sum(chunk[0].shape[1] for chunk in chunks), columns)
    return pl.pallas_call(
        functools.partial(ratio_kernel, n, radius, skip),
        in_specs=[VMEM] * (2 + 4 * len(chunks)) + [ANY] * len(after),
        out_specs=[VMEM] * 2,
        out_shape=[send] * 2,
        compiler_params=PARAMS,
        cost_estimate=cost(micro),
    )(taps_z, obs, *(x for chunk in chunks for x in chunk), *after)


def back_kernel(n, radius, swapped, tz_ref, *refs):
    out_ref = refs[-1]
    if swapped:
        refs = (*refs[:2], refs[3], refs[2])
    _, count, columns = out_ref.shape

    def body(start, lanes):
        rows = at(start, 0)
        total = depth_sum(n, radius, True, tz_ref, refs[:4], rows, lanes)
        for i in range(n):
            out_ref[i, rows, lanes] = total[i]

    tiles(count, columns, body)


def depth_back(taps_z, chunk, n, after, micro=1.0, swapped=False):
    radius, count, columns = chunk[0].shape
    if swapped:
        chunk = (*chunk[:2], chunk[3], chunk[2])
    return pl.pallas_call(
        functools.partial(back_kernel, n, radius, swapped),
        in_specs=[VMEM] * 5 + [ANY],
        out_specs=VMEM,
        out_shape=shape_of(n, count, columns),
        compiler_params=PARAMS,
        cost_estimate=cost(micro),
    )(taps_z, *chunk, after)


def update_kernel(n, last, count, *refs):
    pieces, edge_ref, refs = refs[:count], refs[count - 1], refs[count:]
    est_ref, rn_ref, wa_ref, bh_ref, bl_ref = refs[:5]
    refs = refs[5:]
    rows = est_ref.shape[1]
    halo = edge_ref.shape[1]
    used = rows + halo
    if last:
        out_ref, u_ref, sems = refs
    else:
        wx_ref, ah_ref, al_ref, out_ref, w_ref, top_ref, low_ref, high_ref, u_ref = refs
    for p in range(n):
        c_hi, c_lo = split(jnp.concatenate([piece[p] for piece in pieces], axis=0))
        u_ref[p] = blur_rows(wa_ref[p, 0, :, :used], wa_ref[p, 1, :, :used], c_hi, c_lo)
    if last:
        copies = []
        group = up(n, GROUPS) // GROUPS
        for first in range(0, n, group):
            part = pl.ds(first, min(group, n - first))
            for p in range(first, min(first + group, n)):
                u = blur_columns(u_ref[p], bh_ref[p], bl_ref[p])
                u_ref[p] = est_ref[p] * u * rn_ref[p]
            copies.append(
                pltpu.make_async_copy(
                    u_ref.at[part], out_ref.at[part], sems.at[len(copies)]
                )
            )
            copies[-1].start()
        for copy in copies:
            copy.wait()
        return
    for p in range(n):
        u = blur_columns(u_ref[p], bh_ref[p], bl_ref[p])
        out_ref[p] = est_ref[p] * u * rn_ref[p]
    all_columns(lambda p: out_ref[p], (ah_ref, al_ref), w_ref)
    for p in range(n):
        top_ref[p] = w_ref[p, :halo]
    own_rows(w_ref, wx_ref, low_ref, high_ref)


def update(pieces, est, rn, adjoint, forward, count, radius):
    n, rows, columns = est.shape
    halo = pieces[0].shape[1]
    last = forward is None
    sems = pltpu.SemaphoreType.DMA((GROUPS,))
    args = [*pieces, est, rn, *adjoint] + ([] if last else [*forward])
    out_shape = [shape_of(*est.shape)]
    if not last:
        send = shape_of(radius, count, columns)
        out_shape += [shape_of(*est.shape), shape_of(n, halo, columns), send, send]
    return pl.pallas_call(
        functools.partial(update_kernel, n, last, len(pieces)),
        in_specs=[VMEM] * len(args),
        out_specs=[ANY] if last else [VMEM] * len(out_shape),
        out_shape=out_shape,
        scratch_shapes=[pltpu.VMEM(est.shape, F32)] + [sems] * last,
        compiler_params=PARAMS,
        cost_estimate=cost(1.0),
    )(*args)


def send_up(x):
    steps = range(lax.axis_size("slab") - 1)
    return lax.ppermute(x, "slab", [(i, i + 1) for i in steps])


def send_down(x):
    steps = range(lax.axis_size("slab") - 1)
    return lax.ppermute(x, "slab", [(i + 1, i) for i in steps])


def depth_exchange(low, high):
    return low, high, send_up(high), send_down(low)


def ring(x, step):
    count = lax.axis_size("row")
    return lax.ppermute(x, "row", [(i, (i + step) % count) for i in range(count)])


def on_device(observed, band_index, taps_x, taps_y, taps_z):
    n, rows, columns = observed.shape
    radius = taps_z.shape[0] // 2
    halo = up(2 * radius, 16)
    inner = rows - halo
    half = up(inner // 2, 16)
    width = up(rows + halo, 128)
    beyond = ring(observed[:, :halo], -1)
    ah, al, wx, w = first_blur(band_index, taps_x, taps_y, observed, width)
    est, adjoint = observed, None
    for step in range(ITERS):
        if step:
            v_first = depth_exchange(*first_sends)
            edge_sends = edge_blur(w, beyond, wx, (), radius)
            v_edge = depth_exchange(*edge_sends)
            r_sends = depth_ratio(taps, shifted, [v_first], 0, (edge_sends[0],), 20.0)
            first_low = send_up(r_sends[1])
            r_inner = []
            after = (r_sends[0],)
            inner_sends = inner_blur(w, wx, half, inner - half, radius, after, 1.0)
            v_inner = depth_exchange(*inner_sends)
        else:
            edge_sends = edge_blur(w, beyond, wx, (ah, al), radius)
            v_edge = depth_exchange(*edge_sends)
            after = (edge_sends[0],)
            inner_sends = inner_blur(w, wx, 0, inner, radius, after, 1.0)
            v_inner = depth_exchange(*inner_sends)
            r_inner = []
            bh, bl, wa, rn, shifted, taps = second_weights(
                band_index, taps_x, taps_y, taps_z, inner_sends[0], observed, beyond, width
            )
            adjoint = (wa, bh, bl)
        after = (inner_sends[0],)
        r_edge = depth_exchange(
            *depth_ratio(taps, shifted, [v_edge], inner, after, 1.0),
        )
        after = (r_edge[0],)
        if step:
            again = depth_ratio(taps, shifted, [v_first], 0, after, 20.0)
            r_inner.append((*again, first_low, send_down(again[0])))
            after = (again[0],)
        r_sends = depth_ratio(
            taps, shifted, [v_inner], half if step else 0, after, 1.0
        )
        r_inner.append(depth_exchange(*r_sends))
        after = r_sends[0]
        c_edge = depth_back(taps, r_edge, n, after, 1.0, step > 0)
        before = ring(c_edge, 1)
        after, c_inner = c_edge, []
        if step:
            after = depth_back(taps, r_inner[0], n, after, 1.0)
            c_inner.append(after)
        c_inner.append(depth_back(taps, r_inner[-1], n, after, 100.0))
        last = step == ITERS - 1
        out = update(
            (before, *c_inner, c_edge), est, rn, adjoint,
            None if last else (wx, ah, al), half, radius,
        )
        est = out[0]
        if not last:
            w, top, *first_sends = out[1:]
            beyond = ring(top, -1)
    return est


def solution(mesh):
    in_specs = (P(("grp", "slab"), "row", None), P("slab"), P(), P(), P())
    out_specs = P(("grp", "slab"), "row", None)
    return jax.shard_map(
        on_device, mesh=mesh, in_specs=in_specs, out_specs=out_specs, check_vma=False
    )
```
